256 devices in a mesh: dp: 128 (over x, y, z), shard: 2 (over core).
Axes of the slice: x: 4, y: 4, z: 8, core: 2. Of those that a mesh axis runs over, the one named last changes fastest.
Arguments:
- params: float32 [160272], replicated, may hold values from -5 to 5
- first_moment: float32 [160272], replicated, may hold values from -10 to 10
- second_moment: float32 [160272], replicated, may hold values from 0.05 to 0.5
- positions: float32 [2048, 3, 128], P(('dp', 'shard')), may hold values from 0 to 4
- species: int32 [2048, 128], P(('dp', 'shard')), may hold values from 0 to 9
- neighbours: int32 [2048, 16, 128], P(('dp', 'shard')), may hold values from -1 to 127, as said below
- window_of: int32 [2048], P(('dp', 'shard')), may hold values from 0 to 31
- frame_count: int32 [256], P(('dp', 'shard')), may hold values from 1 to 8, 768 in all
Outputs:
- new_params: float32 [160272], replicated
- new_first: float32 [160272], replicated
- new_second: float32 [160272], replicated
- window_means: float32 [32], replicated
The draws below stay inside these ranges and needn't reach their ends.
Inputs may be any that keep to these rules, and one draw needn't show every extreme that they name: `neighbours`: -1 marks an empty slot; no atom lists itself; the last slot of every atom is empty. Slots 0 to frame_count - 1 of a device hold its frames.
All inputs are finite; a program needn't handle non-finite values.
Results may differ from the reference program's by a relative error of at most 0.0003.
Values sent between devices are 32-bit elements; how exact they have to be, the bound alone decides.
No kernel may reach another device: no remote copies, remote signals or barrier semaphores. Data moves between devices by JAX's collectives and lax.ppermute only.
A program may use at most 128 MiB of HBM per device.

```python
import math
import jax
import jax.numpy as jnp
import numpy as np
from jax import lax

C = 128
HID = 64
NB = 8
SPECIES = 10
RO = 16
LAYERS = 2
WINDOWS = 32
ATOMS = 128
SOLUTE = 16
K = 16
F_SLOT = 8
FRAMES = 2048
VALID = 768
NPAR = 160272
N_DP = 128
N_SHARD = 2


def draw_neighbours(key, part):
    key = jax.random.fold_in(key, 7)
    key_off, key_len = jax.random.split(key)
    offsets = jax.random.randint(key_off, (FRAMES, K, ATOMS), 1, ATOMS)
    atom_ids = jnp.arange(ATOMS, dtype=jnp.int32)[None, None, :]
    partner = (atom_ids + offsets) % ATOMS
    slot_ids = jnp.arange(K, dtype=jnp.int32)[None, :, None]
    partner = jnp.where((atom_ids == 0) & (slot_ids == 0), ATOMS - 1, partner)
    filled = jax.random.randint(key_len, (FRAMES, 1, ATOMS), K // 2, K)
    filled = jnp.maximum(filled, 1)
    return jnp.where(slot_ids < filled, partner, -1).astype(jnp.int32)


def with_ends(result, key, least, high):
    extent = result.shape
    place = [jax.random.randint(jax.random.fold_in(key, axis), (), 0, extent[axis]) for axis in range(len(extent))]
    result = result.at[tuple(place)].set(least)
    longest = extent.index(max(extent))
    place[longest] = (place[longest] + 1) % extent[longest]
    return result.at[tuple(place)].set(high)


def shard_levels(own_key, extent, shards, least, high):
    def one(position, blocks):
        steps = jax.random.uniform(jax.random.fold_in(jax.random.fold_in(own_key, 6), position), (blocks,), jnp.float32, least / len(shards), high / len(shards))
        return jnp.repeat(jnp.exp(steps), extent[position] // blocks).reshape((-1,) + (1,) * (len(extent) - position - 1))

    gain = one(*shards[0])
    for cut in shards[1:]:
        gain = gain * one(*cut)
    return gain


def cumulative_ranks(count, lean):
    loads = [(1 << 20) // math.isqrt(grade ** lean) + 1 for grade in range(1, count + 1)]
    scale = 1 + sum(loads) // (1 << 30)
    return np.cumsum(np.array([max(1, weight // scale) for weight in loads]))


def ranked_ids(key, shape, amount, skew):
    table = cumulative_ranks(amount, skew)
    ticket = jax.random.randint(jax.random.fold_in(key, 1), shape, 0, int(table[amount - 1]))
    standing = jnp.searchsorted(jnp.asarray(table, jnp.int32), ticket, side="right")
    return jax.random.permutation(jax.random.fold_in(key, 2), amount)[standing].astype(jnp.int32)


def split_up(amount, total, limit, slope):
    weights = [(1 << 20) // math.isqrt(rank ** slope) + 1 for rank in range(2, amount + 1)]
    spare, counts = total - limit - (amount - 1), [1] * (amount - 1)
    while spare > 0:
        candidates = [i for i in range(amount - 1) if counts[i] < limit]
        whole, left = sum([weights[i] for i in candidates]), spare
        for i in candidates:
            addition = min(limit - counts[i], max(1, left * weights[i] // whole), spare)
            counts[i] = counts[i] + addition
            spare = spare - addition
    return np.array([limit] + counts)


def ragged(rng, number_of, total, limit, skew):
    if number_of == 2:
        one = jax.random.randint(rng, (), max(1, total - limit), min(limit, total - 1) + 1)
        return jnp.stack([one, total - one])
    sizes = jnp.asarray(split_up(number_of, total, limit, skew), jnp.int32)
    couples = (number_of - 1) // 2
    source_of, receiver = sizes[1:1 + 2 * couples:2], sizes[2:2 + 2 * couples:2]
    room = jnp.minimum(source_of - 1, limit - receiver)
    passed = jax.random.randint(jax.random.fold_in(rng, 1), (couples,), 0, 1 << 20) % (room + 1)
    sizes = sizes.at[1:1 + 2 * couples:2].set(source_of - passed).at[2:2 + 2 * couples:2].set(receiver + passed)
    return sizes[jax.random.permutation(jax.random.fold_in(rng, 2), number_of)]


def centred(key, extent, spread, limit, held_as=jnp.bfloat16):
    array = spread * jax.random.normal(key, extent, jnp.float32)
    return jnp.clip(array, min=-limit, max=limit).astype(held_as)


def setup_inputs(seed: int = 0) -> dict:
    streams_of = jax.random.split(jax.random.key(seed), 9)
    params = centred(streams_of[0], (NPAR,), 1.0, 5.0, jnp.float32)
    first_moment = centred(streams_of[1], (NPAR,), 2.5, 10.0, jnp.float32)
    second_moment = jnp.clip(jnp.exp(jax.random.uniform(streams_of[2], (NPAR,), jnp.float32, math.log(0.05), math.log(0.5))), 0.05, 0.5)
    positions = jnp.clip(4.0 * jax.random.uniform(streams_of[3], (FRAMES, 3, ATOMS), jnp.float32) ** shard_levels(streams_of[3], (FRAMES, 3, ATOMS), ((0, 256),), -0.2, 0.2), 0.0, 4.0)
    species = with_ends(jax.random.randint(streams_of[4], (FRAMES, ATOMS), 0, SPECIES), jax.random.fold_in(streams_of[4], 1), 0, SPECIES - 1).astype(jnp.int32)
    neighbours = draw_neighbours(jax.random.fold_in(streams_of[8], 71), 0)
    window_of = with_ends(ranked_ids(streams_of[6], (FRAMES,), WINDOWS, 2), jax.random.fold_in(streams_of[6], 3), 0, WINDOWS - 1).astype(jnp.int32)
    frame_count = ragged(streams_of[7], N_DP * N_SHARD, VALID, F_SLOT, 2).astype(jnp.int32)
    return {"params": params, "first_moment": first_moment, "second_moment": second_moment, "positions": positions, "species": species, "neighbours": neighbours, "window_of": window_of, "frame_count": frame_count}


RADIUS_CUT = 8.0
SOFTENING = 0.01
GRAD_SCALE = 4.0

def mult(left, right):
    return jnp.dot(left, right, precision=lax.Precision.HIGHEST, preferred_element_type=jnp.float32)

def take_block(theta, offset, rows, cols, fan_in):
    block = theta[offset:offset + rows * cols].reshape(rows, cols) * fan_in ** (-0.5)
    return (block, offset + rows * cols)

def frame_energy(theta, coords, species_row, neighbour_rows, coupling):
    atoms_n = coords.shape[1]
    slots_n = neighbour_rows.shape[0]
    offset = 0
    embed, offset = take_block(theta, offset, C, SPECIES, 1.0)
    onehot = (species_row[None, :] == jnp.arange(SPECIES, dtype=jnp.int32)[:, None]).astype(jnp.float32)
    features = mult(embed, onehot)
    partner = jnp.maximum(neighbour_rows, 0).reshape(-1)
    present = (neighbour_rows >= 0).reshape(-1)
    others = jnp.take(coords, partner, axis=1)
    own_pos = jnp.tile(coords, (1, slots_n))
    delta = others - own_pos
    radius = jnp.sqrt(lax.optimization_barrier(jnp.sum(delta * delta, axis=0)) + SOFTENING)
    atom_ids = jnp.tile(jnp.arange(atoms_n, dtype=jnp.int32), slots_n)
    crossing = (atom_ids < SOLUTE) != (partner < SOLUTE)
    envelope = (1.0 - (radius / RADIUS_CUT) ** 2) ** 2
    factor = jnp.where(present, envelope, 0.0) * jnp.where(crossing, coupling, 1.0)
    orders = jnp.arange(1, NB + 1).astype(jnp.float32)
    basis = jnp.sqrt(2.0 / RADIUS_CUT) * jnp.sin(orders[:, None] * jnp.pi * radius[None, :] / RADIUS_CUT) / radius[None, :]
    energy = jnp.zeros((), jnp.float32)
    for layer_id in range(LAYERS):
        w_one, offset = take_block(theta, offset, HID, NB, NB)
        w_two, offset = take_block(theta, offset, HID, HID, HID)
        w_three, offset = take_block(theta, offset, C, HID, HID)
        w_up, offset = take_block(theta, offset, C, C, C)
        w_lin, offset = take_block(theta, offset, C, C, C)
        w_sq, offset = take_block(theta, offset, C, C, C)
        w_skip, offset = take_block(theta, offset, C, C, C)
        w_read, offset = take_block(theta, offset, C, 1, C)
        radial = mult(w_three, jax.nn.silu(mult(w_two, jax.nn.silu(mult(w_one, basis)))))
        lifted = mult(w_up, features)
        carried = jnp.take(lifted, partner, axis=1)
        message = radial * carried * factor[None, :]
        pooled = message.reshape(C, slots_n, atoms_n).sum(axis=1) / slots_n
        features = mult(w_lin, pooled) + mult(w_sq, pooled * pooled) + mult(w_skip, features)
        energy = energy + jnp.sum(w_read * features)
    w_head, offset = take_block(theta, offset, RO, C, C)
    w_out, offset = take_block(theta, offset, RO, 1, RO)
    energy = energy + jnp.sum(w_out * jax.nn.silu(mult(w_head, features)))
    return energy

def frame_pair(theta, coords, species_row, neighbour_rows, coupling):

    def energy_of(value):
        return frame_energy(theta, coords, species_row, neighbour_rows, value)
    return jax.jvp(energy_of, (coupling,), (jnp.ones_like(coupling),))

def trapezoid():
    index = jnp.arange(WINDOWS, dtype=jnp.int32)
    edges = (index == 0) | (index == WINDOWS - 1)
    return jnp.where(edges, 0.5, 1.0).astype(jnp.float32) / (WINDOWS - 1)

def adam_step(params, first_moment, second_moment, unit):
    new_first = 0.9 * first_moment + 0.1 * unit
    new_second = 0.999 * second_moment + 0.001 * unit * unit
    unbiased_first = new_first / (1.0 - 0.9 ** 10)
    unbiased_second = new_second / (1.0 - 0.999 ** 10)
    new_params = params - 0.01 * unbiased_first / (jnp.sqrt(unbiased_second) + 1e-08)
    return (new_params, new_first, new_second)

def reference(params, first_moment, second_moment, positions, species, neighbours, window_of, frame_count):
    theta = params
    slot_ids = jnp.arange(F_SLOT, dtype=jnp.int32)
    live = (slot_ids[None, :] < frame_count[:, None]).reshape(-1)
    onehot = (window_of[:, None] == jnp.arange(WINDOWS, dtype=jnp.int32)[None, :]).astype(jnp.float32)
    onehot = onehot * live[:, None].astype(jnp.float32)
    sizes = lax.optimization_barrier(jnp.sum(onehot, axis=0))
    couplings = window_of.astype(jnp.float32) / (WINDOWS - 1)

    def forward(item):
        coords, species_row, neighbour_rows, coupling, flag = item
        return lax.cond(flag, lambda: frame_pair(theta, coords, species_row, neighbour_rows, coupling)[1], lambda: jnp.zeros((), jnp.float32))
    deriv = lax.map(forward, (positions, species, neighbours, couplings, live))
    sums = lax.optimization_barrier(jnp.sum(onehot * deriv[:, None], axis=0))
    means = sums / jnp.maximum(sizes, 1.0)
    share = lax.optimization_barrier(jnp.sum(onehot * (trapezoid() / jnp.maximum(sizes, 1.0))[None, :], axis=1))
    centre = lax.optimization_barrier(jnp.sum(onehot * means[None, :], axis=1))
    cot_energy = -share * (deriv - centre)

    def backward(total, item):
        coords, species_row, neighbour_rows, coupling, flag, c_energy, c_deriv = item

        def term():

            def pair_of(th):
                return frame_pair(th, coords, species_row, neighbour_rows, coupling)
            _, pull = jax.vjp(pair_of, theta)
            return pull((c_energy, c_deriv))[0]
        return (total + lax.cond(flag, term, lambda: jnp.zeros((NPAR,), jnp.float32)), None)
    grad, _ = lax.scan(backward, jnp.zeros((NPAR,), jnp.float32), (positions, species, neighbours, couplings, live, cot_energy, share))
    norm = jnp.sqrt(jnp.sum(grad * grad))
    unit = grad * (GRAD_SCALE * math.sqrt(NPAR) / (norm + 1e-06))
    new_params, new_first, new_second = adam_step(params, first_moment, second_moment, unit)
    return (new_params, new_first, new_second, means)
```

```python
import math

import jax
import jax.numpy as jnp
from jax import lax
from jax.experimental import pallas as pl
from jax.experimental.pallas import tpu as pltpu
from jax.sharding import Mesh
from jax.sharding import PartitionSpec as P

C = 128
HID = 64
NB = 8
SPECIES = 10
RO = 16
LAYERS = 2
WINDOWS = 32
ATOMS = 128
SOLUTE = 16
K = 16
SLOTS = K - 1
EDGES = SLOTS * ATOMS
NPAR = 160272
ROWS = 1280

RADIUS_CUT = 8.0
SOFTENING = 0.01
GRAD_SCALE = 4.0

ROW_EMBED = 0
ROW_LAYER = 10
LAYER_ROWS = 613
OFF_W1, OFF_W2, OFF_W3, OFF_UP, OFF_LIN, OFF_SQ, OFF_SKIP, OFF_READ = 0, 4, 36, 100, 228, 356, 484, 612
ROW_HEAD = ROW_LAYER + LAYERS * LAYER_ROWS
ROW_OUT = ROW_HEAD + RO
USED_ROWS = ROW_OUT + 1

CHUNKS = ((0, 4), (4, 8), (8, 12), (12, 15))
F32, BF16 = jnp.float32, jnp.bfloat16

N_H0, N_P0, N_CH1, N_CL0, N_CP0, N_H1, N_P1, N_CH2, N_CL1, N_CP1, N_H2, N_CH0 = range(12)
N_NODES = 12


def halves(x):
    hi = x.astype(BF16)
    return hi, (x - hi.astype(F32)).astype(BF16)


def stack_left(w):
    hi, lo = halves(w)
    return jnp.concatenate([hi, hi, lo], axis=1)


def dot(a, b):
    return jnp.dot(a, b, preferred_element_type=F32)


def dot_nt(a, b):
    return lax.dot_general(a, b, (((1,), (1,)), ((), ())), preferred_element_type=F32)


def mm(left, x):
    hi, lo = halves(x)
    return dot(left, jnp.concatenate([hi, lo, hi], axis=0))


def nt_stacked(xs, ys):
    m, n = xs.shape[0] // 2, ys.shape[0] // 2
    o = dot_nt(xs, ys)
    return o[:m, :n] + (o[:m, n:] + o[m:, :n])


def tall(x):
    return jnp.concatenate(halves(x), axis=0)


def nt(x, y):
    return nt_stacked(tall(x), tall(y))


def tile_rows(x, reps):
    return jnp.concatenate([x] * reps, axis=1)


def unflatten(rows, height, width):
    total = None
    for r, row in enumerate(rows):
        place = lax.broadcasted_iota(jnp.int32, (height, 128), 1) + 128 * r
        own = lax.broadcasted_iota(jnp.int32, (height, 128), 0)
        first = own * width
        kept = jnp.where((place >= first) & (place < first + width), jnp.broadcast_to(row, (height, 128)), 0.0)
        col = lax.broadcasted_iota(jnp.int32, (128, 16), 1)
        pos = (lax.broadcasted_iota(jnp.int32, (128, 16), 0) + 128 * r) % width
        pick = (col == pos).astype(BF16)
        a = kept.astype(BF16)
        rest = kept - a.astype(F32)
        b = rest.astype(BF16)
        c = (rest - b.astype(F32)).astype(BF16)
        piece = dot(a, pick) + (dot(b, pick) + dot(c, pick))
        total = piece if total is None else total + piece
    return total


def flatten(mat, height, width, n_rows):
    a = mat.astype(BF16)
    rest = mat - a.astype(F32)
    b = rest.astype(BF16)
    c = (rest - b.astype(F32)).astype(BF16)
    out = []
    for r in range(n_rows):
        col = lax.broadcasted_iota(jnp.int32, (16, 128), 0)
        pos = (lax.broadcasted_iota(jnp.int32, (16, 128), 1) + 128 * r) % width
        pick = (col == pos).astype(BF16)
        spread = dot(a, pick) + (dot(b, pick) + dot(c, pick))
        place = lax.broadcasted_iota(jnp.int32, (height, 128), 1) + 128 * r
        first = lax.broadcasted_iota(jnp.int32, (height, 128), 0) * width
        kept = jnp.where((place >= first) & (place < first + width), spread, 0.0)
        out.append(jnp.sum(kept, axis=0, keepdims=True))
    return out


def silu_parts(z):
    s = 0.5 * jnp.tanh(0.5 * z) + 0.5
    value = z * s
    return value, s + value * (1.0 - s)


def forward_kernel(
    count_ref, lam_ref, th_ref, pos_ref, spc_ref, nb_ref,
    deriv_ref, basis_ref, fac_ref, act_ref, slope_ref, gath_ref, node_ref, head_ref, w3t_ref, w2t_ref,
    w1_s, w2_s, w3_s, up_s, upt_s, mix_s, mixt_s, hd_s, hdt_s, emb_s, read_s, out_s, tmp_s, tmpw_s, oh_s, rad_s, dist_s,
):
    step = pl.program_id(0)

    def column(row):
        return jnp.transpose(jnp.broadcast_to(row, (128, 128)))[:, :1]

    @pl.when(step == 0)
    def _():
        emb = unflatten([th_ref[ROW_EMBED + r : ROW_EMBED + r + 1, :] for r in range(10)], C, SPECIES)
        emb_s[...] = stack_left(emb)
        for l in range(LAYERS):
            o = ROW_LAYER + l * LAYER_ROWS
            w1 = unflatten([th_ref[o + OFF_W1 + r : o + OFF_W1 + r + 1, :] for r in range(4)], HID, NB) * NB ** (-0.5)
            w1_s[l] = stack_left(w1)
            for off, rows, reach, dst, dst_t in ((OFF_W2, 32, HID, w2_s, w2t_ref), (OFF_W3, 64, HID, w3_s, w3t_ref)):
                packed = th_ref[o + off : o + off + rows, :] * reach ** (-0.5)
                tmp_s[pl.ds(0, rows, stride=2), :] = packed
                tmp_s[pl.ds(1, rows, stride=2), :] = pltpu.roll(packed, HID, 1)
                wide = tmp_s[: 2 * rows, :]
                w = wide[:, :HID]
                dst[l] = stack_left(w)
                if rows == 32:
                    wide = jnp.concatenate([wide, wide], axis=0)
                wt = jnp.transpose(wide)[:HID, : 2 * rows]
                dst_t[l] = stack_left(wt)
            mats, mats_t = [], []
            for off in (OFF_LIN, OFF_SQ, OFF_SKIP):
                w = th_ref[o + off : o + off + C, :] * C ** (-0.5)
                mats.append(w)
                mats_t.append(jnp.transpose(w))
            mix_s[l] = stack_left(jnp.concatenate(mats, axis=1))
            mixt_s[l] = stack_left(jnp.concatenate(mats_t, axis=0))
            w = th_ref[o + OFF_UP : o + OFF_UP + C, :] * C ** (-0.5)
            up_s[l] = stack_left(w)
            upt_s[l] = stack_left(jnp.transpose(w))
            read_s[l] = jnp.transpose(
                jnp.broadcast_to(th_ref[o + OFF_READ : o + OFF_READ + 1, :] * C ** (-0.5), (128, 128))
            )
        w = th_ref[ROW_HEAD : ROW_HEAD + RO, :] * C ** (-0.5)
        hd_s[...] = stack_left(w)
        wide = jnp.concatenate([w, jnp.zeros((128 - RO, 128), F32)], axis=0)
        hdt_s[...] = stack_left(jnp.transpose(wide)[:, :RO])
        out_s[...] = jnp.transpose(jnp.broadcast_to(th_ref[ROW_OUT : ROW_OUT + 1, :] * RO ** (-0.5), (128, 128)))[:RO, :]

    @pl.when(step < count_ref[0])
    def _():
        lam = lam_ref[step]
        nb = nb_ref[0]
        partner = jnp.maximum(nb, 0)
        present = nb >= 0
        r2 = jnp.full((K, ATOMS), SOFTENING, F32)
        for d in range(3):
            row = jnp.broadcast_to(pos_ref[0, d : d + 1, :], (K, ATOMS))
            delta = jnp.take_along_axis(row, partner, axis=1) - row
            r2 = r2 + delta * delta
        radius = jnp.sqrt(r2)
        ratio = radius * (1.0 / RADIUS_CUT)
        env = 1.0 - ratio * ratio
        env = jnp.where(present, env * env, 0.0) * (1.0 / K)
        atom = lax.broadcasted_iota(jnp.int32, (K, ATOMS), 1)
        crossing = (atom < SOLUTE) != (partner < SOLUTE)
        fac = jnp.where(crossing, lam * env, env)
        dfac = jnp.where(crossing, env, 0.0)
        fac_ref[0, 0] = fac
        fac_ref[0, 1] = dfac

        angle = ratio * math.pi
        s1 = jnp.sin(angle) * (math.sqrt(2.0 / RADIUS_CUT) / radius)
        twice = 2.0 * jnp.cos(angle)
        prev, cur = jnp.zeros_like(s1), s1
        for m in range(NB):
            dist_s[m * K : (m + 1) * K, :] = cur
            prev, cur = cur, twice * cur - prev
        basis = jnp.concatenate([dist_s[pl.ds(k, NB, stride=K), :] for k in range(SLOTS)], axis=1)
        bhi, blo = basis.astype(BF16).astype(F32), None
        blo = basis - bhi
        wide = jnp.concatenate([bhi, blo], axis=0).astype(BF16)
        basis_ref[0] = wide
        w1_rhs = jnp.concatenate([bhi, jnp.zeros_like(bhi), blo, jnp.zeros_like(bhi), bhi, jnp.zeros_like(bhi)], axis=0).astype(BF16)

        sub = lax.broadcasted_iota(jnp.int32, (ATOMS, ATOMS), 0)
        for k in range(SLOTS):
            hit = jnp.broadcast_to(partner[k : k + 1, :], (ATOMS, ATOMS)) == sub
            oh_s[:, k * ATOMS : (k + 1) * ATOMS] = jnp.where(hit, 1.0, 0.0).astype(BF16)

        for l in range(LAYERS):
            for k0, k1 in CHUNKS:
                e = slice(k0 * ATOMS, k1 * ATOMS)
                z1 = dot(w1_s[l], w1_rhs[:, e])
                v1, d1 = silu_parts(z1)
                h1, l1 = halves(v1)
                act_ref[0, l, 0, :HID, e] = h1
                act_ref[0, l, 0, HID:, e] = l1
                slope_ref[0, l, 0, :, e] = d1
                z2 = dot(w2_s[l], jnp.concatenate([h1, l1, h1], axis=0))
                v2, d2 = silu_parts(z2)
                h2, l2 = halves(v2)
                act_ref[0, l, 1, :HID, e] = h2
                act_ref[0, l, 1, HID:, e] = l2
                slope_ref[0, l, 1, :, e] = d2
                rad_s[l, :, e] = dot(w3_s[l], jnp.concatenate([h2, l2, h2], axis=0))

        rows16 = lax.broadcasted_iota(jnp.int32, (16, ATOMS), 0)
        spc = jnp.where(rows16 == jnp.broadcast_to(spc_ref[0], (16, ATOMS)), 1.0, 0.0)
        feat = mm(emb_s[...], spc)
        zero = jnp.zeros((C, ATOMS), F32)
        feat = jnp.concatenate([feat, zero], axis=1)
        deriv = jnp.zeros((), F32)
        pools = []
        for l in range(LAYERS):
            node_ref[0, (N_H0, N_H1)[l]] = feat
            if l == 0:
                lift = mm(up_s[l], feat[:, :ATOMS])
                lhs = jnp.concatenate(halves(lift), axis=1)
            else:
                lift = mm(up_s[l], feat)
                lhs = jnp.concatenate(
                    [jnp.concatenate(halves(lift[:, :ATOMS]), axis=1), jnp.concatenate(halves(lift[:, ATOMS:]), axis=1)],
                    axis=0,
                )
            pool, dpool = zero, zero
            for k0, k1 in CHUNKS:
                e = slice(k0 * ATOMS, k1 * ATOMS)
                oh = oh_s[:, e]
                g = dot(lhs, jnp.concatenate([oh, oh], axis=0))
                if l == 0:
                    gath_ref[0, 0, :, e] = g
                else:
                    gath_ref[0, 1, :, e] = g[:C]
                    gath_ref[0, 2, :, e] = g[C:]
                for k in range(k0, k1):
                    t = slice((k - k0) * ATOMS, (k - k0 + 1) * ATOMS)
                    rad = rad_s[l, :, k * ATOMS : (k + 1) * ATOMS]
                    rg = rad * g[:C, t]
                    pool = pool + fac[k : k + 1, :] * rg
                    dpool = dpool + dfac[k : k + 1, :] * rg
                    if l == 1:
                        dpool = dpool + fac[k : k + 1, :] * (rad * g[C:, t])
            node_ref[0, (N_P0, N_P1)[l]] = jnp.concatenate([pool, dpool], axis=1)
            pools.append((pool, dpool))
            x = jnp.concatenate(
                [
                    jnp.concatenate([pool, dpool], axis=1),
                    jnp.concatenate([pool * pool, 2.0 * pool * dpool], axis=1),
                    feat,
                ],
                axis=0,
            )
            feat = mm(mix_s[l], x)
            deriv = deriv + jnp.sum(read_s[l] * feat[:, ATOMS:])
        node_ref[0, N_H2] = feat
        q = mm(hd_s[...], feat)
        q0, q1 = q[:, :ATOMS], q[:, ATOMS:]
        sg = 0.5 * jnp.tanh(0.5 * q0) + 0.5
        val = q0 * sg
        first = sg + val * (1.0 - sg)
        second = sg * (1.0 - sg) * (2.0 + q0 * (1.0 - 2.0 * sg))
        tail = first * q1
        deriv = deriv + jnp.sum(out_s[...] * tail)
        deriv_ref[0] = jnp.full((8, 128), deriv, F32)
        head_ref[0, 1] = jnp.concatenate([val, tail], axis=1)
        co_q = jnp.concatenate([out_s[...] * first, out_s[...] * second * q1], axis=1)
        head_ref[0, 0] = co_q
        co = mm(hdt_s[...], co_q) + jnp.concatenate([read_s[1], zero], axis=1)
        for l in (1, 0):
            node_ref[0, (N_CH1, N_CH2)[l]] = co
            y = mm(mixt_s[l], co)
            pool, dpool = pools[l]
            ya, yb = y[:, :ATOMS], y[:, ATOMS:]
            ap = ya[:C] + 2.0 * pool * ya[C : 2 * C]
            bp = yb[:C] + 2.0 * pool * yb[C : 2 * C] + 2.0 * dpool * ya[C : 2 * C]
            node_ref[0, (N_CP0, N_CP1)[l]] = jnp.concatenate([ap, bp], axis=1)
            acc = None
            for k0, k1 in CHUNKS:
                parts = [[], [], [], []]
                for k in range(k0, k1):
                    rad = rad_s[l, :, k * ATOMS : (k + 1) * ATOMS]
                    f, df = fac[k : k + 1, :], dfac[k : k + 1, :]
                    ah, al = halves(rad * (f * ap))
                    bh, bl = halves(rad * (f * bp + df * ap))
                    for lst, v in zip(parts, (ah, al, bh, bl)):
                        lst.append(v)
                left = jnp.concatenate([jnp.concatenate(lst, axis=1) for lst in parts], axis=0)
                piece = dot_nt(left, oh_s[:, k0 * ATOMS : k1 * ATOMS])
                acc = piece if acc is None else acc + piece
            cl = jnp.concatenate([acc[:C] + acc[C : 2 * C], acc[2 * C : 3 * C] + acc[3 * C :]], axis=1)
            node_ref[0, (N_CL0, N_CL1)[l]] = cl
            co = y[2 * C :] + mm(upt_s[l], cl)
            if l == 1:
                co = co + jnp.concatenate([read_s[0], zero], axis=1)
        node_ref[0, N_CH0] = co


def backward_kernel(
    count_ref, ce_ref, sh_ref, spc_ref, basis_ref, fac_ref, act_ref, slope_ref, gath_ref, node_ref, head_ref, w3t_ref, w2t_ref,
    grad_ref,
    mix_a, up_a, w3_a, w2_a, w1_a, read_a, head_a, out_a, emb_a, tmp_s,
):
    step = pl.program_id(0)

    @pl.when(step == 0)
    def _():
        for ref in (mix_a, up_a, w3_a, w2_a, w1_a, read_a, head_a, out_a, emb_a):
            ref[...] = jnp.zeros(ref.shape, F32)

    @pl.when(step < count_ref[0])
    def _():
        ce, sh = ce_ref[step], sh_ref[step]
        fac, dfac = fac_ref[0, 0], fac_ref[0, 1]

        def pair(x):
            a, b = x[:, :ATOMS], x[:, ATOMS:]
            return jnp.concatenate([ce * a + sh * b, sh * a], axis=1)

        weights = jnp.concatenate([jnp.full((8, ATOMS), ce, F32), jnp.full((8, ATOMS), sh, F32)], axis=1)
        co0 = node_ref[0, N_CH0]
        a0 = ce * co0[:, :ATOMS] + sh * co0[:, ATOMS:]
        rows16 = lax.broadcasted_iota(jnp.int32, (16, ATOMS), 0)
        spc = jnp.where(rows16 == jnp.broadcast_to(spc_ref[0], (16, ATOMS)), 1.0, 0.0).astype(BF16)
        o = dot_nt(tall(a0), spc)
        emb_a[...] += o[:C] + o[C:]
        head_a[...] += nt(pair(head_ref[0, 0]), node_ref[0, N_H2])
        out_a[...] += nt(weights, head_ref[0, 1])
        for l in range(LAYERS):
            feat = node_ref[0, (N_H0, N_H1)[l]]
            pp = node_ref[0, (N_P0, N_P1)[l]]
            pool, dpool = pp[:, :ATOMS], pp[:, ATOMS:]
            x = jnp.concatenate([pp, jnp.concatenate([pool * pool, 2.0 * pool * dpool], axis=1), feat], axis=0)
            mix_a[l] += nt(pair(node_ref[0, (N_CH1, N_CH2)[l]]), x)
            up_a[l] += nt(pair(node_ref[0, (N_CL0, N_CL1)[l]]), feat)
            read_a[l] += nt(weights, node_ref[0, (N_H1, N_H2)[l]])
            cp = pair(node_ref[0, (N_CP0, N_CP1)[l]])
            ap, bp = cp[:, :ATOMS], cp[:, ATOMS:]
            for k0, k1 in CHUNKS:
                e = slice(k0 * ATOMS, k1 * ATOMS)
                parts = []
                for k in range(k0, k1):
                    t = slice(k * ATOMS, (k + 1) * ATOMS)
                    f, df = fac[k : k + 1, :], dfac[k : k + 1, :]
                    u = f * ap + df * bp
                    if l == 0:
                        parts.append(gath_ref[0, 0, :, t] * u)
                    else:
                        parts.append(gath_ref[0, 1, :, t] * u + gath_ref[0, 2, :, t] * (f * bp))
                rh, rl = halves(jnp.concatenate(parts, axis=1))
                w3_a[l] += nt_stacked(jnp.concatenate([rh, rl], axis=0), act_ref[0, l, 1, :, e])
                c2 = dot(w3t_ref[l], jnp.concatenate([rh, rl, rh], axis=0)) * slope_ref[0, l, 1, :, e]
                ch, cl = halves(c2)
                w2_a[l] += nt_stacked(jnp.concatenate([ch, cl], axis=0), act_ref[0, l, 0, :, e])
                c1 = dot(w2t_ref[l], jnp.concatenate([ch, cl, ch], axis=0)) * slope_ref[0, l, 0, :, e]
                o = dot_nt(tall(c1), basis_ref[0, :, e])
                w1_a[l] += o[:HID] + o[HID:]

    @pl.when(step == pl.num_programs(0) - 1)
    def _():
        grad_ref[USED_ROWS // 8 * 8 :, :] = jnp.zeros((ROWS - USED_ROWS // 8 * 8, 128), F32)
        for r, row in enumerate(flatten(emb_a[...], C, SPECIES, 10)):
            grad_ref[ROW_EMBED + r : ROW_EMBED + r + 1, :] = row
        for l in range(LAYERS):
            o = ROW_LAYER + l * LAYER_ROWS
            w1 = w1_a[l] * NB ** (-0.5)
            w1 = w1[:, :NB] + w1[:, NB:]
            w1 = jnp.concatenate([w1, jnp.zeros((HID, 8), F32)], axis=1)
            for r, row in enumerate(flatten(w1, HID, NB, 4)):
                grad_ref[o + OFF_W1 + r : o + OFF_W1 + r + 1, :] = row
            for off, rows, acc in ((OFF_W2, 32, w2_a), (OFF_W3, 64, w3_a)):
                w = acc[l] * HID ** (-0.5)
                tmp_s[: 2 * rows, :] = jnp.concatenate([w, jnp.zeros_like(w)], axis=1)
                even = tmp_s[pl.ds(0, rows, stride=2), :]
                odd = tmp_s[pl.ds(1, rows, stride=2), :]
                grad_ref[o + off : o + off + rows, :] = even + pltpu.roll(odd, HID, 1)
            for i, off in enumerate((OFF_LIN, OFF_SQ, OFF_SKIP)):
                grad_ref[o + off : o + off + C, :] = mix_a[l, :, i * C : (i + 1) * C] * C ** (-0.5)
            grad_ref[o + OFF_UP : o + OFF_UP + C, :] = up_a[l] * C ** (-0.5)
            grad_ref[o + OFF_READ : o + OFF_READ + 1, :] = read_a[l, :1, :] * C ** (-0.5)
        grad_ref[ROW_HEAD : ROW_HEAD + RO, :] = head_a[...] * C ** (-0.5)
        grad_ref[ROW_OUT : ROW_OUT + 1, :] = jnp.concatenate(
            [out_a[:1, :] * RO ** (-0.5), jnp.zeros((1, 128 - RO), F32)], axis=1
        )


def frame_spec(shape, memory_space=None):
    def index(i, count):
        return (jnp.minimum(i, count[0] - 1),) + (0,) * (len(shape) - 1)

    return pl.BlockSpec(shape, index)


def whole_spec(shape):
    return pl.BlockSpec(shape, lambda i, count: (0,) * len(shape))


SMEM_SPEC = pl.BlockSpec(memory_space=pltpu.SMEM)
SAVED = (
    ((2 * NB, EDGES), BF16),
    ((2, K, ATOMS), F32),
    ((LAYERS, 2, 2 * HID, EDGES), BF16),
    ((LAYERS, 2, HID, EDGES), F32),
    ((3, C, EDGES), F32),
    ((N_NODES, C, 2 * ATOMS), F32),
    ((2, RO, 2 * ATOMS), F32),
)
WEIGHTS = (((LAYERS, HID, 3 * C), BF16), ((LAYERS, HID, 3 * HID), BF16))


def run_forward(count, lam, theta, positions, species, neighbours):
    n = positions.shape[0]
    shapes = [((8, 128), F32)] + list(SAVED)
    return pl.pallas_call(
        forward_kernel,
        grid_spec=pltpu.PrefetchScalarGridSpec(
            num_scalar_prefetch=1,
            grid=(n,),
            in_specs=[
                SMEM_SPEC,
                whole_spec((ROWS, 128)),
                frame_spec((1, 3, ATOMS)),
                frame_spec((1, 1, ATOMS)),
                frame_spec((1, K, ATOMS)),
            ],
            out_specs=[frame_spec((1,) + s) for s, _ in shapes] + [whole_spec(s) for s, _ in WEIGHTS],
            scratch_shapes=[
                pltpu.VMEM((LAYERS, HID, 48), BF16),
                pltpu.VMEM((LAYERS, HID, 3 * HID), BF16),
                pltpu.VMEM((LAYERS, C, 3 * HID), BF16),
                pltpu.VMEM((LAYERS, C, 3 * C), BF16),
                pltpu.VMEM((LAYERS, C, 3 * C), BF16),
                pltpu.VMEM((LAYERS, C, 9 * C), BF16),
                pltpu.VMEM((LAYERS, 3 * C, 3 * C), BF16),
                pltpu.VMEM((RO, 3 * C), BF16),
                pltpu.VMEM((C, 3 * RO), BF16),
                pltpu.VMEM((C, 48), BF16),
                pltpu.VMEM((LAYERS, C, 128), F32),
                pltpu.VMEM((RO, 128), F32),
                pltpu.VMEM((128, 128), F32),
                pltpu.VMEM((128, 128), F32),
                pltpu.VMEM((ATOMS, EDGES), BF16),
                pltpu.VMEM((LAYERS, C, EDGES), F32),
                pltpu.VMEM((NB * K, ATOMS), F32),
            ],
        ),
        out_shape=[jax.ShapeDtypeStruct((n,) + s, t) for s, t in shapes]
        + [jax.ShapeDtypeStruct(s, t) for s, t in WEIGHTS],
        compiler_params=pltpu.CompilerParams(vmem_limit_bytes=56 * 2**20),
        name="forward",
    )(count, lam, theta, positions, species.reshape(n, 1, ATOMS), neighbours)


def run_backward(count, cot, share, species, saved):
    n = species.shape[0]
    return pl.pallas_call(
        backward_kernel,
        grid_spec=pltpu.PrefetchScalarGridSpec(
            num_scalar_prefetch=1,
            grid=(n,),
            in_specs=[SMEM_SPEC, SMEM_SPEC, frame_spec((1, 1, ATOMS))]
            + [frame_spec((1,) + s) for s, _ in SAVED]
            + [whole_spec(s) for s, _ in WEIGHTS],
            out_specs=whole_spec((ROWS, 128)),
            scratch_shapes=[
                pltpu.VMEM((LAYERS, C, 3 * C), F32),
                pltpu.VMEM((LAYERS, C, C), F32),
                pltpu.VMEM((LAYERS, C, HID), F32),
                pltpu.VMEM((LAYERS, HID, HID), F32),
                pltpu.VMEM((LAYERS, HID, 2 * NB), F32),
                pltpu.VMEM((LAYERS, 8, C), F32),
                pltpu.VMEM((RO, C), F32),
                pltpu.VMEM((8, RO), F32),
                pltpu.VMEM((C, 16), F32),
                pltpu.VMEM((128, 128), F32),
            ],
        ),
        out_shape=jax.ShapeDtypeStruct((ROWS, 128), F32),
        compiler_params=pltpu.CompilerParams(vmem_limit_bytes=56 * 2**20),
        name="backward",
    )(count, cot, share, species.reshape(n, 1, ATOMS), *saved)


def trapezoid():
    index = jnp.arange(WINDOWS, dtype=jnp.int32)
    edges = (index == 0) | (index == WINDOWS - 1)
    return jnp.where(edges, 0.5, 1.0).astype(jnp.float32) / (WINDOWS - 1)


def adam_step(params, first_moment, second_moment, unit):
    new_first = 0.9 * first_moment + 0.1 * unit
    new_second = 0.999 * second_moment + 0.001 * unit * unit
    unbiased_first = new_first / (1.0 - 0.9**10)
    unbiased_second = new_second / (1.0 - 0.999**10)
    new_params = params - 0.01 * unbiased_first / (jnp.sqrt(unbiased_second) + 1e-08)
    return (new_params, new_first, new_second)


def tally(window_ids, count):
    slot_ids = jnp.arange(window_ids.shape[0], dtype=jnp.int32)
    live = (slot_ids < count).astype(jnp.float32)
    onehot = (window_ids[:, None] == jnp.arange(WINDOWS, dtype=jnp.int32)[None, :]).astype(
        jnp.float32
    )
    return onehot * live[:, None]


AXES = {"x": 4, "y": 4, "z": 8, "core": 2}
CHIP = ("x", "y", "z")
CHIPS = 128


def swap_cores(v):
    return lax.ppermute(v, "core", [(0, 1), (1, 0)])


def sum_small(v):
    v = v + swap_cores(v)
    parts = lax.all_to_all(jnp.broadcast_to(v[None], (CHIPS, 8, 128)), CHIP, 0, 0, tiled=True)
    return jnp.sum(parts, axis=0)


def sum_large(v):
    half = ROWS // 2
    piece = half // CHIPS
    core = lax.axis_index("core")
    own = lax.dynamic_slice_in_dim(v, core * half, half)
    own = own + swap_cores(lax.dynamic_slice_in_dim(v, (1 - core) * half, half))
    parts = lax.all_to_all(own.reshape(CHIPS, piece, 128), CHIP, 0, 0, tiled=True)
    total = jnp.broadcast_to(jnp.sum(parts, axis=0)[None], (CHIPS, piece, 128))
    own = lax.all_to_all(total, CHIP, 0, 0, tiled=True).reshape(half, 128)
    other = swap_cores(own)
    first = core == 0
    return jnp.concatenate([jnp.where(first, own, other), jnp.where(first, other, own)], axis=0)


def on_device(
    params, first_moment, second_moment, positions, species, neighbours, window_of, frame_count
):
    count = frame_count[0]
    onehot = tally(window_of, count)
    couplings = window_of.astype(jnp.float32) / (WINDOWS - 1)
    theta = jnp.pad(params, (0, ROWS * 128 - NPAR)).reshape(ROWS, 128)
    out = run_forward(frame_count, couplings, theta, positions, species, neighbours)
    deriv = jnp.where(jnp.arange(positions.shape[0]) < count, out[0][:, 0, 0], 0.0)
    local = jnp.concatenate([jnp.sum(onehot, axis=0), jnp.sum(onehot * deriv[:, None], axis=0), jnp.zeros((64,), F32)])
    total = sum_small(jnp.broadcast_to(local[None], (8, 128)))[0]
    sizes, sums = total[:WINDOWS], total[WINDOWS : 2 * WINDOWS]
    means = sums / jnp.maximum(sizes, 1.0)
    share = jnp.sum(onehot * (trapezoid() / jnp.maximum(sizes, 1.0))[None, :], axis=1)
    centre = jnp.sum(onehot * means[None, :], axis=1)
    cot_energy = -share * (deriv - centre)
    grad = run_backward(frame_count, cot_energy, share, species, out[1:])
    summed = sum_large(grad).reshape(-1)[:NPAR]
    norm = jnp.sqrt(jnp.sum(summed * summed))
    unit = summed * (GRAD_SCALE * math.sqrt(NPAR) / (norm + 1e-06))
    new_params, new_first, new_second = adam_step(params, first_moment, second_moment, unit)
    return (new_params, new_first, new_second, means)


def solution(mesh):
    axes = tuple(AXES)
    split = Mesh(mesh.devices.reshape(tuple(AXES.values())), axes)
    in_specs = (
        P(),
        P(),
        P(),
        P(axes, None, None),
        P(axes, None),
        P(axes, None, None),
        P(axes),
        P(axes),
    )
    out_specs = (P(), P(), P(), P())
    return jax.shard_map(
        on_device, mesh=split, in_specs=in_specs, out_specs=out_specs, check_vma=False
    )
```

```python
import math

import jax
import jax.numpy as jnp
from jax import lax
from jax.experimental import pallas as pl
from jax.experimental.pallas import tpu as pltpu
from jax.sharding import Mesh
from jax.sharding import PartitionSpec as P

C = 128
HID = 64
NB = 8
SPECIES = 10
RO = 16
LAYERS = 2
WINDOWS = 32
ATOMS = 128
SOLUTE = 16
K = 16
SLOTS = K - 1
EDGES = SLOTS * ATOMS
NPAR = 160272
ROWS = 1280

RADIUS_CUT = 8.0
SOFTENING = 0.01
GRAD_SCALE = 4.0

ROW_EMBED = 0
ROW_LAYER = 10
LAYER_ROWS = 613
OFF_W1, OFF_W2, OFF_W3, OFF_UP, OFF_LIN, OFF_SQ, OFF_SKIP, OFF_READ = 0, 4, 36, 100, 228, 356, 484, 612
ROW_HEAD = ROW_LAYER + LAYERS * LAYER_ROWS
ROW_OUT = ROW_HEAD + RO
USED_ROWS = ROW_OUT + 1

ROW_POS, ROW_SPECIES, ROW_META, FRAME_ROWS = SLOTS, SLOTS + 3, SLOTS + 4, 24
KEEP = 4
GROUP = 16
PLAN_COUNT, PLAN_OWN = 8, 9

CHUNKS = ((0, 4), (4, 8), (8, 12), (12, 15))
F32, BF16 = jnp.float32, jnp.bfloat16

N_H0, N_P0, N_CH1, N_CL0, N_CP0, N_H1, N_P1, N_CH2, N_CL1, N_CP1, N_H2, N_CH0 = range(12)
N_NODES = 12


def halves(x):
    hi = x.astype(BF16)
    return hi, (x - hi.astype(F32)).astype(BF16)


def stack_left(w):
    hi, lo = halves(w)
    return jnp.concatenate([hi, hi, lo], axis=1)


def dot(a, b):
    return jnp.dot(a, b, preferred_element_type=F32)


def dot_nt(a, b):
    return lax.dot_general(a, b, (((1,), (1,)), ((), ())), preferred_element_type=F32)


def mm(left, x):
    hi, lo = halves(x)
    return dot(left, jnp.concatenate([hi, lo, hi], axis=0))


def nt_stacked(xs, ys):
    m, n = xs.shape[0] // 2, ys.shape[0] // 2
    o = dot_nt(xs, ys)
    return o[:m, :n] + (o[:m, n:] + o[m:, :n])


def tall(x):
    return jnp.concatenate(halves(x), axis=0)


def nt(x, y):
    return nt_stacked(tall(x), tall(y))


def tile_rows(x, reps):
    return jnp.concatenate([x] * reps, axis=1)


def unflatten(rows, height, width):
    total = None
    for r, row in enumerate(rows):
        place = lax.broadcasted_iota(jnp.int32, (height, 128), 1) + 128 * r
        own = lax.broadcasted_iota(jnp.int32, (height, 128), 0)
        first = own * width
        kept = jnp.where((place >= first) & (place < first + width), jnp.broadcast_to(row, (height, 128)), 0.0)
        col = lax.broadcasted_iota(jnp.int32, (128, 16), 1)
        pos = (lax.broadcasted_iota(jnp.int32, (128, 16), 0) + 128 * r) % width
        pick = (col == pos).astype(BF16)
        a = kept.astype(BF16)
        rest = kept - a.astype(F32)
        b = rest.astype(BF16)
        c = (rest - b.astype(F32)).astype(BF16)
        piece = dot(a, pick) + (dot(b, pick) + dot(c, pick))
        total = piece if total is None else total + piece
    return total


def flatten(mat, height, width, n_rows):
    a = mat.astype(BF16)
    rest = mat - a.astype(F32)
    b = rest.astype(BF16)
    c = (rest - b.astype(F32)).astype(BF16)
    out = []
    for r in range(n_rows):
        col = lax.broadcasted_iota(jnp.int32, (16, 128), 0)
        pos = (lax.broadcasted_iota(jnp.int32, (16, 128), 1) + 128 * r) % width
        pick = (col == pos).astype(BF16)
        spread = dot(a, pick) + (dot(b, pick) + dot(c, pick))
        place = lax.broadcasted_iota(jnp.int32, (height, 128), 1) + 128 * r
        first = lax.broadcasted_iota(jnp.int32, (height, 128), 0) * width
        kept = jnp.where((place >= first) & (place < first + width), spread, 0.0)
        out.append(jnp.sum(kept, axis=0, keepdims=True))
    return out


def silu_parts(z):
    s = 0.5 * jnp.tanh(0.5 * z) + 0.5
    value = z * s
    return value, s + value * (1.0 - s)


def prepare(th_ref, w1_s, w2_s, w3_s, up_s, upt_s, mix_s, mixt_s, hd_s, hdt_s, emb_s, read_s, out_s, w3t_ref, w2t_ref, tmp_s):
    emb = unflatten([th_ref[ROW_EMBED + r : ROW_EMBED + r + 1, :] for r in range(10)], C, SPECIES)
    emb_s[...] = stack_left(emb)
    for l in range(LAYERS):
        o = ROW_LAYER + l * LAYER_ROWS
        w1 = unflatten([th_ref[o + OFF_W1 + r : o + OFF_W1 + r + 1, :] for r in range(4)], HID, NB) * NB ** (-0.5)
        w1_s[l] = stack_left(w1)
        for off, rows, reach, dst, dst_t in ((OFF_W2, 32, HID, w2_s, w2t_ref), (OFF_W3, 64, HID, w3_s, w3t_ref)):
            packed = th_ref[o + off : o + off + rows, :] * reach ** (-0.5)
            tmp_s[pl.ds(0, rows, stride=2), :] = packed
            tmp_s[pl.ds(1, rows, stride=2), :] = pltpu.roll(packed, HID, 1)
            wide = tmp_s[: 2 * rows, :]
            w = wide[:, :HID]
            dst[l] = stack_left(w)
            if rows == 32:
                wide = jnp.concatenate([wide, wide], axis=0)
            wt = jnp.transpose(wide)[:HID, : 2 * rows]
            dst_t[l] = jnp.concatenate(halves(wt), axis=1)
        mats, mats_t = [], []
        for off in (OFF_LIN, OFF_SQ, OFF_SKIP):
            w = th_ref[o + off : o + off + C, :] * C ** (-0.5)
            mats.append(w)
            mats_t.append(jnp.transpose(w))
        mix_s[l] = stack_left(jnp.concatenate(mats, axis=1))
        mixt_s[l] = stack_left(jnp.concatenate(mats_t, axis=0))
        w = th_ref[o + OFF_UP : o + OFF_UP + C, :] * C ** (-0.5)
        up_s[l] = stack_left(w)
        upt_s[l] = stack_left(jnp.transpose(w))
        read_s[l] = jnp.transpose(
            jnp.broadcast_to(th_ref[o + OFF_READ : o + OFF_READ + 1, :] * C ** (-0.5), (128, 128))
        )
    w = th_ref[ROW_HEAD : ROW_HEAD + RO, :] * C ** (-0.5)
    hd_s[...] = stack_left(w)
    wide = jnp.concatenate([w, jnp.zeros((128 - RO, 128), F32)], axis=0)
    hdt_s[...] = stack_left(jnp.transpose(wide)[:, :RO])
    out_s[...] = jnp.transpose(jnp.broadcast_to(th_ref[ROW_OUT : ROW_OUT + 1, :] * RO ** (-0.5), (128, 128)))[:RO, :]


def run_frame(
    x,
    w1_s, w2_s, w3_s, up_s, upt_s, mix_s, mixt_s, hd_s, hdt_s, emb_s, read_s, out_s,
    deriv_ref, basis_ref, fac_ref, act_ref, slope_ref, first_ref, gath_ref, node_ref, head_ref,
    oh_s, rad_s, dist_s,
):
    window = x[ROW_META : ROW_META + 1, :1]
    lam = window / (WINDOWS - 1)
    slot = lax.broadcasted_iota(jnp.int32, (K, ATOMS), 0)
    nb = jnp.where(slot < SLOTS, x[:K].astype(jnp.int32), -1)
    partner = jnp.maximum(nb, 0)
    present = nb >= 0
    species = x[ROW_SPECIES : ROW_SPECIES + 1, :]
    r2 = jnp.full((K, ATOMS), SOFTENING, F32)
    for d in range(3):
        row = jnp.broadcast_to(x[ROW_POS + d : ROW_POS + d + 1, :], (K, ATOMS))
        delta = jnp.take_along_axis(row, partner, axis=1) - row
        r2 = r2 + delta * delta
    radius = jnp.sqrt(r2)
    ratio = radius * (1.0 / RADIUS_CUT)
    env = 1.0 - ratio * ratio
    env = jnp.where(present, env * env, 0.0) * (1.0 / K)
    atom = lax.broadcasted_iota(jnp.int32, (K, ATOMS), 1)
    crossing = (atom < SOLUTE) != (partner < SOLUTE)
    fac = jnp.where(crossing, lam * env, env)
    dfac = jnp.where(crossing, env, 0.0)
    fac_ref[0, 0] = fac
    fac_ref[0, 1] = dfac
    fac_ref[0, 2] = jnp.broadcast_to(species, (K, ATOMS))

    angle = ratio * math.pi
    s1 = jnp.sin(angle) * (math.sqrt(2.0 / RADIUS_CUT) / radius)
    twice = 2.0 * jnp.cos(angle)
    prev, cur = jnp.zeros_like(s1), s1
    for m in range(NB):
        dist_s[m * K : (m + 1) * K, :] = cur
        prev, cur = cur, twice * cur - prev
    basis = jnp.concatenate([dist_s[pl.ds(k, NB, stride=K), :] for k in range(SLOTS)], axis=1)
    bhi, blo = basis.astype(BF16).astype(F32), None
    blo = basis - bhi
    wide = jnp.concatenate([bhi, blo], axis=0).astype(BF16)
    basis_ref[0] = wide
    w1_rhs = jnp.concatenate([bhi, jnp.zeros_like(bhi), blo, jnp.zeros_like(bhi), bhi, jnp.zeros_like(bhi)], axis=0).astype(BF16)

    sub = lax.broadcasted_iota(jnp.int32, (ATOMS, ATOMS), 0)
    for k in range(SLOTS):
        hit = jnp.broadcast_to(partner[k : k + 1, :], (ATOMS, ATOMS)) == sub
        oh_s[:, k * ATOMS : (k + 1) * ATOMS] = jnp.where(hit, 1.0, 0.0).astype(BF16)

    for l in range(LAYERS):
        for k0, k1 in CHUNKS:
            e = slice(k0 * ATOMS, k1 * ATOMS)
            z1 = dot(w1_s[l], w1_rhs[:, e])
            v1, d1 = silu_parts(z1)
            h1, l1 = halves(v1)
            act_ref[0, l, 0, :, e] = h1
            slope_ref[0, l, 0, :, e] = d1.astype(BF16)
            z2 = dot(w2_s[l], jnp.concatenate([h1, l1, h1], axis=0))
            v2, d2 = silu_parts(z2)
            h2, l2 = halves(v2)
            act_ref[0, l, 1, :, e] = h2
            slope_ref[0, l, 1, :, e] = d2.astype(BF16)
            rad_s[l, :, e] = dot(w3_s[l], jnp.concatenate([h2, l2, h2], axis=0))

    rows16 = lax.broadcasted_iota(jnp.int32, (16, ATOMS), 0)
    spc = jnp.where(rows16 == jnp.broadcast_to(species, (16, ATOMS)).astype(jnp.int32), 1.0, 0.0)
    feat = mm(emb_s[...], spc)
    zero = jnp.zeros((C, ATOMS), F32)
    feat = jnp.concatenate([feat, zero], axis=1)
    deriv = jnp.zeros((), F32)
    pools = []
    for l in range(LAYERS):
        node_ref[0, (N_H0, N_H1)[l]] = feat
        if l == 0:
            lift = mm(up_s[l], feat[:, :ATOMS])
            lhs = jnp.concatenate(halves(lift), axis=1)
        else:
            lift = mm(up_s[l], feat)
            lhs = jnp.concatenate(
                [jnp.concatenate(halves(lift[:, :ATOMS]), axis=1), jnp.concatenate(halves(lift[:, ATOMS:]), axis=1)],
                axis=0,
            )
        pool, dpool = zero, zero
        for k0, k1 in CHUNKS:
            e = slice(k0 * ATOMS, k1 * ATOMS)
            oh = oh_s[:, e]
            g = dot(lhs, jnp.concatenate([oh, oh], axis=0))
            if l == 0:
                first_ref[0, :, e] = g
            else:
                gath_ref[0, 0, :, e] = g[:C].astype(BF16)
                gath_ref[0, 1, :, e] = g[C:].astype(BF16)
            for k in range(k0, k1):
                t = slice((k - k0) * ATOMS, (k - k0 + 1) * ATOMS)
                rad = rad_s[l, :, k * ATOMS : (k + 1) * ATOMS]
                rg = rad * g[:C, t]
                pool = pool + fac[k : k + 1, :] * rg
                dpool = dpool + dfac[k : k + 1, :] * rg
                if l == 1:
                    dpool = dpool + fac[k : k + 1, :] * (rad * g[C:, t])
        node_ref[0, (N_P0, N_P1)[l]] = jnp.concatenate([pool, dpool], axis=1)
        pools.append((pool, dpool))
        x = jnp.concatenate(
            [
                jnp.concatenate([pool, dpool], axis=1),
                jnp.concatenate([pool * pool, 2.0 * pool * dpool], axis=1),
                feat,
            ],
            axis=0,
        )
        feat = mm(mix_s[l], x)
        deriv = deriv + jnp.sum(read_s[l] * feat[:, ATOMS:])
    node_ref[0, N_H2] = feat
    q = mm(hd_s[...], feat)
    q0, q1 = q[:, :ATOMS], q[:, ATOMS:]
    sg = 0.5 * jnp.tanh(0.5 * q0) + 0.5
    val = q0 * sg
    first = sg + val * (1.0 - sg)
    second = sg * (1.0 - sg) * (2.0 + q0 * (1.0 - 2.0 * sg))
    tail = first * q1
    deriv = deriv + jnp.sum(out_s[...] * tail)
    lane = lax.broadcasted_iota(jnp.int32, (8, 128), 1)
    deriv_ref[0] = jnp.where(lane == 0, deriv, jnp.broadcast_to(window, (8, 128)))
    head_ref[0, 1] = jnp.concatenate([val, tail], axis=1)
    co_q = jnp.concatenate([out_s[...] * first, out_s[...] * second * q1], axis=1)
    head_ref[0, 0] = co_q
    co = mm(hdt_s[...], co_q) + jnp.concatenate([read_s[1], zero], axis=1)
    for l in (1, 0):
        node_ref[0, (N_CH1, N_CH2)[l]] = co
        y = mm(mixt_s[l], co)
        pool, dpool = pools[l]
        ya, yb = y[:, :ATOMS], y[:, ATOMS:]
        ap = ya[:C] + 2.0 * pool * ya[C : 2 * C]
        bp = yb[:C] + 2.0 * pool * yb[C : 2 * C] + 2.0 * dpool * ya[C : 2 * C]
        node_ref[0, (N_CP0, N_CP1)[l]] = jnp.concatenate([ap, bp], axis=1)
        acc = None
        for k0, k1 in CHUNKS:
            parts = [[], []]
            for k in range(k0, k1):
                rad = rad_s[l, :, k * ATOMS : (k + 1) * ATOMS]
                f, df = fac[k : k + 1, :], dfac[k : k + 1, :]
                parts[0].append((rad * (f * ap)).astype(BF16))
                parts[1].append((rad * (f * bp + df * ap)).astype(BF16))
            left = jnp.concatenate([jnp.concatenate(lst, axis=1) for lst in parts], axis=0)
            piece = dot_nt(left, oh_s[:, k0 * ATOMS : k1 * ATOMS])
            acc = piece if acc is None else acc + piece
        cl = jnp.concatenate([acc[:C], acc[C:]], axis=1)
        node_ref[0, (N_CL0, N_CL1)[l]] = cl
        co = y[2 * C :] + mm(upt_s[l], cl)
        if l == 1:
            co = co + jnp.concatenate([read_s[0], zero], axis=1)
    node_ref[0, N_CH0] = co
    at = jnp.broadcast_to(window.astype(jnp.int32), (8, 128))
    return jnp.where(lane == at, 1.0, jnp.where(lane == at + WINDOWS, deriv, 0.0))


N_WEIGHTS = 12
N_SAVED = 9


def pack_kernel(count_ref, window_ref, pos_ref, spc_ref, nb_ref, own_ref, send_ref, wide_s):
    n = nb_ref.shape[0]
    lane = lax.broadcasted_iota(jnp.int32, (1, 128), 1)
    for f in range(n):
        own_ref[f, :SLOTS, :] = nb_ref[f, :SLOTS, :].astype(F32)
        for d in range(3):
            own_ref[f, ROW_POS + d : ROW_POS + d + 1, :] = pos_ref[d, f : f + 1, :]
        own_ref[f, ROW_SPECIES : ROW_SPECIES + 1, :] = spc_ref[f : f + 1, :].astype(F32)
        own_ref[f, ROW_META + 1 :, :] = jnp.zeros((FRAME_ROWS - ROW_META - 1, 128), F32)
        own_ref[f, ROW_META : ROW_META + 1, :] = jnp.where(lane == 0, window_ref[f], count_ref[0]).astype(F32)
    for f in range(KEEP, n):
        wide_s[(f - KEEP) * FRAME_ROWS : (f - KEEP + 1) * FRAME_ROWS, :] = own_ref[f]
    wide = wide_s[...]
    for g in range(GROUP):
        send_ref[g] = wide


def deal_kernel(me_ref, rows_ref, plan_ref):
    n = 8
    lane = lax.broadcasted_iota(jnp.int32, (GROUP, 128), 1)
    gid = lax.broadcasted_iota(jnp.int32, (GROUP, 128), 0)
    meta = rows_ref[:, ROW_META % 8, :]
    counts = jnp.broadcast_to(jnp.sum(jnp.where(lane == 1, meta, 0.0), axis=1, keepdims=True), (GROUP, 128))
    base = jnp.minimum(counts, float(KEEP))
    surplus = counts - base
    total = jnp.sum(surplus, axis=0, keepdims=True)
    lane_f = lane.astype(F32)
    room = jnp.sum(jnp.maximum(lane_f + 1.0 - base, 0.0), axis=0, keepdims=True)
    full = jnp.where((room <= total) & (lane[:1] < n), 1.0, 0.0)
    level = jnp.broadcast_to(jnp.sum(full, axis=1, keepdims=True), (GROUP, 128))
    taken = jnp.maximum(level - base, 0.0)
    left = total - jnp.sum(taken, axis=0, keepdims=True)
    tri_r = lax.broadcasted_iota(jnp.int32, (GROUP, GROUP), 0)
    tri_c = lax.broadcasted_iota(jnp.int32, (GROUP, GROUP), 1)
    before = jnp.where(tri_c < tri_r, 1.0, 0.0).astype(BF16)
    open_ = jnp.where(base <= level, 1.0, 0.0)
    rank = dot(before, open_.astype(BF16))
    taken = taken + jnp.where(rank < left, open_, 0.0)
    offset = dot(before, surplus.astype(BF16))
    me = me_ref[0]
    start = jnp.sum(jnp.where(gid < me, taken, 0.0), axis=0, keepdims=True)
    mine = jnp.sum(jnp.where(gid == me, base + taken, 0.0), axis=0, keepdims=True)
    held = jnp.sum(jnp.where(gid == me, base, 0.0), axis=0, keepdims=True)
    order = jnp.where(lane_f < surplus, offset + lane_f, -1.0)
    place = (gid * (n - KEEP) + lane).astype(F32)
    for j in range(n):
        hit = jnp.where(order == start + float(j), place, 0.0)
        one = jnp.sum(jnp.sum(hit, axis=0, keepdims=True), axis=1, keepdims=True)
        plan_ref[j : j + 1, :] = jnp.broadcast_to(one, (1, 128)).astype(jnp.int32)
    plan_ref[n : n + 1, :] = mine.astype(jnp.int32)
    plan_ref[n + 1 : n + 2, :] = held.astype(jnp.int32)
    plan_ref[n + 2 :, :] = jnp.zeros((GROUP - n - 2, 128), jnp.int32)


def first_kernel(th_ref, own_ref, *refs):
    weights, spare = refs[:N_WEIGHTS], refs[N_WEIGHTS : N_WEIGHTS + 2]
    saved = refs[N_WEIGHTS + 2 : N_WEIGHTS + 2 + N_SAVED]
    tally_ref, oh_s, rad_s, dist_s, tmp_s = refs[N_WEIGHTS + 2 + N_SAVED :]
    prepare(th_ref, *weights, *spare, tmp_s)
    tally_ref[...] = run_frame(own_ref[0], *weights, *saved, oh_s, rad_s, dist_s)


def rest_kernel(plan_ref, own_ref, other_ref, first_ref, *refs):
    weights = refs[:N_WEIGHTS]
    saved = refs[N_WEIGHTS + N_SAVED : N_WEIGHTS + 2 * N_SAVED]
    tally_ref, oh_s, rad_s, dist_s = refs[N_WEIGHTS + 2 * N_SAVED :]
    step = pl.program_id(0)

    @pl.when(step == 0)
    def _():
        tally_ref[...] = first_ref[...]

    @pl.when(step + 1 < plan_ref[PLAN_COUNT, 0])
    def _():
        x = jnp.where(step + 1 < plan_ref[PLAN_OWN, 0], own_ref[0], other_ref[0])
        tally_ref[...] += run_frame(x, *weights, *saved, oh_s, rad_s, dist_s)


def backward_kernel(
    plan_ref, core_ref, parts_ref, deriv_ref, basis_ref, fac_ref, act_ref, slope_ref, first_ref, gath_ref, node_ref, head_ref, w3t_ref, w2t_ref,
    mine_ref, other_ref, means_ref,
    grad_ref, window_s, mix_a, up_a, w3_a, w2_a, w1_a, read_a, head_a, out_a, emb_a, tmp_s,
):
    step = pl.program_id(0)

    @pl.when(step == 0)
    def _():
        for ref in (mix_a, up_a, w3_a, w2_a, w1_a, read_a, head_a, out_a, emb_a):
            ref[...] = jnp.zeros(ref.shape, F32)
        total = jnp.broadcast_to(jnp.sum(parts_ref[...], axis=0, keepdims=True), (8, 128))
        lane = lax.broadcasted_iota(jnp.int32, (8, 128), 1)
        sizes = jnp.maximum(total, 1.0)
        means = pltpu.roll(total, 128 - WINDOWS, 1) / sizes
        ends = (lane == 0) | (lane == WINDOWS - 1)
        weight = jnp.where(ends, 0.5, 1.0) / (WINDOWS - 1)
        means_ref[...] = means
        window_s[0] = means
        window_s[1] = weight / sizes

    @pl.when(step < plan_ref[PLAN_COUNT, 0])
    def _():
        mine = lax.broadcasted_iota(jnp.int32, (1, 128), 1) == deriv_ref[0, :1, 1:2].astype(jnp.int32)
        centre = jnp.sum(jnp.where(mine, window_s[0, :1], 0.0), axis=1, keepdims=True)
        sh = jnp.sum(jnp.where(mine, window_s[1, :1], 0.0), axis=1, keepdims=True)
        ce = -sh * (deriv_ref[0, :1, :1] - centre)
        fac, dfac = fac_ref[0, 0], fac_ref[0, 1]

        def pair(x):
            a, b = x[:, :ATOMS], x[:, ATOMS:]
            return jnp.concatenate([ce * a + sh * b, sh * a], axis=1)

        weights = jnp.concatenate([jnp.broadcast_to(ce, (8, ATOMS)), jnp.broadcast_to(sh, (8, ATOMS))], axis=1)
        co0 = node_ref[0, N_CH0]
        a0 = ce * co0[:, :ATOMS] + sh * co0[:, ATOMS:]
        rows16 = lax.broadcasted_iota(jnp.int32, (16, ATOMS), 0)
        spc = jnp.where(rows16 == fac_ref[0, 2].astype(jnp.int32), 1.0, 0.0).astype(BF16)
        o = dot_nt(tall(a0), spc)
        emb_a[...] += o[:C] + o[C:]
        head_a[...] += nt(pair(head_ref[0, 0]), node_ref[0, N_H2])
        out_a[...] += nt(weights, head_ref[0, 1])
        for l in range(LAYERS):
            feat = node_ref[0, (N_H0, N_H1)[l]]
            pp = node_ref[0, (N_P0, N_P1)[l]]
            pool, dpool = pp[:, :ATOMS], pp[:, ATOMS:]
            x = jnp.concatenate([pp, jnp.concatenate([pool * pool, 2.0 * pool * dpool], axis=1), feat], axis=0)
            mix_a[l] += nt(pair(node_ref[0, (N_CH1, N_CH2)[l]]), x)
            up_a[l] += nt(pair(node_ref[0, (N_CL0, N_CL1)[l]]), feat)
            read_a[l] += nt(weights, node_ref[0, (N_H1, N_H2)[l]])
            cp = pair(node_ref[0, (N_CP0, N_CP1)[l]])
            ap, bp = cp[:, :ATOMS], cp[:, ATOMS:]
            for k0, k1 in CHUNKS:
                e = slice(k0 * ATOMS, k1 * ATOMS)
                parts = []
                for k in range(k0, k1):
                    t = slice(k * ATOMS, (k + 1) * ATOMS)
                    f, df = fac[k : k + 1, :], dfac[k : k + 1, :]
                    u = f * ap + df * bp
                    if l == 0:
                        r = first_ref[0, :, t] * u
                    else:
                        r = gath_ref[0, 0, :, t].astype(F32) * u + gath_ref[0, 1, :, t].astype(F32) * (f * bp)
                    parts.append(r.astype(BF16))
                rh = jnp.concatenate(parts, axis=1)
                w3_a[l] += dot_nt(rh, act_ref[0, l, 1, :, e])
                c2 = (dot(w3t_ref[l], jnp.concatenate([rh, rh], axis=0)) * slope_ref[0, l, 1, :, e].astype(F32)).astype(BF16)
                w2_a[l] += dot_nt(c2, act_ref[0, l, 0, :, e])
                c1 = (dot(w2t_ref[l], jnp.concatenate([c2, c2], axis=0)) * slope_ref[0, l, 0, :, e].astype(F32)).astype(BF16)
                w1_a[l] += dot_nt(c1, basis_ref[0, :, e])

    @pl.when(step == pl.num_programs(0) - 1)
    def _():
        grad_ref[USED_ROWS // 8 * 8 :, :] = jnp.zeros((ROWS - USED_ROWS // 8 * 8, 128), F32)
        for r, row in enumerate(flatten(emb_a[...], C, SPECIES, 10)):
            grad_ref[ROW_EMBED + r : ROW_EMBED + r + 1, :] = row
        for l in range(LAYERS):
            o = ROW_LAYER + l * LAYER_ROWS
            w1 = w1_a[l] * NB ** (-0.5)
            w1 = w1[:, :NB] + w1[:, NB:]
            w1 = jnp.concatenate([w1, jnp.zeros((HID, 8), F32)], axis=1)
            for r, row in enumerate(flatten(w1, HID, NB, 4)):
                grad_ref[o + OFF_W1 + r : o + OFF_W1 + r + 1, :] = row
            for off, rows, acc in ((OFF_W2, 32, w2_a), (OFF_W3, 64, w3_a)):
                w = acc[l] * HID ** (-0.5)
                tmp_s[: 2 * rows, :] = jnp.concatenate([w, jnp.zeros_like(w)], axis=1)
                even = tmp_s[pl.ds(0, rows, stride=2), :]
                odd = tmp_s[pl.ds(1, rows, stride=2), :]
                grad_ref[o + off : o + off + rows, :] = even + pltpu.roll(odd, HID, 1)
            for i, off in enumerate((OFF_LIN, OFF_SQ, OFF_SKIP)):
                grad_ref[o + off : o + off + C, :] = mix_a[l, :, i * C : (i + 1) * C] * C ** (-0.5)
            grad_ref[o + OFF_UP : o + OFF_UP + C, :] = up_a[l] * C ** (-0.5)
            grad_ref[o + OFF_READ : o + OFF_READ + 1, :] = read_a[l, :1, :] * C ** (-0.5)
        grad_ref[ROW_HEAD : ROW_HEAD + RO, :] = head_a[...] * C ** (-0.5)
        grad_ref[ROW_OUT : ROW_OUT + 1, :] = jnp.concatenate(
            [out_a[:1, :] * RO ** (-0.5), jnp.zeros((1, 128 - RO), F32)], axis=1
        )
        half = ROWS // 2
        core = core_ref[0]
        mine_ref[...] = grad_ref[pl.ds(pl.multiple_of(core * half, half), half), :]
        other_ref[...] = grad_ref[pl.ds(pl.multiple_of((1 - core) * half, half), half), :]


def whole_spec(shape):
    return pl.BlockSpec(shape, lambda i, *_: (0,) * len(shape))


SMEM_SPEC = pl.BlockSpec(memory_space=pltpu.SMEM)
SAVED = (
    ((8, 128), F32),
    ((2 * NB, EDGES), BF16),
    ((3, K, ATOMS), F32),
    ((LAYERS, 2, HID, EDGES), BF16),
    ((LAYERS, 2, HID, EDGES), BF16),
    ((C, EDGES), F32),
    ((2, C, EDGES), BF16),
    ((N_NODES, C, 2 * ATOMS), F32),
    ((2, RO, 2 * ATOMS), F32),
)
WEIGHTS = (
    ((LAYERS, HID, 48), BF16),
    ((LAYERS, HID, 3 * HID), BF16),
    ((LAYERS, C, 3 * HID), BF16),
    ((LAYERS, C, 3 * C), BF16),
    ((LAYERS, C, 3 * C), BF16),
    ((LAYERS, C, 9 * C), BF16),
    ((LAYERS, 3 * C, 3 * C), BF16),
    ((RO, 3 * C), BF16),
    ((C, 3 * RO), BF16),
    ((C, 48), BF16),
    ((LAYERS, C, 128), F32),
    ((RO, 128), F32),
)
SPARE = (((LAYERS, HID, 2 * C), BF16), ((LAYERS, HID, 2 * HID), BF16))
FRAME_SCRATCH = [
    pltpu.VMEM((ATOMS, EDGES), BF16),
    pltpu.VMEM((LAYERS, C, EDGES), F32),
    pltpu.VMEM((NB * K, ATOMS), F32),
]
LIMIT = pltpu.CompilerParams(vmem_limit_bytes=56 * 2**20)


TALLY = jax.ShapeDtypeStruct((8, 128), F32)


def run_pack(count, window_of, positions, species, neighbours):
    n = positions.shape[0]
    return pl.pallas_call(
        pack_kernel,
        in_specs=[SMEM_SPEC, SMEM_SPEC] + [pl.BlockSpec(memory_space=pltpu.VMEM)] * 3,
        out_specs=[pl.BlockSpec(memory_space=pltpu.VMEM)] * 2,
        scratch_shapes=[pltpu.VMEM(((n - KEEP) * FRAME_ROWS, 128), F32)],
        out_shape=[
            jax.ShapeDtypeStruct((n, FRAME_ROWS, 128), F32),
            jax.ShapeDtypeStruct((GROUP, (n - KEEP) * FRAME_ROWS, 128), F32),
        ],
        name="pack",
    )(count, window_of, jnp.transpose(positions, (1, 0, 2)), species, neighbours)


def run_deal(me, sent):
    return pl.pallas_call(
        deal_kernel,
        grid=(1,),
        in_specs=[SMEM_SPEC, pl.BlockSpec((GROUP, 8, 128), lambda i: (0, ROW_META // 8, 0))],
        out_specs=whole_spec((GROUP, 128)),
        out_shape=jax.ShapeDtypeStruct((GROUP, 128), jnp.int32),
        name="deal",
    )(me, sent)


def run_first(theta, own):
    n = own.shape[0]
    held = WEIGHTS + SPARE
    out = pl.pallas_call(
        first_kernel,
        grid=(1,),
        in_specs=[whole_spec((ROWS, 128)), whole_spec((1, FRAME_ROWS, 128))],
        out_specs=[whole_spec(s) for s, _ in held] + [whole_spec((1,) + s) for s, _ in SAVED] + [whole_spec(TALLY.shape)],
        scratch_shapes=FRAME_SCRATCH + [pltpu.VMEM((128, 128), F32)],
        out_shape=[jax.ShapeDtypeStruct(s, t) for s, t in held]
        + [jax.ShapeDtypeStruct((n,) + s, t) for s, t in SAVED]
        + [TALLY],
        compiler_params=LIMIT,
        cost_estimate=pl.CostEstimate(flops=10**9, bytes_accessed=4 * 10**7, transcendentals=10**6),
        name="first_frame",
    )(theta, own)
    return out[:N_WEIGHTS], out[N_WEIGHTS : N_WEIGHTS + 2], out[N_WEIGHTS + 2 : -1], out[-1]


def run_rest(plan, own, others, tally, weights, saved):
    n = own.shape[0]

    def own_index(i, plan):
        return (jnp.minimum(i + 1, plan[PLAN_OWN, 0] - 1), 0, 0)

    def other_index(i, plan):
        return (plan[jnp.maximum(i + 1 - plan[PLAN_OWN, 0], 0), 0], 0, 0)

    def saved_spec(shape):
        def index(i, plan):
            return (jnp.maximum(jnp.minimum(i + 1, plan[PLAN_COUNT, 0] - 1), 1),) + (0,) * len(shape)

        return pl.BlockSpec((1,) + shape, index)

    frame = (1, FRAME_ROWS, 128)
    first_saved = 4 + N_WEIGHTS
    out = pl.pallas_call(
        rest_kernel,
        grid_spec=pltpu.PrefetchScalarGridSpec(
            num_scalar_prefetch=1,
            grid=(n - 1,),
            in_specs=[pl.BlockSpec(frame, own_index), pl.BlockSpec(frame, other_index), whole_spec(TALLY.shape)]
            + [whole_spec(s) for s, _ in WEIGHTS]
            + [pl.BlockSpec(memory_space=pl.ANY)] * N_SAVED,
            out_specs=[saved_spec(s) for s, _ in SAVED] + [whole_spec(TALLY.shape)],
            scratch_shapes=FRAME_SCRATCH,
        ),
        out_shape=[jax.ShapeDtypeStruct((n,) + s, t) for s, t in SAVED] + [TALLY],
        input_output_aliases={first_saved + k: k for k in range(N_SAVED)},
        compiler_params=LIMIT,
        name="other_frames",
    )(plan, own, others, tally, *weights, *saved)
    return out[:-1], out[-1]


def run_backward(plan, core, parts, saved, spare):
    n = saved[0].shape[0]

    def saved_spec(shape):
        return pl.BlockSpec((1,) + shape, lambda i, plan: (jnp.minimum(i, plan[PLAN_COUNT, 0] - 1),) + (0,) * len(shape))

    half = (ROWS // 2, 128)
    return pl.pallas_call(
        backward_kernel,
        grid_spec=pltpu.PrefetchScalarGridSpec(
            num_scalar_prefetch=1,
            grid=(n,),
            in_specs=[SMEM_SPEC, whole_spec(parts.shape)]
            + [saved_spec(s) for s, _ in SAVED]
            + [whole_spec(s) for s, _ in SPARE],
            out_specs=[whole_spec(half), whole_spec(half), whole_spec(TALLY.shape)],
            scratch_shapes=[
                pltpu.VMEM((ROWS, 128), F32),
                pltpu.VMEM((2, 8, 128), F32),
                pltpu.VMEM((LAYERS, C, 3 * C), F32),
                pltpu.VMEM((LAYERS, C, C), F32),
                pltpu.VMEM((LAYERS, C, HID), F32),
                pltpu.VMEM((LAYERS, HID, HID), F32),
                pltpu.VMEM((LAYERS, HID, 2 * NB), F32),
                pltpu.VMEM((LAYERS, 8, C), F32),
                pltpu.VMEM((RO, C), F32),
                pltpu.VMEM((8, RO), F32),
                pltpu.VMEM((C, 16), F32),
                pltpu.VMEM((128, 128), F32),
            ],
        ),
        out_shape=[jax.ShapeDtypeStruct(half, F32), jax.ShapeDtypeStruct(half, F32), TALLY],
        compiler_params=LIMIT,
        name="backward",
    )(plan, core, parts, *saved, *spare)


def adam_step(params, first_moment, second_moment, unit):
    new_first = 0.9 * first_moment + 0.1 * unit
    new_second = 0.999 * second_moment + 0.001 * unit * unit
    unbiased_first = new_first / (1.0 - 0.9**10)
    unbiased_second = new_second / (1.0 - 0.999**10)
    new_params = params - 0.01 * unbiased_first / (jnp.sqrt(unbiased_second) + 1e-08)
    return (new_params, new_first, new_second)


AXES = {"x": 4, "y": 4, "z": 8, "core": 2}
PLANE = ("x", "y")
CHIPS = 128
DEPTH = 8


def swap_cores(v):
    return lax.ppermute(v, "core", [(0, 1), (1, 0)])


def gather_tallies(v):
    v = v[:1]
    v = v + swap_cores(v)
    return lax.all_to_all(jnp.broadcast_to(v, (CHIPS, 128)), PLANE + ("z",), 0, 0, tiled=True)


def to_all(v, axes, size):
    return lax.all_to_all(jnp.broadcast_to(v[None], (size,) + v.shape), axes, 0, 0, tiled=True)


def sum_large(mine, other, core):
    half = mine.shape[0]
    piece = half // GROUP
    own = mine + swap_cores(other)
    own = jnp.sum(lax.all_to_all(own.reshape(GROUP, piece, 128), PLANE, 0, 0, tiled=True), axis=0)
    own = jnp.sum(to_all(own, "z", DEPTH), axis=0)
    own = to_all(own, PLANE, GROUP).reshape(half, 128)
    other = swap_cores(own)
    first = core == 0
    return jnp.concatenate([jnp.where(first, own, other), jnp.where(first, other, own)], axis=0)


def on_device(
    params, first_moment, second_moment, positions, species, neighbours, window_of, frame_count
):
    n = positions.shape[0]
    core = lax.axis_index("core")
    own, send = run_pack(frame_count, window_of, positions, species, neighbours)
    sent = lax.all_to_all(send, PLANE, 0, 0, tiled=True)
    theta = jnp.pad(params, (0, ROWS * 128 - NPAR)).reshape(ROWS, 128)
    weights, spare, saved, tally = run_first(theta, own)
    plan = run_deal(lax.axis_index(PLANE)[None], sent)
    others = sent.reshape(GROUP * (n - KEEP), FRAME_ROWS, 128)
    saved, tally = run_rest(plan, own, others, tally, weights, saved)
    mine, other, means = run_backward(plan, core[None], gather_tallies(tally), saved, spare)
    summed = sum_large(mine, other, core).reshape(-1)[:NPAR]
    norm = jnp.sqrt(jnp.sum(summed * summed))
    unit = summed * (GRAD_SCALE * math.sqrt(NPAR) / (norm + 1e-06))
    new_params, new_first, new_second = adam_step(params, first_moment, second_moment, unit)
    return (new_params, new_first, new_second, means[0, :WINDOWS])


def solution(mesh):
    axes = tuple(AXES)
    split = Mesh(mesh.devices.reshape(tuple(AXES.values())), axes)
    in_specs = (
        P(),
        P(),
        P(),
        P(axes, None, None),
        P(axes, None),
        P(axes, None, None),
        P(axes),
        P(axes),
    )
    out_specs = (P(), P(), P(), P())
    return jax.shard_map(
        on_device, mesh=split, in_specs=in_specs, out_specs=out_specs, check_vma=False
    )
```

```python
import math

import jax
import jax.numpy as jnp
from jax import lax
from jax.experimental import pallas as pl
from jax.experimental.pallas import tpu as pltpu
from jax.sharding import Mesh
from jax.sharding import PartitionSpec as P

C = 128
HID = 64
NB = 8
SPECIES = 10
RO = 16
LAYERS = 2
WINDOWS = 32
ATOMS = 128
SOLUTE = 16
K = 16
SLOTS = K - 1
EDGES = SLOTS * ATOMS
NPAR = 160272
ROWS = 1280

RADIUS_CUT = 8.0
SOFTENING = 0.01
GRAD_SCALE = 4.0

ROW_EMBED = 0
ROW_LAYER = 10
LAYER_ROWS = 613
OFF_W1, OFF_W2, OFF_W3, OFF_UP, OFF_LIN, OFF_SQ, OFF_SKIP, OFF_READ = 0, 4, 36, 100, 228, 356, 484, 612
ROW_HEAD = ROW_LAYER + LAYERS * LAYER_ROWS
ROW_OUT = ROW_HEAD + RO
USED_ROWS = ROW_OUT + 1

ROW_POS, ROW_SPECIES, ROW_META, FRAME_ROWS = SLOTS, SLOTS + 3, SLOTS + 4, 24
KEEP = 4
GROUP = 32
PLAN_ROWS = 16
PLAN_COUNT, PLAN_OWN = 8, 9

AXES = {"x": 4, "y": 4, "z": 8, "core": 2}
PLANE = ("x", "y")
PLANE_CHIPS = 16
CHIPS = 128
DEPTH = 8

CHUNKS = ((0, SLOTS),)
F32, BF16 = jnp.float32, jnp.bfloat16

N_H0, N_P0, N_CH1, N_CL0, N_CP0, N_H1, N_P1, N_CH2, N_CL1, N_CP1, N_H2, N_CH0 = range(12)
N_NODES = 12


def halves(x):
    hi = x.astype(BF16)
    return hi, (x - hi.astype(F32)).astype(BF16)


def stack_left(w):
    hi, lo = halves(w)
    return jnp.concatenate([hi, hi, lo], axis=1)


def dot(a, b):
    return jnp.dot(a, b, preferred_element_type=F32)


def dot_nt(a, b):
    return lax.dot_general(a, b, (((1,), (1,)), ((), ())), preferred_element_type=F32)


def mm(left, x):
    hi, lo = halves(x)
    return dot(left, jnp.concatenate([hi, lo, hi], axis=0))


def nt_stacked(xs, ys):
    m, n = xs.shape[0] // 2, ys.shape[0] // 2
    o = dot_nt(xs, ys)
    return o[:m, :n] + (o[:m, n:] + o[m:, :n])


def tall(x):
    return jnp.concatenate(halves(x), axis=0)


def nt(x, y):
    return nt_stacked(tall(x), tall(y))


def tile_rows(x, reps):
    return jnp.concatenate([x] * reps, axis=1)


def unflatten(rows, height, width):
    total = None
    for r, row in enumerate(rows):
        place = lax.broadcasted_iota(jnp.int32, (height, 128), 1) + 128 * r
        own = lax.broadcasted_iota(jnp.int32, (height, 128), 0)
        first = own * width
        kept = jnp.where((place >= first) & (place < first + width), jnp.broadcast_to(row, (height, 128)), 0.0)
        col = lax.broadcasted_iota(jnp.int32, (128, 16), 1)
        pos = (lax.broadcasted_iota(jnp.int32, (128, 16), 0) + 128 * r) % width
        pick = (col == pos).astype(BF16)
        a = kept.astype(BF16)
        rest = kept - a.astype(F32)
        b = rest.astype(BF16)
        c = (rest - b.astype(F32)).astype(BF16)
        piece = dot(a, pick) + (dot(b, pick) + dot(c, pick))
        total = piece if total is None else total + piece
    return total


def flatten(mat, height, width, n_rows):
    a = mat.astype(BF16)
    rest = mat - a.astype(F32)
    b = rest.astype(BF16)
    c = (rest - b.astype(F32)).astype(BF16)
    out = []
    for r in range(n_rows):
        col = lax.broadcasted_iota(jnp.int32, (16, 128), 0)
        pos = (lax.broadcasted_iota(jnp.int32, (16, 128), 1) + 128 * r) % width
        pick = (col == pos).astype(BF16)
        spread = dot(a, pick) + (dot(b, pick) + dot(c, pick))
        place = lax.broadcasted_iota(jnp.int32, (height, 128), 1) + 128 * r
        first = lax.broadcasted_iota(jnp.int32, (height, 128), 0) * width
        kept = jnp.where((place >= first) & (place < first + width), spread, 0.0)
        out.append(jnp.sum(kept, axis=0, keepdims=True))
    return out


def silu_parts(z):
    s = 0.5 * jnp.tanh(0.5 * z) + 0.5
    value = z * s
    return value, s + value * (1.0 - s)


def prepare(th_ref, w1_s, w2_s, w3_s, up_s, upt_s, mix_s, mixt_s, hd_s, hdt_s, emb_s, read_s, out_s, w3t_ref, w2t_ref, tmp_s):
    emb = unflatten([th_ref[ROW_EMBED + r : ROW_EMBED + r + 1, :] for r in range(10)], C, SPECIES)
    emb_s[...] = stack_left(emb)
    for l in range(LAYERS):
        o = ROW_LAYER + l * LAYER_ROWS
        w1 = unflatten([th_ref[o + OFF_W1 + r : o + OFF_W1 + r + 1, :] for r in range(4)], HID, NB) * NB ** (-0.5)
        w1_s[l] = stack_left(w1)
        for off, rows, reach, dst, dst_t in ((OFF_W2, 32, HID, w2_s, w2t_ref), (OFF_W3, 64, HID, w3_s, w3t_ref)):
            packed = th_ref[o + off : o + off + rows, :] * reach ** (-0.5)
            tmp_s[pl.ds(0, rows, stride=2), :] = packed
            tmp_s[pl.ds(1, rows, stride=2), :] = pltpu.roll(packed, HID, 1)
            wide = tmp_s[: 2 * rows, :]
            w = wide[:, :HID]
            dst[l] = stack_left(w)
            if rows == 32:
                wide = jnp.concatenate([wide, wide], axis=0)
            wt = jnp.transpose(wide)[:HID, : 2 * rows]
            dst_t[l] = jnp.concatenate(halves(wt), axis=1)
        mats, mats_t = [], []
        for off in (OFF_LIN, OFF_SQ, OFF_SKIP):
            w = th_ref[o + off : o + off + C, :] * C ** (-0.5)
            mats.append(w)
            mats_t.append(jnp.transpose(w))
        mix_s[l] = stack_left(jnp.concatenate(mats, axis=1))
        mixt_s[l] = stack_left(jnp.concatenate(mats_t, axis=0))
        w = th_ref[o + OFF_UP : o + OFF_UP + C, :] * C ** (-0.5)
        up_s[l] = stack_left(w)
        upt_s[l] = stack_left(jnp.transpose(w))
        read_s[l] = jnp.transpose(
            jnp.broadcast_to(th_ref[o + OFF_READ : o + OFF_READ + 1, :] * C ** (-0.5), (128, 128))
        )
    w = th_ref[ROW_HEAD : ROW_HEAD + RO, :] * C ** (-0.5)
    hd_s[...] = stack_left(w)
    wide = jnp.concatenate([w, jnp.zeros((128 - RO, 128), F32)], axis=0)
    hdt_s[...] = stack_left(jnp.transpose(wide)[:, :RO])
    out_s[...] = jnp.transpose(jnp.broadcast_to(th_ref[ROW_OUT : ROW_OUT + 1, :] * RO ** (-0.5), (128, 128)))[:RO, :]


def run_frame(
    x,
    w1_s, w2_s, w3_s, up_s, upt_s, mix_s, mixt_s, hd_s, hdt_s, emb_s, read_s, out_s,
    deriv_ref, basis_ref, fac_ref, act_ref, slope_ref, first_ref, gath_ref, node_ref, head_ref,
    oh_s, rad_s, dist_s,
):
    window = x[ROW_META : ROW_META + 1, :1]
    lam = window / (WINDOWS - 1)
    slot = lax.broadcasted_iota(jnp.int32, (K, ATOMS), 0)
    nb = jnp.where(slot < SLOTS, x[:K].astype(jnp.int32), -1)
    partner = jnp.maximum(nb, 0)
    present = nb >= 0
    species = x[ROW_SPECIES : ROW_SPECIES + 1, :]
    r2 = jnp.full((K, ATOMS), SOFTENING, F32)
    for d in range(3):
        row = jnp.broadcast_to(x[ROW_POS + d : ROW_POS + d + 1, :], (K, ATOMS))
        delta = jnp.take_along_axis(row, partner, axis=1) - row
        r2 = r2 + delta * delta
    radius = jnp.sqrt(r2)
    ratio = radius * (1.0 / RADIUS_CUT)
    env = 1.0 - ratio * ratio
    env = jnp.where(present, env * env, 0.0) * (1.0 / K)
    atom = lax.broadcasted_iota(jnp.int32, (K, ATOMS), 1)
    crossing = (atom < SOLUTE) != (partner < SOLUTE)
    fac = jnp.where(crossing, lam * env, env)
    dfac = jnp.where(crossing, env, 0.0)
    fac_ref[0, 0] = fac
    fac_ref[0, 1] = dfac
    fac_ref[0, 2] = jnp.broadcast_to(species, (K, ATOMS))

    angle = ratio * math.pi
    s1 = jnp.sin(angle) * (math.sqrt(2.0 / RADIUS_CUT) / radius)
    twice = 2.0 * jnp.cos(angle)
    prev, cur = jnp.zeros_like(s1), s1
    for m in range(NB):
        dist_s[m * K : (m + 1) * K, :] = cur
        prev, cur = cur, twice * cur - prev
    basis = jnp.concatenate([dist_s[pl.ds(k, NB, stride=K), :] for k in range(SLOTS)], axis=1)
    bhi, blo = basis.astype(BF16).astype(F32), None
    blo = basis - bhi
    wide = jnp.concatenate([bhi, blo], axis=0).astype(BF16)
    basis_ref[0] = wide
    w1_rhs = jnp.concatenate([bhi, jnp.zeros_like(bhi), blo, jnp.zeros_like(bhi), bhi, jnp.zeros_like(bhi)], axis=0).astype(BF16)

    sub = lax.broadcasted_iota(jnp.int32, (ATOMS, ATOMS), 0)
    for k in range(SLOTS):
        hit = jnp.broadcast_to(partner[k : k + 1, :], (ATOMS, ATOMS)) == sub
        oh_s[:, k * ATOMS : (k + 1) * ATOMS] = jnp.where(hit, 1.0, 0.0).astype(BF16)

    for l in range(LAYERS):
        for k0, k1 in CHUNKS:
            e = slice(k0 * ATOMS, k1 * ATOMS)
            z1 = dot(w1_s[l], w1_rhs[:, e])
            v1, d1 = silu_parts(z1)
            h1, l1 = halves(v1)
            act_ref[0, l, 0, :, e] = h1
            slope_ref[0, l, 0, :, e] = d1.astype(BF16)
            z2 = dot(w2_s[l], jnp.concatenate([h1, l1, h1], axis=0))
            v2, d2 = silu_parts(z2)
            h2, l2 = halves(v2)
            act_ref[0, l, 1, :, e] = h2
            slope_ref[0, l, 1, :, e] = d2.astype(BF16)
            rad_s[l, :, e] = dot(w3_s[l], jnp.concatenate([h2, l2, h2], axis=0))

    rows16 = lax.broadcasted_iota(jnp.int32, (16, ATOMS), 0)
    spc = jnp.where(rows16 == jnp.broadcast_to(species, (16, ATOMS)).astype(jnp.int32), 1.0, 0.0)
    feat = mm(emb_s[...], spc)
    zero = jnp.zeros((C, ATOMS), F32)
    feat = jnp.concatenate([feat, zero], axis=1)
    deriv = jnp.zeros((), F32)
    pools = []
    for l in range(LAYERS):
        node_ref[0, (N_H0, N_H1)[l]] = feat
        if l == 0:
            lift = mm(up_s[l], feat[:, :ATOMS])
            lhs = jnp.concatenate(halves(lift), axis=1)
        else:
            lift = mm(up_s[l], feat)
            lhs = jnp.concatenate(
                [jnp.concatenate(halves(lift[:, :ATOMS]), axis=1), jnp.concatenate(halves(lift[:, ATOMS:]), axis=1)],
                axis=0,
            )
        pool, dpool = zero, zero
        for k0, k1 in CHUNKS:
            e = slice(k0 * ATOMS, k1 * ATOMS)
            oh = oh_s[:, e]
            g = dot(lhs, jnp.concatenate([oh, oh], axis=0))
            if l == 0:
                first_ref[0, :, e] = g
            else:
                gath_ref[0, 0, :, e] = g[:C].astype(BF16)
                gath_ref[0, 1, :, e] = g[C:].astype(BF16)
            for k in range(k0, k1):
                t = slice((k - k0) * ATOMS, (k - k0 + 1) * ATOMS)
                rad = rad_s[l, :, k * ATOMS : (k + 1) * ATOMS]
                rg = rad * g[:C, t]
                pool = pool + fac[k : k + 1, :] * rg
                dpool = dpool + dfac[k : k + 1, :] * rg
                if l == 1:
                    dpool = dpool + fac[k : k + 1, :] * (rad * g[C:, t])
        node_ref[0, (N_P0, N_P1)[l]] = jnp.concatenate([pool, dpool], axis=1)
        pools.append((pool, dpool))
        x = jnp.concatenate(
            [
                jnp.concatenate([pool, dpool], axis=1),
                jnp.concatenate([pool * pool, 2.0 * pool * dpool], axis=1),
                feat,
            ],
            axis=0,
        )
        feat = mm(mix_s[l], x)
        deriv = deriv + jnp.sum(read_s[l] * feat[:, ATOMS:])
    node_ref[0, N_H2] = feat
    q = mm(hd_s[...], feat)
    q0, q1 = q[:, :ATOMS], q[:, ATOMS:]
    sg = 0.5 * jnp.tanh(0.5 * q0) + 0.5
    val = q0 * sg
    first = sg + val * (1.0 - sg)
    second = sg * (1.0 - sg) * (2.0 + q0 * (1.0 - 2.0 * sg))
    tail = first * q1
    deriv = deriv + jnp.sum(out_s[...] * tail)
    lane = lax.broadcasted_iota(jnp.int32, (8, 128), 1)
    deriv_ref[0] = jnp.where(lane == 0, deriv, jnp.broadcast_to(window, (8, 128)))
    head_ref[0, 1] = jnp.concatenate([val, tail], axis=1)
    co_q = jnp.concatenate([out_s[...] * first, out_s[...] * second * q1], axis=1)
    head_ref[0, 0] = co_q
    co = mm(hdt_s[...], co_q) + jnp.concatenate([read_s[1], zero], axis=1)
    for l in (1, 0):
        node_ref[0, (N_CH1, N_CH2)[l]] = co
        y = mm(mixt_s[l], co)
        pool, dpool = pools[l]
        ya, yb = y[:, :ATOMS], y[:, ATOMS:]
        ap = ya[:C] + 2.0 * pool * ya[C : 2 * C]
        bp = yb[:C] + 2.0 * pool * yb[C : 2 * C] + 2.0 * dpool * ya[C : 2 * C]
        node_ref[0, (N_CP0, N_CP1)[l]] = jnp.concatenate([ap, bp], axis=1)
        acc = None
        for k0, k1 in CHUNKS:
            parts = [[], []]
            for k in range(k0, k1):
                rad = rad_s[l, :, k * ATOMS : (k + 1) * ATOMS]
                f, df = fac[k : k + 1, :], dfac[k : k + 1, :]
                parts[0].append((rad * (f * ap)).astype(BF16))
                parts[1].append((rad * (f * bp + df * ap)).astype(BF16))
            left = jnp.concatenate([jnp.concatenate(lst, axis=1) for lst in parts], axis=0)
            piece = dot_nt(left, oh_s[:, k0 * ATOMS : k1 * ATOMS])
            acc = piece if acc is None else acc + piece
        cl = jnp.concatenate([acc[:C], acc[C:]], axis=1)
        node_ref[0, (N_CL0, N_CL1)[l]] = cl
        co = y[2 * C :] + mm(upt_s[l], cl)
        if l == 1:
            co = co + jnp.concatenate([read_s[0], zero], axis=1)
    node_ref[0, N_CH0] = co
    at = jnp.broadcast_to(window.astype(jnp.int32), (8, 128))
    return jnp.where(lane == at, 1.0, jnp.where(lane == at + WINDOWS, deriv, 0.0))


N_WEIGHTS = 12
N_SAVED = 9


def pack_kernel(count_ref, window_ref, pos_ref, spc_ref, nb_ref, own_ref, send_ref, wide_s):
    n = nb_ref.shape[0]
    lane = lax.broadcasted_iota(jnp.int32, (1, 128), 1)
    for f in range(n):
        own_ref[f, :SLOTS, :] = nb_ref[f, :SLOTS, :].astype(F32)
        for d in range(3):
            own_ref[f, ROW_POS + d : ROW_POS + d + 1, :] = pos_ref[d, f : f + 1, :]
        own_ref[f, ROW_SPECIES : ROW_SPECIES + 1, :] = spc_ref[f : f + 1, :].astype(F32)
        own_ref[f, ROW_META + 1 :, :] = jnp.zeros((FRAME_ROWS - ROW_META - 1, 128), F32)
        own_ref[f, ROW_META : ROW_META + 1, :] = jnp.where(lane == 0, window_ref[f], count_ref[0]).astype(F32)
    for f in range(KEEP, n):
        wide_s[(f - KEEP) * FRAME_ROWS : (f - KEEP + 1) * FRAME_ROWS, :] = own_ref[f]
    wide = wide_s[...]
    for g in range(PLANE_CHIPS):
        send_ref[g] = wide


def deal_kernel(me_ref, here_ref, there_ref, plan_ref):
    n = 8
    lane = lax.broadcasted_iota(jnp.int32, (GROUP, 128), 1)
    gid = lax.broadcasted_iota(jnp.int32, (GROUP, 128), 0)
    core = me_ref[0] // PLANE_CHIPS
    here, there = here_ref[:, ROW_META % 8, :], there_ref[:, ROW_META % 8, :]
    meta = jnp.concatenate([jnp.where(core == 0, here, there), jnp.where(core == 0, there, here)], axis=0)
    counts = jnp.broadcast_to(jnp.sum(jnp.where(lane == 1, meta, 0.0), axis=1, keepdims=True), (GROUP, 128))
    base = jnp.minimum(counts, float(KEEP))
    surplus = counts - base
    total = jnp.sum(surplus, axis=0, keepdims=True)
    lane_f = lane.astype(F32)
    room = jnp.sum(jnp.maximum(lane_f + 1.0 - base, 0.0), axis=0, keepdims=True)
    full = jnp.where((room <= total) & (lane[:1] < n), 1.0, 0.0)
    level = jnp.broadcast_to(jnp.sum(full, axis=1, keepdims=True), (GROUP, 128))
    taken = jnp.maximum(level - base, 0.0)
    left = total - jnp.sum(taken, axis=0, keepdims=True)
    tri_r = lax.broadcasted_iota(jnp.int32, (GROUP, GROUP), 0)
    tri_c = lax.broadcasted_iota(jnp.int32, (GROUP, GROUP), 1)
    before = jnp.where(tri_c < tri_r, 1.0, 0.0).astype(BF16)
    open_ = jnp.where(base <= level, 1.0, 0.0)
    rank = dot(before, open_.astype(BF16))
    taken = taken + jnp.where(rank < left, open_, 0.0)
    offset = dot(before, surplus.astype(BF16))
    me = me_ref[0]
    start = jnp.sum(jnp.where(gid < me, taken, 0.0), axis=0, keepdims=True)
    mine = jnp.sum(jnp.where(gid == me, base + taken, 0.0), axis=0, keepdims=True)
    held = jnp.sum(jnp.where(gid == me, base, 0.0), axis=0, keepdims=True)
    order = jnp.where(lane_f < surplus, offset + lane_f, -1.0)
    place = ((gid % PLANE_CHIPS) * (n - KEEP) + lane).astype(F32)
    away = jnp.where(gid // PLANE_CHIPS == core, 0.0, 1.0)
    for j in range(n):
        hit = order == start + float(j)
        one = jnp.sum(jnp.sum(jnp.where(hit, place, 0.0), axis=0, keepdims=True), axis=1, keepdims=True)
        two = jnp.sum(jnp.sum(jnp.where(hit, away, 0.0), axis=0, keepdims=True), axis=1, keepdims=True)
        plan_ref[j : j + 1, :] = jnp.where(lane[:1] == 0, one, two).astype(jnp.int32)
    plan_ref[n : n + 1, :] = mine.astype(jnp.int32)
    plan_ref[n + 1 : n + 2, :] = held.astype(jnp.int32)
    plan_ref[n + 2 :, :] = jnp.zeros((PLAN_ROWS - n - 2, 128), jnp.int32)


def first_kernel(th_ref, own_ref, *refs):
    weights, spare = refs[:N_WEIGHTS], refs[N_WEIGHTS : N_WEIGHTS + 2]
    saved = refs[N_WEIGHTS + 2 : N_WEIGHTS + 2 + N_SAVED]
    tally_ref, oh_s, rad_s, dist_s, tmp_s = refs[N_WEIGHTS + 2 + N_SAVED :]
    prepare(th_ref, *weights, *spare, tmp_s)
    tally_ref[...] = run_frame(own_ref[0], *weights, *saved, oh_s, rad_s, dist_s)


def rest_kernel(plan_ref, own_ref, here_ref, there_ref, first_ref, *refs):
    weights = refs[:N_WEIGHTS]
    saved = refs[N_WEIGHTS + N_SAVED : N_WEIGHTS + 2 * N_SAVED]
    tally_ref, oh_s, rad_s, dist_s, sum_s = refs[N_WEIGHTS + 2 * N_SAVED :]
    step = pl.program_id(0)

    @pl.when(step == 0)
    def _():
        sum_s[...] = first_ref[...]

    @pl.when(step + 1 < plan_ref[PLAN_COUNT, 0])
    def _():
        own = plan_ref[PLAN_OWN, 0]
        away = plan_ref[jnp.maximum(step + 1 - own, 0), 1]
        x = jnp.where(step + 1 < own, own_ref[0], jnp.where(away == 0, here_ref[0], there_ref[0]))
        sum_s[...] += run_frame(x, *weights, *saved, oh_s, rad_s, dist_s)

    @pl.when(step == pl.num_programs(0) - 1)
    def _():
        tally_ref[...] = jnp.broadcast_to(sum_s[:1, :], (CHIPS, 128))


def backward_kernel(
    plan_ref, core_ref, parts_ref, more_ref, deriv_ref, basis_ref, fac_ref, act_ref, slope_ref, first_ref, gath_ref, node_ref, head_ref, w3t_ref, w2t_ref,
    mine_ref, other_ref, means_ref,
    grad_ref, window_s, mix_a, up_a, w3_a, w2_a, w1_a, read_a, head_a, out_a, emb_a, tmp_s,
):
    step = pl.program_id(0)

    @pl.when(step == 0)
    def _():
        for ref in (mix_a, up_a, w3_a, w2_a, w1_a, read_a, head_a, out_a, emb_a):
            ref[...] = jnp.zeros(ref.shape, F32)
        total = jnp.broadcast_to(jnp.sum(parts_ref[...] + more_ref[...], axis=0, keepdims=True), (8, 128))
        lane = lax.broadcasted_iota(jnp.int32, (8, 128), 1)
        sizes = jnp.maximum(total, 1.0)
        means = pltpu.roll(total, 128 - WINDOWS, 1) / sizes
        ends = (lane == 0) | (lane == WINDOWS - 1)
        weight = jnp.where(ends, 0.5, 1.0) / (WINDOWS - 1)
        means_ref[...] = means
        window_s[0] = means
        window_s[1] = weight / sizes

    @pl.when(step < plan_ref[PLAN_COUNT, 0])
    def _():
        mine = lax.broadcasted_iota(jnp.int32, (1, 128), 1) == deriv_ref[0, :1, 1:2].astype(jnp.int32)
        centre = jnp.sum(jnp.where(mine, window_s[0, :1], 0.0), axis=1, keepdims=True)
        sh = jnp.sum(jnp.where(mine, window_s[1, :1], 0.0), axis=1, keepdims=True)
        ce = -sh * (deriv_ref[0, :1, :1] - centre)
        fac, dfac = fac_ref[0, 0], fac_ref[0, 1]

        def pair(x):
            a, b = x[:, :ATOMS], x[:, ATOMS:]
            return jnp.concatenate([ce * a + sh * b, sh * a], axis=1)

        weights = jnp.concatenate([jnp.broadcast_to(ce, (8, ATOMS)), jnp.broadcast_to(sh, (8, ATOMS))], axis=1)
        co0 = node_ref[0, N_CH0]
        a0 = ce * co0[:, :ATOMS] + sh * co0[:, ATOMS:]
        rows16 = lax.broadcasted_iota(jnp.int32, (16, ATOMS), 0)
        spc = jnp.where(rows16 == fac_ref[0, 2].astype(jnp.int32), 1.0, 0.0).astype(BF16)
        o = dot_nt(tall(a0), spc)
        emb_a[...] += o[:C] + o[C:]
        head_a[...] += nt(pair(head_ref[0, 0]), node_ref[0, N_H2])
        out_a[...] += nt(weights, head_ref[0, 1])
        for l in range(LAYERS):
            feat = node_ref[0, (N_H0, N_H1)[l]]
            pp = node_ref[0, (N_P0, N_P1)[l]]
            pool, dpool = pp[:, :ATOMS], pp[:, ATOMS:]
            x = jnp.concatenate([pp, jnp.concatenate([pool * pool, 2.0 * pool * dpool], axis=1), feat], axis=0)
            mix_a[l] += nt(pair(node_ref[0, (N_CH1, N_CH2)[l]]), x)
            up_a[l] += nt(pair(node_ref[0, (N_CL0, N_CL1)[l]]), feat)
            read_a[l] += nt(weights, node_ref[0, (N_H1, N_H2)[l]])
            cp = pair(node_ref[0, (N_CP0, N_CP1)[l]])
            ap, bp = cp[:, :ATOMS], cp[:, ATOMS:]
            for k0, k1 in CHUNKS:
                e = slice(k0 * ATOMS, k1 * ATOMS)
                parts = []
                for k in range(k0, k1):
                    t = slice(k * ATOMS, (k + 1) * ATOMS)
                    f, df = fac[k : k + 1, :], dfac[k : k + 1, :]
                    u = f * ap + df * bp
                    if l == 0:
                        r = first_ref[0, :, t] * u
                    else:
                        r = gath_ref[0, 0, :, t].astype(F32) * u + gath_ref[0, 1, :, t].astype(F32) * (f * bp)
                    parts.append(r.astype(BF16))
                rh = jnp.concatenate(parts, axis=1)
                w3_a[l] += dot_nt(rh, act_ref[0, l, 1, :, e])
                c2 = (dot(w3t_ref[l], jnp.concatenate([rh, rh], axis=0)) * slope_ref[0, l, 1, :, e].astype(F32)).astype(BF16)
                w2_a[l] += dot_nt(c2, act_ref[0, l, 0, :, e])
                c1 = (dot(w2t_ref[l], jnp.concatenate([c2, c2], axis=0)) * slope_ref[0, l, 0, :, e].astype(F32)).astype(BF16)
                w1_a[l] += dot_nt(c1, basis_ref[0, :, e])

    @pl.when(step == pl.num_programs(0) - 1)
    def _():
        grad_ref[USED_ROWS // 8 * 8 :, :] = jnp.zeros((ROWS - USED_ROWS // 8 * 8, 128), F32)
        for r, row in enumerate(flatten(emb_a[...], C, SPECIES, 10)):
            grad_ref[ROW_EMBED + r : ROW_EMBED + r + 1, :] = row
        for l in range(LAYERS):
            o = ROW_LAYER + l * LAYER_ROWS
            w1 = w1_a[l] * NB ** (-0.5)
            w1 = w1[:, :NB] + w1[:, NB:]
            w1 = jnp.concatenate([w1, jnp.zeros((HID, 8), F32)], axis=1)
            for r, row in enumerate(flatten(w1, HID, NB, 4)):
                grad_ref[o + OFF_W1 + r : o + OFF_W1 + r + 1, :] = row
            for off, rows, acc in ((OFF_W2, 32, w2_a), (OFF_W3, 64, w3_a)):
                w = acc[l] * HID ** (-0.5)
                tmp_s[: 2 * rows, :] = jnp.concatenate([w, jnp.zeros_like(w)], axis=1)
                even = tmp_s[pl.ds(0, rows, stride=2), :]
                odd = tmp_s[pl.ds(1, rows, stride=2), :]
                grad_ref[o + off : o + off + rows, :] = even + pltpu.roll(odd, HID, 1)
            for i, off in enumerate((OFF_LIN, OFF_SQ, OFF_SKIP)):
                grad_ref[o + off : o + off + C, :] = mix_a[l, :, i * C : (i + 1) * C] * C ** (-0.5)
            grad_ref[o + OFF_UP : o + OFF_UP + C, :] = up_a[l] * C ** (-0.5)
            grad_ref[o + OFF_READ : o + OFF_READ + 1, :] = read_a[l, :1, :] * C ** (-0.5)
        grad_ref[ROW_HEAD : ROW_HEAD + RO, :] = head_a[...] * C ** (-0.5)
        grad_ref[ROW_OUT : ROW_OUT + 1, :] = jnp.concatenate(
            [out_a[:1, :] * RO ** (-0.5), jnp.zeros((1, 128 - RO), F32)], axis=1
        )
        half = ROWS // 2
        core = core_ref[0]
        mine_ref[...] = grad_ref[pl.ds(pl.multiple_of(core * half, half), half), :]
        other_ref[...] = grad_ref[pl.ds(pl.multiple_of((1 - core) * half, half), half), :]


def whole_spec(shape):
    return pl.BlockSpec(shape, lambda i, *_: (0,) * len(shape))


SMEM_SPEC = pl.BlockSpec(memory_space=pltpu.SMEM)
SAVED = (
    ((8, 128), F32),
    ((2 * NB, EDGES), BF16),
    ((3, K, ATOMS), F32),
    ((LAYERS, 2, HID, EDGES), BF16),
    ((LAYERS, 2, HID, EDGES), BF16),
    ((C, EDGES), F32),
    ((2, C, EDGES), BF16),
    ((N_NODES, C, 2 * ATOMS), F32),
    ((2, RO, 2 * ATOMS), F32),
)
WEIGHTS = (
    ((LAYERS, HID, 48), BF16),
    ((LAYERS, HID, 3 * HID), BF16),
    ((LAYERS, C, 3 * HID), BF16),
    ((LAYERS, C, 3 * C), BF16),
    ((LAYERS, C, 3 * C), BF16),
    ((LAYERS, C, 9 * C), BF16),
    ((LAYERS, 3 * C, 3 * C), BF16),
    ((RO, 3 * C), BF16),
    ((C, 3 * RO), BF16),
    ((C, 48), BF16),
    ((LAYERS, C, 128), F32),
    ((RO, 128), F32),
)
SPARE = (((LAYERS, HID, 2 * C), BF16), ((LAYERS, HID, 2 * HID), BF16))
FRAME_SCRATCH = [
    pltpu.VMEM((ATOMS, EDGES), BF16),
    pltpu.VMEM((LAYERS, C, EDGES), F32),
    pltpu.VMEM((NB * K, ATOMS), F32),
]
LIMIT = pltpu.CompilerParams(vmem_limit_bytes=56 * 2**20)


TALLY = jax.ShapeDtypeStruct((8, 128), F32)


def run_pack(count, window_of, positions, species, neighbours):
    n = positions.shape[0]
    return pl.pallas_call(
        pack_kernel,
        in_specs=[SMEM_SPEC, SMEM_SPEC] + [pl.BlockSpec(memory_space=pltpu.VMEM)] * 3,
        out_specs=[pl.BlockSpec(memory_space=pltpu.VMEM)] * 2,
        scratch_shapes=[pltpu.VMEM(((n - KEEP) * FRAME_ROWS, 128), F32)],
        out_shape=[
            jax.ShapeDtypeStruct((n, FRAME_ROWS, 128), F32),
            jax.ShapeDtypeStruct((PLANE_CHIPS, (n - KEEP) * FRAME_ROWS, 128), F32),
        ],
        name="pack",
    )(count, window_of, jnp.transpose(positions, (1, 0, 2)), species, neighbours)


def run_deal(me, here, there):
    return pl.pallas_call(
        deal_kernel,
        grid=(1,),
        in_specs=[SMEM_SPEC] + [pl.BlockSpec((PLANE_CHIPS, 8, 128), lambda i: (0, ROW_META // 8, 0))] * 2,
        out_specs=whole_spec((PLAN_ROWS, 128)),
        out_shape=jax.ShapeDtypeStruct((PLAN_ROWS, 128), jnp.int32),
        name="deal",
    )(me, here, there)


def run_first(theta, own):
    n = own.shape[0]
    held = WEIGHTS + SPARE
    out = pl.pallas_call(
        first_kernel,
        grid=(1,),
        in_specs=[whole_spec((ROWS, 128)), whole_spec((1, FRAME_ROWS, 128))],
        out_specs=[whole_spec(s) for s, _ in held] + [whole_spec((1,) + s) for s, _ in SAVED] + [whole_spec(TALLY.shape)],
        scratch_shapes=FRAME_SCRATCH + [pltpu.VMEM((128, 128), F32)],
        out_shape=[jax.ShapeDtypeStruct(s, t) for s, t in held]
        + [jax.ShapeDtypeStruct((n,) + s, t) for s, t in SAVED]
        + [TALLY],
        compiler_params=LIMIT,
        cost_estimate=pl.CostEstimate(flops=10**9, bytes_accessed=4 * 10**7, transcendentals=10**6),
        name="first_frame",
    )(theta, own)
    return out[:N_WEIGHTS], out[N_WEIGHTS : N_WEIGHTS + 2], out[N_WEIGHTS + 2 : -1], out[-1]


def run_rest(plan, own, here, there, tally, weights, saved):
    n = own.shape[0]

    def own_index(i, plan):
        return (jnp.minimum(i + 1, plan[PLAN_OWN, 0] - 1), 0, 0)

    def other_index(i, plan):
        return (plan[jnp.maximum(i + 1 - plan[PLAN_OWN, 0], 0), 0], 0, 0)

    def saved_spec(shape):
        def index(i, plan):
            return (jnp.maximum(jnp.minimum(i + 1, plan[PLAN_COUNT, 0] - 1), 1),) + (0,) * len(shape)

        return pl.BlockSpec((1,) + shape, index)

    frame = (1, FRAME_ROWS, 128)
    first_saved = 5 + N_WEIGHTS
    out = pl.pallas_call(
        rest_kernel,
        grid_spec=pltpu.PrefetchScalarGridSpec(
            num_scalar_prefetch=1,
            grid=(n - 1,),
            in_specs=[pl.BlockSpec(frame, own_index), pl.BlockSpec(frame, other_index), pl.BlockSpec(frame, other_index)]
            + [whole_spec(TALLY.shape)]
            + [whole_spec(s) for s, _ in WEIGHTS]
            + [pl.BlockSpec(memory_space=pl.ANY)] * N_SAVED,
            out_specs=[saved_spec(s) for s, _ in SAVED] + [whole_spec((CHIPS, 128))],
            scratch_shapes=FRAME_SCRATCH + [pltpu.VMEM(TALLY.shape, F32)],
        ),
        out_shape=[jax.ShapeDtypeStruct((n,) + s, t) for s, t in SAVED] + [jax.ShapeDtypeStruct((CHIPS, 128), F32)],
        input_output_aliases={first_saved + k: k for k in range(N_SAVED)},
        compiler_params=LIMIT,
        name="other_frames",
    )(plan, own, here, there, tally, *weights, *saved)
    return out[:-1], out[-1]


def run_backward(plan, core, parts, more, saved, spare):
    n = saved[0].shape[0]

    def saved_spec(shape):
        return pl.BlockSpec((1,) + shape, lambda i, plan: (jnp.minimum(i, plan[PLAN_COUNT, 0] - 1),) + (0,) * len(shape))

    half = (ROWS // 2, 128)
    return pl.pallas_call(
        backward_kernel,
        grid_spec=pltpu.PrefetchScalarGridSpec(
            num_scalar_prefetch=1,
            grid=(n,),
            in_specs=[SMEM_SPEC, whole_spec(parts.shape), whole_spec(parts.shape)]
            + [saved_spec(s) for s, _ in SAVED]
            + [whole_spec(s) for s, _ in SPARE],
            out_specs=[whole_spec(half), whole_spec(half), whole_spec(TALLY.shape)],
            scratch_shapes=[
                pltpu.VMEM((ROWS, 128), F32),
                pltpu.VMEM((2, 8, 128), F32),
                pltpu.VMEM((LAYERS, C, 3 * C), F32),
                pltpu.VMEM((LAYERS, C, C), F32),
                pltpu.VMEM((LAYERS, C, HID), F32),
                pltpu.VMEM((LAYERS, HID, HID), F32),
                pltpu.VMEM((LAYERS, HID, 2 * NB), F32),
                pltpu.VMEM((LAYERS, 8, C), F32),
                pltpu.VMEM((RO, C), F32),
                pltpu.VMEM((8, RO), F32),
                pltpu.VMEM((C, 16), F32),
                pltpu.VMEM((128, 128), F32),
            ],
        ),
        out_shape=[jax.ShapeDtypeStruct(half, F32), jax.ShapeDtypeStruct(half, F32), TALLY],
        compiler_params=LIMIT,
        name="backward",
    )(plan, core, parts, more, *saved, *spare)


def adam_step(params, first_moment, second_moment, unit):
    new_first = 0.9 * first_moment + 0.1 * unit
    new_second = 0.999 * second_moment + 0.001 * unit * unit
    unbiased_first = new_first / (1.0 - 0.9**10)
    unbiased_second = new_second / (1.0 - 0.999**10)
    new_params = params - 0.01 * unbiased_first / (jnp.sqrt(unbiased_second) + 1e-08)
    return (new_params, new_first, new_second)


def swap_cores(v):
    return lax.ppermute(v, "core", [(0, 1), (1, 0)])


def gather_tallies(v):
    own = lax.all_to_all(v, PLANE + ("z",), 0, 0, tiled=True)
    return own, swap_cores(own)


def to_all(v, axes, size):
    return lax.all_to_all(jnp.broadcast_to(v[None], (size,) + v.shape), axes, 0, 0, tiled=True)


def sum_large(mine, other, core):
    half = mine.shape[0]
    piece = half // PLANE_CHIPS
    own = mine + swap_cores(other)
    own = jnp.sum(lax.all_to_all(own.reshape(PLANE_CHIPS, piece, 128), PLANE, 0, 0, tiled=True), axis=0)
    own = jnp.sum(to_all(own, "z", DEPTH), axis=0)
    own = to_all(own, PLANE, PLANE_CHIPS).reshape(half, 128)
    other = swap_cores(own)
    first = core == 0
    return jnp.concatenate([jnp.where(first, own, other), jnp.where(first, other, own)], axis=0)


def on_device(
    params, first_moment, second_moment, positions, species, neighbours, window_of, frame_count
):
    n = positions.shape[0]
    core = lax.axis_index("core")
    own, send = run_pack(frame_count, window_of, positions, species, neighbours)
    here = lax.all_to_all(send, PLANE, 0, 0, tiled=True)
    theta = jnp.pad(params, (0, ROWS * 128 - NPAR)).reshape(ROWS, 128)
    weights, spare, saved, tally = run_first(theta, own)
    here, tally = lax.optimization_barrier((here, tally))
    there = swap_cores(here)
    plan = run_deal((core * PLANE_CHIPS + lax.axis_index(PLANE))[None], here, there)
    here, there = (v.reshape(PLANE_CHIPS * (n - KEEP), FRAME_ROWS, 128) for v in (here, there))
    saved, tally = run_rest(plan, own, here, there, tally, weights, saved)
    mine, other, means = run_backward(plan, core[None], *gather_tallies(tally), saved, spare)
    summed = sum_large(mine, other, core).reshape(-1)[:NPAR]
    norm = jnp.sqrt(jnp.sum(summed * summed))
    unit = summed * (GRAD_SCALE * math.sqrt(NPAR) / (norm + 1e-06))
    new_params, new_first, new_second = adam_step(params, first_moment, second_moment, unit)
    return (new_params, new_first, new_second, means[0, :WINDOWS])


def solution(mesh):
    axes = tuple(AXES)
    split = Mesh(mesh.devices.reshape(tuple(AXES.values())), axes)
    in_specs = (
        P(),
        P(),
        P(),
        P(axes, None, None),
        P(axes, None),
        P(axes, None, None),
        P(axes),
        P(axes),
    )
    out_specs = (P(), P(), P(), P())
    return jax.shard_map(
        on_device, mesh=split, in_specs=in_specs, out_specs=out_specs, check_vma=False
    )
```

```python
import math

import jax
import jax.numpy as jnp
from jax import lax
from jax.experimental import pallas as pl
from jax.experimental.pallas import tpu as pltpu
from jax.sharding import Mesh
from jax.sharding import PartitionSpec as P

C = 128
HID = 64
NB = 8
SPECIES = 10
RO = 16
LAYERS = 2
WINDOWS = 32
ATOMS = 128
SOLUTE = 16
K = 16
SLOTS = K - 1
EDGES = SLOTS * ATOMS
NPAR = 160272
ROWS = 1280

RADIUS_CUT = 8.0
SOFTENING = 0.01
GRAD_SCALE = 4.0

ROW_EMBED = 0
ROW_LAYER = 10
LAYER_ROWS = 613
OFF_W1, OFF_W2, OFF_W3, OFF_UP, OFF_LIN, OFF_SQ, OFF_SKIP, OFF_READ = 0, 4, 36, 100, 228, 356, 484, 612
ROW_HEAD = ROW_LAYER + LAYERS * LAYER_ROWS
ROW_OUT = ROW_HEAD + RO
USED_ROWS = ROW_OUT + 1

ROW_POS, ROW_SPECIES, ROW_META, FRAME_ROWS = SLOTS, SLOTS + 3, SLOTS + 4, 24
KEEP = 4
GROUP = 32
PLAN_ROWS = 16
PLAN_COUNT, PLAN_OWN = 8, 9

AXES = {"x": 4, "y": 4, "z": 8, "core": 2}
PLANE = ("x", "y")
PLANE_CHIPS = 16
CHIPS = 128
DEPTH = 8

F32, BF16 = jnp.float32, jnp.bfloat16


def halves(x):
    hi = x.astype(BF16)
    return hi, (x - hi.astype(F32)).astype(BF16)


def stack_left(w):
    hi, lo = halves(w)
    return jnp.concatenate([hi, hi, lo], axis=1)


def dot(a, b):
    return jnp.dot(a, b, preferred_element_type=F32)


def dot_nt(a, b):
    return lax.dot_general(a, b, (((1,), (1,)), ((), ())), preferred_element_type=F32)


def mm(left, x):
    hi, lo = halves(x)
    return dot(left, jnp.concatenate([hi, lo, hi], axis=0))


def nt_stacked(xs, ys):
    m, n = xs.shape[0] // 2, ys.shape[0] // 2
    o = dot_nt(xs, ys)
    return o[:m, :n] + (o[:m, n:] + o[m:, :n])


def tall(x):
    return jnp.concatenate(halves(x), axis=0)


def nt(x, y):
    return nt_stacked(tall(x), tall(y))


def tile_rows(x, reps):
    return jnp.concatenate([x] * reps, axis=1)


def unflatten(rows, height, width):
    total = None
    for r, row in enumerate(rows):
        place = lax.broadcasted_iota(jnp.int32, (height, 128), 1) + 128 * r
        own = lax.broadcasted_iota(jnp.int32, (height, 128), 0)
        first = own * width
        kept = jnp.where((place >= first) & (place < first + width), jnp.broadcast_to(row, (height, 128)), 0.0)
        col = lax.broadcasted_iota(jnp.int32, (128, 16), 1)
        pos = (lax.broadcasted_iota(jnp.int32, (128, 16), 0) + 128 * r) % width
        pick = (col == pos).astype(BF16)
        a = kept.astype(BF16)
        rest = kept - a.astype(F32)
        b = rest.astype(BF16)
        c = (rest - b.astype(F32)).astype(BF16)
        piece = dot(a, pick) + (dot(b, pick) + dot(c, pick))
        total = piece if total is None else total + piece
    return total


def flatten(mat, height, width, n_rows):
    a = mat.astype(BF16)
    rest = mat - a.astype(F32)
    b = rest.astype(BF16)
    c = (rest - b.astype(F32)).astype(BF16)
    out = []
    for r in range(n_rows):
        col = lax.broadcasted_iota(jnp.int32, (16, 128), 0)
        pos = (lax.broadcasted_iota(jnp.int32, (16, 128), 1) + 128 * r) % width
        pick = (col == pos).astype(BF16)
        spread = dot(a, pick) + (dot(b, pick) + dot(c, pick))
        place = lax.broadcasted_iota(jnp.int32, (height, 128), 1) + 128 * r
        first = lax.broadcasted_iota(jnp.int32, (height, 128), 0) * width
        kept = jnp.where((place >= first) & (place < first + width), spread, 0.0)
        out.append(jnp.sum(kept, axis=0, keepdims=True))
    return out


def silu_parts(z):
    s = 0.5 * jnp.tanh(0.5 * z) + 0.5
    value = z * s
    return value, s + value * (1.0 - s)


def prepare(th_ref, w1_s, w2_s, w3_s, up_s, upt_s, mix_s, mixt_s, hd_s, hdt_s, emb_s, read_s, out_s, w3t_ref, w2t_ref, tmp_s):
    emb = unflatten([th_ref[ROW_EMBED + r : ROW_EMBED + r + 1, :] for r in range(10)], C, SPECIES)
    emb_s[...] = stack_left(emb)
    for l in range(LAYERS):
        o = ROW_LAYER + l * LAYER_ROWS
        w1 = unflatten([th_ref[o + OFF_W1 + r : o + OFF_W1 + r + 1, :] for r in range(4)], HID, NB) * NB ** (-0.5)
        w1_s[l] = stack_left(w1)
        for off, rows, reach, dst, dst_t in ((OFF_W2, 32, HID, w2_s, w2t_ref), (OFF_W3, 64, HID, w3_s, w3t_ref)):
            packed = th_ref[o + off : o + off + rows, :] * reach ** (-0.5)
            tmp_s[pl.ds(0, rows, stride=2), :] = packed
            tmp_s[pl.ds(1, rows, stride=2), :] = pltpu.roll(packed, HID, 1)
            wide = tmp_s[: 2 * rows, :]
            w = wide[:, :HID]
            dst[l] = stack_left(w)
            if rows == 32:
                wide = jnp.concatenate([wide, wide], axis=0)
            wt = jnp.transpose(wide)[:HID, : 2 * rows]
            dst_t[l] = jnp.concatenate(halves(wt), axis=1)
        mats, mats_t = [], []
        for off in (OFF_LIN, OFF_SQ, OFF_SKIP):
            w = th_ref[o + off : o + off + C, :] * C ** (-0.5)
            mats.append(w)
            mats_t.append(jnp.transpose(w))
        mix_s[l] = stack_left(jnp.concatenate(mats, axis=1))
        mixt_s[l] = stack_left(jnp.concatenate(mats_t, axis=0))
        w = th_ref[o + OFF_UP : o + OFF_UP + C, :] * C ** (-0.5)
        up_s[l] = stack_left(w)
        upt_s[l] = stack_left(jnp.transpose(w))
        read_s[l] = jnp.transpose(
            jnp.broadcast_to(th_ref[o + OFF_READ : o + OFF_READ + 1, :] * C ** (-0.5), (128, 128))
        )
    w = th_ref[ROW_HEAD : ROW_HEAD + RO, :] * C ** (-0.5)
    hd_s[...] = stack_left(w)
    wide = jnp.concatenate([w, jnp.zeros((128 - RO, 128), F32)], axis=0)
    hdt_s[...] = stack_left(jnp.transpose(wide)[:, :RO])
    out_s[...] = jnp.transpose(jnp.broadcast_to(th_ref[ROW_OUT : ROW_OUT + 1, :] * RO ** (-0.5), (128, 128)))[:RO, :]


def pair_products(co, x):
    m = co.shape[0]
    a, b = co[:, :ATOMS], co[:, ATOMS:]
    left = jnp.concatenate([jnp.concatenate([a, jnp.zeros_like(a)], axis=1), jnp.concatenate([b, a], axis=1)], axis=0)
    o = nt(left, x)
    return o[:m], o[m:]


def pair_sums(x):
    n = x.shape[0]
    row = lax.broadcasted_iota(jnp.int32, (16, 2 * ATOMS), 0)
    col = lax.broadcasted_iota(jnp.int32, (16, 2 * ATOMS), 1)
    o = dot_nt(jnp.where((row < 8) == (col < ATOMS), 1.0, 0.0).astype(BF16), tall(x))
    return o[:, :n] + o[:, n:]


def wide(x):
    return jnp.concatenate([x, jnp.zeros((x.shape[0], 128 - x.shape[1]), x.dtype)], axis=1)


def run_frame(x, weights, spare, deriv_ref, grad_ref, scratch):
    w1_s, w2_s, w3_s, up_s, upt_s, mix_s, mixt_s, hd_s, hdt_s, emb_s, read_s, out_s = weights
    w3t_s, w2t_s = spare
    oh_s, rad_s, act_s, slope_s, first_s, gath_s, dist_s = scratch
    window = x[ROW_META : ROW_META + 1, :1]
    lam = window / (WINDOWS - 1)
    slot = lax.broadcasted_iota(jnp.int32, (K, ATOMS), 0)
    nb = jnp.where(slot < SLOTS, x[:K].astype(jnp.int32), -1)
    partner = jnp.maximum(nb, 0)
    present = nb >= 0
    species = x[ROW_SPECIES : ROW_SPECIES + 1, :]
    r2 = jnp.full((K, ATOMS), SOFTENING, F32)
    for d in range(3):
        row = jnp.broadcast_to(x[ROW_POS + d : ROW_POS + d + 1, :], (K, ATOMS))
        delta = jnp.take_along_axis(row, partner, axis=1) - row
        r2 = r2 + delta * delta
    radius = jnp.sqrt(r2)
    ratio = radius * (1.0 / RADIUS_CUT)
    env = 1.0 - ratio * ratio
    env = jnp.where(present, env * env, 0.0) * (1.0 / K)
    atom = lax.broadcasted_iota(jnp.int32, (K, ATOMS), 1)
    crossing = (atom < SOLUTE) != (partner < SOLUTE)
    fac = jnp.where(crossing, lam * env, env)
    dfac = jnp.where(crossing, env, 0.0)
    angle = ratio * math.pi
    s1 = jnp.sin(angle) * (math.sqrt(2.0 / RADIUS_CUT) / radius)
    twice = 2.0 * jnp.cos(angle)
    prev, cur = jnp.zeros_like(s1), s1
    for m in range(NB):
        dist_s[m * K : (m + 1) * K, :] = cur
        prev, cur = cur, twice * cur - prev
    basis = jnp.concatenate([dist_s[pl.ds(k, NB, stride=K), :] for k in range(SLOTS)], axis=1)
    bhi = basis.astype(BF16).astype(F32)
    blo = basis - bhi
    basis = jnp.concatenate([bhi, blo], axis=0).astype(BF16)
    none = jnp.zeros_like(bhi)
    w1_rhs = jnp.concatenate([bhi, none, blo, none, bhi, none], axis=0).astype(BF16)
    yield
    sub = lax.broadcasted_iota(jnp.int32, (ATOMS, ATOMS), 0)
    for k in range(SLOTS):
        hit = jnp.broadcast_to(partner[k : k + 1, :], (ATOMS, ATOMS)) == sub
        oh_s[:, k * ATOMS : (k + 1) * ATOMS] = jnp.where(hit, 1.0, 0.0).astype(BF16)
    yield
    for l in range(LAYERS):
        z1 = dot(w1_s[l], w1_rhs)
        v1, d1 = silu_parts(z1)
        h1, l1 = halves(v1)
        act_s[l, 0] = h1
        slope_s[l, 0] = d1.astype(BF16)
        yield
        z2 = dot(w2_s[l], jnp.concatenate([h1, l1, h1], axis=0))
        v2, d2 = silu_parts(z2)
        h2, l2 = halves(v2)
        act_s[l, 1] = h2
        slope_s[l, 1] = d2.astype(BF16)
        yield
        rad_s[l] = dot(w3_s[l], jnp.concatenate([h2, l2, h2], axis=0))
        yield

    rows16 = lax.broadcasted_iota(jnp.int32, (16, ATOMS), 0)
    spc = jnp.where(rows16 == jnp.broadcast_to(species, (16, ATOMS)).astype(jnp.int32), 1.0, 0.0)
    feat = mm(emb_s[...], spc)
    zero = jnp.zeros((C, ATOMS), F32)
    feat = jnp.concatenate([feat, zero], axis=1)
    yield
    deriv = jnp.zeros((), F32)
    pools, feats = [], [feat]
    for l in range(LAYERS):
        if l == 0:
            lift = mm(up_s[l], feat[:, :ATOMS])
            lhs = jnp.concatenate(halves(lift), axis=1)
        else:
            lift = mm(up_s[l], feat)
            lhs = jnp.concatenate(
                [jnp.concatenate(halves(lift[:, :ATOMS]), axis=1), jnp.concatenate(halves(lift[:, ATOMS:]), axis=1)],
                axis=0,
            )
        yield
        oh = oh_s[...]
        g = dot(lhs, jnp.concatenate([oh, oh], axis=0))
        if l == 0:
            first_s[...] = g
        else:
            gath_s[0] = g[:C].astype(BF16)
            gath_s[1] = g[C:].astype(BF16)
        yield
        pool, dpool = zero, zero
        for k in range(SLOTS):
            t = slice(k * ATOMS, (k + 1) * ATOMS)
            rad = rad_s[l, :, t]
            rg = rad * g[:C, t]
            pool = pool + fac[k : k + 1, :] * rg
            dpool = dpool + dfac[k : k + 1, :] * rg
            if l == 1:
                dpool = dpool + fac[k : k + 1, :] * (rad * g[C:, t])
        pools.append((pool, dpool))
        yield
        x = jnp.concatenate(
            [
                jnp.concatenate([pool, dpool], axis=1),
                jnp.concatenate([pool * pool, 2.0 * pool * dpool], axis=1),
                feat,
            ],
            axis=0,
        )
        feat = mm(mix_s[l], x)
        feats.append(feat)
        deriv = deriv + jnp.sum(read_s[l] * feat[:, ATOMS:])
        yield
    q = mm(hd_s[...], feat)
    q0, q1 = q[:, :ATOMS], q[:, ATOMS:]
    sg = 0.5 * jnp.tanh(0.5 * q0) + 0.5
    val = q0 * sg
    first = sg + val * (1.0 - sg)
    second = sg * (1.0 - sg) * (2.0 + q0 * (1.0 - 2.0 * sg))
    tail = first * q1
    deriv = deriv + jnp.sum(out_s[...] * tail)
    lane = lax.broadcasted_iota(jnp.int32, (8, 128), 1)
    deriv_ref[...] = jnp.where(lane == 0, deriv, jnp.broadcast_to(window, (8, 128)))
    at = jnp.broadcast_to(window.astype(jnp.int32), (8, 128))
    tally = jnp.where(lane == at, 1.0, jnp.where(lane == at + WINDOWS, deriv, 0.0))

    def put(row, a, b):
        grad_ref[0, row : row + a.shape[0], :] = a
        grad_ref[1, row : row + b.shape[0], :] = b

    co_q = jnp.concatenate([out_s[...] * first, out_s[...] * second * q1], axis=1)
    co = mm(hdt_s[...], co_q) + jnp.concatenate([read_s[1], zero], axis=1)
    yield
    put(G_HEAD, *pair_products(co_q, feat))
    o = wide(pair_sums(jnp.concatenate([val, tail], axis=1)))
    put(G_OUT, o[:8], o[8:])
    for l in range(LAYERS):
        o = pair_sums(feats[l + 1])
        put(G_READ + 8 * l, o[:8], o[8:])
    yield
    w3_parts, w2_parts, w1_parts = {}, {}, {}
    for l in (1, 0):
        y = mm(mixt_s[l], co)
        pool, dpool = pools[l]
        ya, yb = y[:, :ATOMS], y[:, ATOMS:]
        ap = ya[:C] + 2.0 * pool * ya[C : 2 * C]
        bp = yb[:C] + 2.0 * pool * yb[C : 2 * C] + 2.0 * dpool * ya[C : 2 * C]
        yield
        lefts, rights = [[], []], [[], []]
        for k in range(SLOTS):
            t = slice(k * ATOMS, (k + 1) * ATOMS)
            f, df = fac[k : k + 1, :], dfac[k : k + 1, :]
            u, v = f * ap, f * bp + df * ap
            rad = rad_s[l, :, t]
            lefts[0].append((rad * u).astype(BF16))
            lefts[1].append((rad * v).astype(BF16))
            if l == 0:
                g = first_s[:, t]
                rights[0].append((g * u).astype(BF16))
                rights[1].append((g * v).astype(BF16))
            else:
                g = gath_s[0, :, t].astype(F32)
                rights[0].append((g * u).astype(BF16))
                rights[1].append((g * v + gath_s[1, :, t].astype(F32) * u).astype(BF16))
        left = jnp.concatenate([jnp.concatenate(lst, axis=1) for lst in lefts], axis=0)
        yield
        acc = dot_nt(left, oh_s[...])
        cl = jnp.concatenate([acc[:C], acc[C:]], axis=1)
        yield
        co_in, co = co, y[2 * C :] + mm(upt_s[l], cl)
        if l == 1:
            co = co + jnp.concatenate([read_s[0], zero], axis=1)
        yield
        right = [jnp.concatenate(lst, axis=1) for lst in rights]
        o = dot_nt(jnp.concatenate(right, axis=0), act_s[l, 1])
        w3_parts[l] = o
        c2 = [(dot(w3t_s[l], jnp.concatenate([r, r], axis=0)) * slope_s[l, 1].astype(F32)).astype(BF16) for r in right]
        yield
        w2_parts[l] = dot_nt(jnp.concatenate(c2, axis=0), act_s[l, 0])
        c1 = [(dot(w2t_s[l], jnp.concatenate([r, r], axis=0)) * slope_s[l, 0].astype(F32)).astype(BF16) for r in c2]
        yield
        w1_parts[l] = dot_nt(jnp.concatenate(c1, axis=0), basis)
        yield
        x = jnp.concatenate(
            [
                jnp.concatenate([pool, dpool], axis=1),
                jnp.concatenate([pool * pool, 2.0 * pool * dpool], axis=1),
                feats[l],
            ],
            axis=0,
        )
        a, b = pair_products(co_in, x)
        for i in range(3):
            put(G_MIX + (3 * l + i) * C, a[:, i * C : (i + 1) * C], b[:, i * C : (i + 1) * C])
        yield
        put(G_UP + l * C, *pair_products(cl, feats[l]))
        yield
    o = dot_nt(tall(jnp.concatenate([co[:, :ATOMS], co[:, ATOMS:]], axis=0)), spc.astype(BF16))
    emb = o[: 2 * C] + o[2 * C :]
    w3 = jnp.concatenate([w3_parts[0], w3_parts[1]], axis=1)
    put(G_W3, w3[:C], w3[C:])
    w2 = jnp.concatenate([w2_parts[0], w2_parts[1]], axis=1)
    put(G_W2, w2[:HID], w2[HID:])
    low = [jnp.concatenate([w1_parts[0][h], w1_parts[1][h]], axis=0) for h in (slice(0, HID), slice(HID, 2 * HID))]
    put(
        G_MISC,
        wide(jnp.concatenate([emb[:C], low[0]], axis=1)),
        wide(jnp.concatenate([emb[C:], low[1]], axis=1)),
    )
    return tally


def in_turns(frames):
    results = [None] * len(frames)
    waiting = list(range(len(frames)))
    for i, frame in enumerate(frames):
        for _ in range(2 * (len(frames) - 1 - i)):
            next(frame)
    while waiting:
        for i in list(waiting):
            try:
                next(frames[i])
            except StopIteration as end:
                results[i] = end.value
                waiting.remove(i)
    return results


N_WEIGHTS = 12
G_MIX, G_UP, G_W3, G_W2, G_MISC, G_HEAD, G_READ, G_OUT = 0, 768, 1024, 1152, 1216, 1344, 1360, 1376
G_ROWS = 1384
BATCH = 3


def pack_kernel(count_ref, window_ref, pos_ref, spc_ref, nb_ref, own_ref, send_ref, wide_s):
    n = nb_ref.shape[0]
    lane = lax.broadcasted_iota(jnp.int32, (1, 128), 1)
    for f in range(n):
        own_ref[f, :SLOTS, :] = nb_ref[f, :SLOTS, :].astype(F32)
        for d in range(3):
            own_ref[f, ROW_POS + d : ROW_POS + d + 1, :] = pos_ref[d, f : f + 1, :]
        own_ref[f, ROW_SPECIES : ROW_SPECIES + 1, :] = spc_ref[f : f + 1, :].astype(F32)
        own_ref[f, ROW_META + 1 :, :] = jnp.zeros((FRAME_ROWS - ROW_META - 1, 128), F32)
        own_ref[f, ROW_META : ROW_META + 1, :] = jnp.where(lane == 0, window_ref[f], count_ref[0]).astype(F32)
    for f in range(KEEP, n):
        wide_s[(f - KEEP) * FRAME_ROWS : (f - KEEP + 1) * FRAME_ROWS, :] = own_ref[f]
    wide = wide_s[...]
    for g in range(PLANE_CHIPS):
        send_ref[g] = wide


def deal_kernel(me_ref, here_ref, there_ref, plan_ref):
    n = 8
    lane = lax.broadcasted_iota(jnp.int32, (GROUP, 128), 1)
    gid = lax.broadcasted_iota(jnp.int32, (GROUP, 128), 0)
    core = me_ref[0] // PLANE_CHIPS
    here, there = here_ref[:, ROW_META % 8, :], there_ref[:, ROW_META % 8, :]
    meta = jnp.concatenate([jnp.where(core == 0, here, there), jnp.where(core == 0, there, here)], axis=0)
    counts = jnp.broadcast_to(jnp.sum(jnp.where(lane == 1, meta, 0.0), axis=1, keepdims=True), (GROUP, 128))
    base = jnp.minimum(counts, float(KEEP))
    surplus = counts - base
    total = jnp.sum(surplus, axis=0, keepdims=True)
    lane_f = lane.astype(F32)
    room = jnp.sum(jnp.maximum(lane_f + 1.0 - base, 0.0), axis=0, keepdims=True)
    full = jnp.where((room <= total) & (lane[:1] < n), 1.0, 0.0)
    level = jnp.broadcast_to(jnp.sum(full, axis=1, keepdims=True), (GROUP, 128))
    taken = jnp.maximum(level - base, 0.0)
    left = total - jnp.sum(taken, axis=0, keepdims=True)
    tri_r = lax.broadcasted_iota(jnp.int32, (GROUP, GROUP), 0)
    tri_c = lax.broadcasted_iota(jnp.int32, (GROUP, GROUP), 1)
    before = jnp.where(tri_c < tri_r, 1.0, 0.0).astype(BF16)
    open_ = jnp.where(base <= level, 1.0, 0.0)
    rank = dot(before, open_.astype(BF16))
    taken = taken + jnp.where(rank < left, open_, 0.0)
    offset = dot(before, surplus.astype(BF16))
    me = me_ref[0]
    start = jnp.sum(jnp.where(gid < me, taken, 0.0), axis=0, keepdims=True)
    mine = jnp.sum(jnp.where(gid == me, base + taken, 0.0), axis=0, keepdims=True)
    held = jnp.sum(jnp.where(gid == me, base, 0.0), axis=0, keepdims=True)
    order = jnp.where(lane_f < surplus, offset + lane_f, -1.0)
    place = ((gid % PLANE_CHIPS) * (n - KEEP) + lane).astype(F32)
    away = jnp.where(gid // PLANE_CHIPS == core, 0.0, 1.0)
    for j in range(n):
        hit = order == start + float(j)
        one = jnp.sum(jnp.sum(jnp.where(hit, place, 0.0), axis=0, keepdims=True), axis=1, keepdims=True)
        two = jnp.sum(jnp.sum(jnp.where(hit, away, 0.0), axis=0, keepdims=True), axis=1, keepdims=True)
        plan_ref[j : j + 1, :] = jnp.where(lane[:1] == 0, one, two).astype(jnp.int32)
    plan_ref[n : n + 1, :] = mine.astype(jnp.int32)
    plan_ref[n + 1 : n + 2, :] = held.astype(jnp.int32)
    plan_ref[n + 2 :, :] = jnp.zeros((PLAN_ROWS - n - 2, 128), jnp.int32)


def first_kernel(th_ref, own_ref, *refs):
    weights, spare = refs[:N_WEIGHTS], refs[N_WEIGHTS : N_WEIGHTS + 2]
    deriv_ref, grad_ref, tally_ref, tmp_s, *scratch = refs[N_WEIGHTS + 2 :]
    prepare(th_ref, *weights, *spare, tmp_s)
    frame = run_frame(own_ref[0], weights, spare, deriv_ref.at[0], grad_ref.at[0], [ref.at[0] for ref in scratch])
    tally_ref[...] = in_turns([frame])[0]


def rest_kernel(plan_ref, own_ref, *refs):
    here, there = refs[:BATCH], refs[BATCH : 2 * BATCH]
    first_ref, *refs = refs[2 * BATCH :]
    weights, spare = refs[:N_WEIGHTS], refs[N_WEIGHTS : N_WEIGHTS + 2]
    deriv_ref, grad_ref, tally_ref, sum_s, *scratch = refs[N_WEIGHTS + 2 :]
    step = pl.program_id(0)
    count, own = plan_ref[PLAN_COUNT, 0], plan_ref[PLAN_OWN, 0]

    @pl.when(step == 0)
    def _():
        sum_s[...] = first_ref[...]

    @pl.when(step * BATCH + 1 < count)
    def _():
        frames = []
        for j in range(BATCH):
            at = step * BATCH + 1 + j
            away = plan_ref[jnp.clip(at - own, 0, 7), 1]
            taken = jnp.where(away == 0, here[j][0], there[j][0])
            kept = own_ref[jnp.where(at < own, at, 0)]
            x = jnp.where((at >= own) & (at < count), taken, kept)
            frames.append(
                run_frame(x, weights, spare, deriv_ref.at[j], grad_ref.at[j], [ref.at[j] for ref in scratch])
            )
        total = sum_s[...]
        for j, row in enumerate(in_turns(frames)):
            total = total + jnp.where(step * BATCH + 1 + j < count, row, 0.0)
        sum_s[...] = total

    @pl.when(step == pl.num_programs(0) - 1)
    def _():
        tally_ref[...] = jnp.broadcast_to(sum_s[:1, :], (CHIPS, 128))


def combine_kernel(
    plan_ref, core_ref, parts_ref, more_ref, deriv0_ref, grad0_ref, deriv_ref, grad_ref,
    mine_ref, other_ref, means_ref,
    all_s, acc_s, window_s, tmp_s,
):
    step = pl.program_id(0)

    def scaled(deriv, grads):
        mine = lax.broadcasted_iota(jnp.int32, (1, 128), 1) == deriv[:1, 1:2].astype(jnp.int32)
        centre = jnp.sum(jnp.where(mine, window_s[0, :1], 0.0), axis=1, keepdims=True)
        share = jnp.sum(jnp.where(mine, window_s[1, :1], 0.0), axis=1, keepdims=True)
        return share * grads[1] - share * (deriv[:1, :1] - centre) * grads[0]

    @pl.when(step == 0)
    def _():
        total = jnp.broadcast_to(jnp.sum(parts_ref[...] + more_ref[...], axis=0, keepdims=True), (8, 128))
        lane = lax.broadcasted_iota(jnp.int32, (8, 128), 1)
        sizes = jnp.maximum(total, 1.0)
        means = pltpu.roll(total, 128 - WINDOWS, 1) / sizes
        ends = (lane == 0) | (lane == WINDOWS - 1)
        weight = jnp.where(ends, 0.5, 1.0) / (WINDOWS - 1)
        means_ref[...] = means
        window_s[0] = means
        window_s[1] = weight / sizes
        acc_s[...] = scaled(deriv0_ref[0], grad0_ref[0])

    @pl.when((step > 0) & (step < plan_ref[PLAN_COUNT, 0]))
    def _():
        acc_s[...] += scaled(deriv_ref[0], grad_ref[0])

    @pl.when(step == pl.num_programs(0) - 1)
    def _():
        all_s[USED_ROWS // 8 * 8 :, :] = jnp.zeros((ROWS - USED_ROWS // 8 * 8, 128), F32)
        misc = acc_s[G_MISC : G_MISC + C, :]
        for r, row in enumerate(flatten(misc[:, :16], C, SPECIES, 10)):
            all_s[ROW_EMBED + r : ROW_EMBED + r + 1, :] = row
        for l in range(LAYERS):
            o = ROW_LAYER + l * LAYER_ROWS
            w1 = misc[l * HID : (l + 1) * HID, 16:32] * NB ** (-0.5)
            w1 = w1[:, :NB] + w1[:, NB:]
            w1 = jnp.concatenate([w1, jnp.zeros((HID, 8), F32)], axis=1)
            for r, row in enumerate(flatten(w1, HID, NB, 4)):
                all_s[o + OFF_W1 + r : o + OFF_W1 + r + 1, :] = row
            for off, rows, at in ((OFF_W2, 32, G_W2), (OFF_W3, 64, G_W3)):
                tmp_s[: 2 * rows, :] = acc_s[at : at + 2 * rows, :] * HID ** (-0.5)
                even = tmp_s[pl.ds(0, rows, stride=2), :]
                odd = tmp_s[pl.ds(1, rows, stride=2), :]
                left = lax.broadcasted_iota(jnp.int32, (rows, 128), 1) < HID
                if l == 0:
                    both = jnp.where(left, even, pltpu.roll(odd, HID, 1))
                else:
                    both = jnp.where(left, pltpu.roll(even, HID, 1), odd)
                all_s[o + off : o + off + rows, :] = both
            for i, off in enumerate((OFF_LIN, OFF_SQ, OFF_SKIP)):
                at = G_MIX + (3 * l + i) * C
                all_s[o + off : o + off + C, :] = acc_s[at : at + C, :] * C ** (-0.5)
            all_s[o + OFF_UP : o + OFF_UP + C, :] = acc_s[G_UP + l * C : G_UP + (l + 1) * C, :] * C ** (-0.5)
            all_s[o + OFF_READ : o + OFF_READ + 1, :] = acc_s[G_READ + 8 * l : G_READ + 8 * l + 1, :] * C ** (-0.5)
        all_s[ROW_HEAD : ROW_HEAD + RO, :] = acc_s[G_HEAD : G_HEAD + RO, :] * C ** (-0.5)
        all_s[ROW_OUT : ROW_OUT + 1, :] = acc_s[G_OUT : G_OUT + 1, :] * RO ** (-0.5)
        half = ROWS // 2
        core = core_ref[0]
        mine_ref[...] = all_s[pl.ds(pl.multiple_of(core * half, half), half), :]
        other_ref[...] = all_s[pl.ds(pl.multiple_of((1 - core) * half, half), half), :]


def whole_spec(shape):
    return pl.BlockSpec(shape, lambda i, *_: (0,) * len(shape))


SMEM_SPEC = pl.BlockSpec(memory_space=pltpu.SMEM)
WEIGHTS = (
    ((LAYERS, HID, 48), BF16),
    ((LAYERS, HID, 3 * HID), BF16),
    ((LAYERS, C, 3 * HID), BF16),
    ((LAYERS, C, 3 * C), BF16),
    ((LAYERS, C, 3 * C), BF16),
    ((LAYERS, C, 9 * C), BF16),
    ((LAYERS, 3 * C, 3 * C), BF16),
    ((RO, 3 * C), BF16),
    ((C, 3 * RO), BF16),
    ((C, 48), BF16),
    ((LAYERS, C, 128), F32),
    ((RO, 128), F32),
)
SPARE = (((LAYERS, HID, 2 * C), BF16), ((LAYERS, HID, 2 * HID), BF16))


def frame_scratch(n):
    return [
        pltpu.VMEM((n, ATOMS, EDGES), BF16),
        pltpu.VMEM((n, LAYERS, C, EDGES), F32),
        pltpu.VMEM((n, LAYERS, 2, HID, EDGES), BF16),
        pltpu.VMEM((n, LAYERS, 2, HID, EDGES), BF16),
        pltpu.VMEM((n, C, EDGES), F32),
        pltpu.VMEM((n, 2, C, EDGES), BF16),
        pltpu.VMEM((n, NB * K, ATOMS), F32),
    ]


LIMIT = pltpu.CompilerParams(vmem_limit_bytes=56 * 2**20)


TALLY = jax.ShapeDtypeStruct((8, 128), F32)


def run_pack(count, window_of, positions, species, neighbours):
    n = positions.shape[0]
    return pl.pallas_call(
        pack_kernel,
        in_specs=[SMEM_SPEC, SMEM_SPEC] + [pl.BlockSpec(memory_space=pltpu.VMEM)] * 3,
        out_specs=[pl.BlockSpec(memory_space=pltpu.VMEM)] * 2,
        scratch_shapes=[pltpu.VMEM(((n - KEEP) * FRAME_ROWS, 128), F32)],
        out_shape=[
            jax.ShapeDtypeStruct((n, FRAME_ROWS, 128), F32),
            jax.ShapeDtypeStruct((PLANE_CHIPS, (n - KEEP) * FRAME_ROWS, 128), F32),
        ],
        name="pack",
    )(count, window_of, jnp.transpose(positions, (1, 0, 2)), species, neighbours)


def run_deal(me, here, there):
    return pl.pallas_call(
        deal_kernel,
        grid=(1,),
        in_specs=[SMEM_SPEC] + [pl.BlockSpec((PLANE_CHIPS, 8, 128), lambda i: (0, ROW_META // 8, 0))] * 2,
        out_specs=whole_spec((PLAN_ROWS, 128)),
        out_shape=jax.ShapeDtypeStruct((PLAN_ROWS, 128), jnp.int32),
        name="deal",
    )(me, here, there)


def run_first(theta, own):
    held = WEIGHTS + SPARE
    shapes = [(s, t) for s, t in held] + [((1, 8, 128), F32), ((1, 2, G_ROWS, 128), F32), (TALLY.shape, F32)]
    out = pl.pallas_call(
        first_kernel,
        grid=(1,),
        in_specs=[whole_spec((ROWS, 128)), whole_spec((1, FRAME_ROWS, 128))],
        out_specs=[whole_spec(s) for s, _ in shapes],
        scratch_shapes=[pltpu.VMEM((128, 128), F32)] + frame_scratch(1),
        out_shape=[jax.ShapeDtypeStruct(s, t) for s, t in shapes],
        compiler_params=LIMIT,
        cost_estimate=pl.CostEstimate(flops=10**9, bytes_accessed=4 * 10**7, transcendentals=10**6),
        name="first_frame",
    )(theta, own)
    return out[: N_WEIGHTS + 2], out[N_WEIGHTS + 2], out[N_WEIGHTS + 3], out[N_WEIGHTS + 4]


def run_rest(plan, own, here, there, tally, held):
    n = own.shape[0]
    steps = -(-(n - 1) // BATCH)

    def taken_spec(j):
        def index(i, plan):
            return (plan[jnp.clip(i * BATCH + 1 + j - plan[PLAN_OWN, 0], 0, 7), 0], 0, 0)

        return pl.BlockSpec((1, FRAME_ROWS, 128), index)

    def result_spec(shape):
        def index(i, plan):
            return (jnp.minimum(i, jnp.maximum((plan[PLAN_COUNT, 0] + BATCH - 2) // BATCH - 1, 0)),) + (0,) * len(shape)

        return pl.BlockSpec((BATCH,) + shape, index)

    results = ((8, 128), (2, G_ROWS, 128))
    return pl.pallas_call(
        rest_kernel,
        grid_spec=pltpu.PrefetchScalarGridSpec(
            num_scalar_prefetch=1,
            grid=(steps,),
            in_specs=[whole_spec(own.shape)]
            + [taken_spec(j) for j in range(BATCH)] * 2
            + [whole_spec(TALLY.shape)]
            + [whole_spec(s) for s, _ in WEIGHTS + SPARE],
            out_specs=[result_spec(s) for s in results] + [whole_spec((CHIPS, 128))],
            scratch_shapes=[pltpu.VMEM(TALLY.shape, F32)] + frame_scratch(BATCH),
        ),
        out_shape=[jax.ShapeDtypeStruct((steps * BATCH,) + s, F32) for s in results]
        + [jax.ShapeDtypeStruct((CHIPS, 128), F32)],
        compiler_params=LIMIT,
        name="other_frames",
    )(plan, own, *[here] * BATCH, *[there] * BATCH, tally, *held)


def run_combine(plan, core, parts, more, deriv0, grad0, deriv, grad, n):
    def rest_spec(shape):
        def index(i, plan):
            return (jnp.clip(i - 1, 0, jnp.maximum(plan[PLAN_COUNT, 0] - 2, 0)),) + (0,) * len(shape)

        return pl.BlockSpec((1,) + shape, index)

    half = (ROWS // 2, 128)
    return pl.pallas_call(
        combine_kernel,
        grid_spec=pltpu.PrefetchScalarGridSpec(
            num_scalar_prefetch=1,
            grid=(n,),
            in_specs=[SMEM_SPEC]
            + [whole_spec(v.shape) for v in (parts, more, deriv0, grad0)]
            + [rest_spec(v.shape[1:]) for v in (deriv, grad)],
            out_specs=[whole_spec(half), whole_spec(half), whole_spec(TALLY.shape)],
            scratch_shapes=[
                pltpu.VMEM((ROWS, 128), F32),
                pltpu.VMEM((G_ROWS, 128), F32),
                pltpu.VMEM((2, 8, 128), F32),
                pltpu.VMEM((128, 128), F32),
            ],
        ),
        out_shape=[jax.ShapeDtypeStruct(half, F32), jax.ShapeDtypeStruct(half, F32), TALLY],
        compiler_params=LIMIT,
        name="combine",
    )(plan, core, parts, more, deriv0, grad0, deriv, grad)


def adam_step(params, first_moment, second_moment, unit):
    new_first = 0.9 * first_moment + 0.1 * unit
    new_second = 0.999 * second_moment + 0.001 * unit * unit
    unbiased_first = new_first / (1.0 - 0.9**10)
    unbiased_second = new_second / (1.0 - 0.999**10)
    new_params = params - 0.01 * unbiased_first / (jnp.sqrt(unbiased_second) + 1e-08)
    return (new_params, new_first, new_second)


def swap_cores(v):
    return lax.ppermute(v, "core", [(0, 1), (1, 0)])


def gather_tallies(v):
    own = lax.all_to_all(v, PLANE + ("z",), 0, 0, tiled=True)
    return own, swap_cores(own)


def to_all(v, axes, size):
    return lax.all_to_all(jnp.broadcast_to(v[None], (size,) + v.shape), axes, 0, 0, tiled=True)


def sum_large(mine, other, core):
    half = mine.shape[0]
    piece = half // PLANE_CHIPS
    own = mine + swap_cores(other)
    own = jnp.sum(lax.all_to_all(own.reshape(PLANE_CHIPS, piece, 128), PLANE, 0, 0, tiled=True), axis=0)
    own = jnp.sum(to_all(own, "z", DEPTH), axis=0)
    own = to_all(own, PLANE, PLANE_CHIPS).reshape(half, 128)
    other = swap_cores(own)
    first = core == 0
    return jnp.concatenate([jnp.where(first, own, other), jnp.where(first, other, own)], axis=0)


def on_device(
    params, first_moment, second_moment, positions, species, neighbours, window_of, frame_count
):
    n = positions.shape[0]
    core = lax.axis_index("core")
    own, send = run_pack(frame_count, window_of, positions, species, neighbours)
    here = lax.all_to_all(send, PLANE, 0, 0, tiled=True)
    theta = jnp.pad(params, (0, ROWS * 128 - NPAR)).reshape(ROWS, 128)
    held, deriv0, grad0, tally = run_first(theta, own)
    here, tally = lax.optimization_barrier((here, tally))
    there = swap_cores(here)
    plan = run_deal((core * PLANE_CHIPS + lax.axis_index(PLANE))[None], here, there)
    here, there = (v.reshape(PLANE_CHIPS * (n - KEEP), FRAME_ROWS, 128) for v in (here, there))
    deriv, grad, tally = run_rest(plan, own, here, there, tally, held)
    mine, other, means = run_combine(plan, core[None], *gather_tallies(tally), deriv0, grad0, deriv, grad, n)
    summed = sum_large(mine, other, core).reshape(-1)[:NPAR]
    norm = jnp.sqrt(jnp.sum(summed * summed))
    unit = summed * (GRAD_SCALE * math.sqrt(NPAR) / (norm + 1e-06))
    new_params, new_first, new_second = adam_step(params, first_moment, second_moment, unit)
    return (new_params, new_first, new_second, means[0, :WINDOWS])


def solution(mesh):
    axes = tuple(AXES)
    split = Mesh(mesh.devices.reshape(tuple(AXES.values())), axes)
    in_specs = (
        P(),
        P(),
        P(),
        P(axes, None, None),
        P(axes, None),
        P(axes, None, None),
        P(axes),
        P(axes),
    )
    out_specs = (P(), P(), P(), P())
    return jax.shard_map(
        on_device, mesh=split, in_specs=in_specs, out_specs=out_specs, check_vma=False
    )
```

```python
import math

import jax
import jax.numpy as jnp
from jax import lax
from jax.experimental import pallas as pl
from jax.experimental.pallas import tpu as pltpu
from jax.sharding import Mesh
from jax.sharding import PartitionSpec as P

C = 128
HID = 64
NB = 8
SPECIES = 10
RO = 16
LAYERS = 2
WINDOWS = 32
ATOMS = 128
SOLUTE = 16
K = 16
SLOTS = K - 1
EDGES = SLOTS * ATOMS
NPAR = 160272
ROWS = 1280

RADIUS_CUT = 8.0
SOFTENING = 0.01
GRAD_SCALE = 4.0

ROW_EMBED = 0
ROW_LAYER = 10
LAYER_ROWS = 613
OFF_W1, OFF_W2, OFF_W3, OFF_UP, OFF_LIN, OFF_SQ, OFF_SKIP, OFF_READ = 0, 4, 36, 100, 228, 356, 484, 612
ROW_HEAD = ROW_LAYER + LAYERS * LAYER_ROWS
ROW_OUT = ROW_HEAD + RO
USED_ROWS = ROW_OUT + 1

ROW_POS, ROW_SPECIES, ROW_META, FRAME_ROWS = SLOTS, SLOTS + 3, SLOTS + 4, 24
KEEP = 4
GROUP = 32
PLAN_ROWS = 16
PLAN_COUNT, PLAN_OWN = 8, 9

AXES = {"x": 4, "y": 4, "z": 8, "core": 2}
PLANE = ("x", "y")
PLANE_CHIPS = 16
CHIPS = 128
DEPTH = 8

F32, BF16 = jnp.float32, jnp.bfloat16


def halves(x):
    hi = x.astype(BF16)
    return hi, (x - hi.astype(F32)).astype(BF16)


def stack_left(w):
    hi, lo = halves(w)
    return jnp.concatenate([hi, hi, lo], axis=1)


def dot(a, b):
    return jnp.dot(a, b, preferred_element_type=F32)


def dot_nt(a, b):
    return lax.dot_general(a, b, (((1,), (1,)), ((), ())), preferred_element_type=F32)


def mm(left, x):
    hi, lo = halves(x)
    return dot(left, jnp.concatenate([hi, lo, hi], axis=0))


def nt_stacked(xs, ys):
    m, n = xs.shape[0] // 2, ys.shape[0] // 2
    o = dot_nt(xs, ys)
    return o[:m, :n] + (o[:m, n:] + o[m:, :n])


def tall(x):
    return jnp.concatenate(halves(x), axis=0)


def nt(x, y):
    return nt_stacked(tall(x), tall(y))


def tile_rows(x, reps):
    return jnp.concatenate([x] * reps, axis=1)


def unflatten(rows, height, width):
    total = None
    for r, row in enumerate(rows):
        place = lax.broadcasted_iota(jnp.int32, (height, 128), 1) + 128 * r
        own = lax.broadcasted_iota(jnp.int32, (height, 128), 0)
        first = own * width
        kept = jnp.where((place >= first) & (place < first + width), jnp.broadcast_to(row, (height, 128)), 0.0)
        col = lax.broadcasted_iota(jnp.int32, (128, 16), 1)
        pos = (lax.broadcasted_iota(jnp.int32, (128, 16), 0) + 128 * r) % width
        pick = (col == pos).astype(BF16)
        a = kept.astype(BF16)
        rest = kept - a.astype(F32)
        b = rest.astype(BF16)
        c = (rest - b.astype(F32)).astype(BF16)
        piece = dot(a, pick) + (dot(b, pick) + dot(c, pick))
        total = piece if total is None else total + piece
    return total


def flatten(mat, height, width, n_rows):
    a = mat.astype(BF16)
    rest = mat - a.astype(F32)
    b = rest.astype(BF16)
    c = (rest - b.astype(F32)).astype(BF16)
    out = []
    for r in range(n_rows):
        col = lax.broadcasted_iota(jnp.int32, (16, 128), 0)
        pos = (lax.broadcasted_iota(jnp.int32, (16, 128), 1) + 128 * r) % width
        pick = (col == pos).astype(BF16)
        spread = dot(a, pick) + (dot(b, pick) + dot(c, pick))
        place = lax.broadcasted_iota(jnp.int32, (height, 128), 1) + 128 * r
        first = lax.broadcasted_iota(jnp.int32, (height, 128), 0) * width
        kept = jnp.where((place >= first) & (place < first + width), spread, 0.0)
        out.append(jnp.sum(kept, axis=0, keepdims=True))
    return out


def silu_parts(z):
    s = 0.5 * jnp.tanh(0.5 * z) + 0.5
    value = z * s
    return value, s + value * (1.0 - s)


def prepare(th_ref, w1_s, w2_s, w3_s, up_s, upt_s, mix_s, mixt_s, hd_s, hdt_s, emb_s, read_s, out_s, w3t_ref, w2t_ref, tmp_s):
    emb = unflatten([th_ref[ROW_EMBED + r : ROW_EMBED + r + 1, :] for r in range(10)], C, SPECIES)
    emb_s[...] = stack_left(emb)
    for l in range(LAYERS):
        o = ROW_LAYER + l * LAYER_ROWS
        w1 = unflatten([th_ref[o + OFF_W1 + r : o + OFF_W1 + r + 1, :] for r in range(4)], HID, NB) * NB ** (-0.5)
        w1_s[l] = stack_left(w1)
        for off, rows, reach, dst, dst_t in ((OFF_W2, 32, HID, w2_s, w2t_ref), (OFF_W3, 64, HID, w3_s, w3t_ref)):
            packed = th_ref[o + off : o + off + rows, :] * reach ** (-0.5)
            tmp_s[pl.ds(0, rows, stride=2), :] = packed
            tmp_s[pl.ds(1, rows, stride=2), :] = pltpu.roll(packed, HID, 1)
            wide = tmp_s[: 2 * rows, :]
            w = wide[:, :HID]
            dst[l] = stack_left(w)
            if rows == 32:
                wide = jnp.concatenate([wide, wide], axis=0)
            wt = jnp.transpose(wide)[:HID, : 2 * rows]
            dst_t[l] = jnp.concatenate(halves(wt), axis=1)
        mats, mats_t = [], []
        for off in (OFF_LIN, OFF_SQ, OFF_SKIP):
            w = th_ref[o + off : o + off + C, :] * C ** (-0.5)
            mats.append(w)
            mats_t.append(jnp.transpose(w))
        mix_s[l] = stack_left(jnp.concatenate(mats, axis=1))
        mixt_s[l] = stack_left(jnp.concatenate(mats_t, axis=0))
        w = th_ref[o + OFF_UP : o + OFF_UP + C, :] * C ** (-0.5)
        up_s[l] = stack_left(w)
        upt_s[l] = stack_left(jnp.transpose(w))
        read_s[l] = jnp.transpose(
            jnp.broadcast_to(th_ref[o + OFF_READ : o + OFF_READ + 1, :] * C ** (-0.5), (128, 128))
        )
    w = th_ref[ROW_HEAD : ROW_HEAD + RO, :] * C ** (-0.5)
    hd_s[...] = stack_left(w)
    wide = jnp.concatenate([w, jnp.zeros((128 - RO, 128), F32)], axis=0)
    hdt_s[...] = stack_left(jnp.transpose(wide)[:, :RO])
    out_s[...] = jnp.transpose(jnp.broadcast_to(th_ref[ROW_OUT : ROW_OUT + 1, :] * RO ** (-0.5), (128, 128)))[:RO, :]


def pair_products(co, x):
    m = co.shape[0]
    a, b = co[:, :ATOMS], co[:, ATOMS:]
    left = jnp.concatenate([jnp.concatenate([a, jnp.zeros_like(a)], axis=1), jnp.concatenate([b, a], axis=1)], axis=0)
    o = nt(left, x)
    return o[:m], o[m:]


def pair_sums(x):
    n = x.shape[0]
    row = lax.broadcasted_iota(jnp.int32, (16, 2 * ATOMS), 0)
    col = lax.broadcasted_iota(jnp.int32, (16, 2 * ATOMS), 1)
    o = dot_nt(jnp.where((row < 8) == (col < ATOMS), 1.0, 0.0).astype(BF16), tall(x))
    return o[:, :n] + o[:, n:]


def wide(x):
    return jnp.concatenate([x, jnp.zeros((x.shape[0], 128 - x.shape[1]), x.dtype)], axis=1)


def run_frame(x, weights, spare, deriv_ref, grad_ref, scratch):
    w1_s, w2_s, w3_s, up_s, upt_s, mix_s, mixt_s, hd_s, hdt_s, emb_s, read_s, out_s = weights
    w3t_s, w2t_s = spare
    oh_s, rad_s, act_s, slope_s, first_s, gath_s, dist_s = scratch
    window = x[ROW_META : ROW_META + 1, :1]
    lam = window / (WINDOWS - 1)
    slot = lax.broadcasted_iota(jnp.int32, (K, ATOMS), 0)
    nb = jnp.where(slot < SLOTS, x[:K].astype(jnp.int32), -1)
    partner = jnp.maximum(nb, 0)
    present = nb >= 0
    species = x[ROW_SPECIES : ROW_SPECIES + 1, :]
    r2 = jnp.full((K, ATOMS), SOFTENING, F32)
    for d in range(3):
        row = jnp.broadcast_to(x[ROW_POS + d : ROW_POS + d + 1, :], (K, ATOMS))
        delta = jnp.take_along_axis(row, partner, axis=1) - row
        r2 = r2 + delta * delta
    radius = jnp.sqrt(r2)
    ratio = radius * (1.0 / RADIUS_CUT)
    env = 1.0 - ratio * ratio
    env = jnp.where(present, env * env, 0.0) * (1.0 / K)
    atom = lax.broadcasted_iota(jnp.int32, (K, ATOMS), 1)
    crossing = (atom < SOLUTE) != (partner < SOLUTE)
    fac = jnp.where(crossing, lam * env, env)
    dfac = jnp.where(crossing, env, 0.0)
    angle = ratio * math.pi
    s1 = jnp.sin(angle) * (math.sqrt(2.0 / RADIUS_CUT) / radius)
    twice = 2.0 * jnp.cos(angle)
    prev, cur = jnp.zeros_like(s1), s1
    for m in range(NB):
        dist_s[m * K : (m + 1) * K, :] = cur
        prev, cur = cur, twice * cur - prev
    basis = jnp.concatenate([dist_s[pl.ds(k, NB, stride=K), :] for k in range(SLOTS)], axis=1)
    bhi = basis.astype(BF16).astype(F32)
    blo = basis - bhi
    basis = jnp.concatenate([bhi, blo], axis=0).astype(BF16)
    none = jnp.zeros_like(bhi)
    w1_rhs = jnp.concatenate([bhi, none, blo, none, bhi, none], axis=0).astype(BF16)
    yield
    sub = lax.broadcasted_iota(jnp.int32, (ATOMS, ATOMS), 0)
    for k in range(SLOTS):
        hit = jnp.broadcast_to(partner[k : k + 1, :], (ATOMS, ATOMS)) == sub
        oh_s[:, k * ATOMS : (k + 1) * ATOMS] = jnp.where(hit, 1.0, 0.0).astype(BF16)
    yield
    for l in range(LAYERS):
        z1 = dot(w1_s[l], w1_rhs)
        v1, d1 = silu_parts(z1)
        h1, l1 = halves(v1)
        act_s[l, 0] = h1
        slope_s[l, 0] = d1.astype(BF16)
        yield
        z2 = dot(w2_s[l], jnp.concatenate([h1, l1, h1], axis=0))
        v2, d2 = silu_parts(z2)
        h2, l2 = halves(v2)
        act_s[l, 1] = h2
        slope_s[l, 1] = d2.astype(BF16)
        yield
        rad_s[l] = dot(w3_s[l], jnp.concatenate([h2, l2, h2], axis=0))
        yield

    rows16 = lax.broadcasted_iota(jnp.int32, (16, ATOMS), 0)
    spc = jnp.where(rows16 == jnp.broadcast_to(species, (16, ATOMS)).astype(jnp.int32), 1.0, 0.0)
    feat = mm(emb_s[...], spc)
    zero = jnp.zeros((C, ATOMS), F32)
    feat = jnp.concatenate([feat, zero], axis=1)
    yield
    deriv = jnp.zeros((), F32)
    pools, feats = [], [feat]
    for l in range(LAYERS):
        if l == 0:
            lift = mm(up_s[l], feat[:, :ATOMS])
            lhs = jnp.concatenate(halves(lift), axis=1)
        else:
            lift = mm(up_s[l], feat)
            lhs = jnp.concatenate(
                [jnp.concatenate(halves(lift[:, :ATOMS]), axis=1), jnp.concatenate(halves(lift[:, ATOMS:]), axis=1)],
                axis=0,
            )
        yield
        oh = oh_s[...]
        g = dot(lhs, jnp.concatenate([oh, oh], axis=0))
        if l == 0:
            first_s[...] = g
        else:
            gath_s[0] = g[:C].astype(BF16)
            gath_s[1] = g[C:].astype(BF16)
        yield
        pool, dpool = zero, zero
        for k in range(SLOTS):
            t = slice(k * ATOMS, (k + 1) * ATOMS)
            rad = rad_s[l, :, t]
            rg = rad * g[:C, t]
            pool = pool + fac[k : k + 1, :] * rg
            dpool = dpool + dfac[k : k + 1, :] * rg
            if l == 1:
                dpool = dpool + fac[k : k + 1, :] * (rad * g[C:, t])
        pools.append((pool, dpool))
        yield
        x = jnp.concatenate(
            [
                jnp.concatenate([pool, dpool], axis=1),
                jnp.concatenate([pool * pool, 2.0 * pool * dpool], axis=1),
                feat,
            ],
            axis=0,
        )
        feat = mm(mix_s[l], x)
        feats.append(feat)
        deriv = deriv + jnp.sum(read_s[l] * feat[:, ATOMS:])
        yield
    q = mm(hd_s[...], feat)
    q0, q1 = q[:, :ATOMS], q[:, ATOMS:]
    sg = 0.5 * jnp.tanh(0.5 * q0) + 0.5
    val = q0 * sg
    first = sg + val * (1.0 - sg)
    second = sg * (1.0 - sg) * (2.0 + q0 * (1.0 - 2.0 * sg))
    tail = first * q1
    deriv = deriv + jnp.sum(out_s[...] * tail)
    lane = lax.broadcasted_iota(jnp.int32, (8, 128), 1)
    deriv_ref[...] = jnp.where(lane == 0, deriv, jnp.broadcast_to(window, (8, 128)))
    at = jnp.broadcast_to(window.astype(jnp.int32), (8, 128))
    tally = jnp.where(lane == at, 1.0, jnp.where(lane == at + WINDOWS, deriv, 0.0))

    def put(row, a, b):
        grad_ref[0, row : row + a.shape[0], :] = a
        grad_ref[1, row : row + b.shape[0], :] = b

    co_q = jnp.concatenate([out_s[...] * first, out_s[...] * second * q1], axis=1)
    co = mm(hdt_s[...], co_q) + jnp.concatenate([read_s[1], zero], axis=1)
    yield
    put(G_HEAD, *pair_products(co_q, feat))
    o = wide(pair_sums(jnp.concatenate([val, tail], axis=1)))
    put(G_OUT, o[:8], o[8:])
    for l in range(LAYERS):
        o = pair_sums(feats[l + 1])
        put(G_READ + 8 * l, o[:8], o[8:])
    yield
    w3_parts, w2_parts, w1_parts = {}, {}, {}
    for l in (1, 0):
        y = mm(mixt_s[l], co)
        pool, dpool = pools[l]
        ya, yb = y[:, :ATOMS], y[:, ATOMS:]
        ap = ya[:C] + 2.0 * pool * ya[C : 2 * C]
        bp = yb[:C] + 2.0 * pool * yb[C : 2 * C] + 2.0 * dpool * ya[C : 2 * C]
        yield
        lefts, rights = [[], []], [[], []]
        for k in range(SLOTS):
            t = slice(k * ATOMS, (k + 1) * ATOMS)
            f, df = fac[k : k + 1, :], dfac[k : k + 1, :]
            u, v = f * ap, f * bp + df * ap
            rad = rad_s[l, :, t]
            lefts[0].append((rad * u).astype(BF16))
            lefts[1].append((rad * v).astype(BF16))
            if l == 0:
                g = first_s[:, t]
                rights[0].append((g * u).astype(BF16))
                rights[1].append((g * v).astype(BF16))
            else:
                g = gath_s[0, :, t].astype(F32)
                rights[0].append((g * u).astype(BF16))
                rights[1].append((g * v + gath_s[1, :, t].astype(F32) * u).astype(BF16))
        left = jnp.concatenate([jnp.concatenate(lst, axis=1) for lst in lefts], axis=0)
        yield
        acc = dot_nt(left, oh_s[...])
        cl = jnp.concatenate([acc[:C], acc[C:]], axis=1)
        yield
        co_in, co = co, y[2 * C :] + mm(upt_s[l], cl)
        if l == 1:
            co = co + jnp.concatenate([read_s[0], zero], axis=1)
        yield
        right = [jnp.concatenate(lst, axis=1) for lst in rights]
        o = dot_nt(jnp.concatenate(right, axis=0), act_s[l, 1])
        w3_parts[l] = o
        c2 = [(dot(w3t_s[l], jnp.concatenate([r, r], axis=0)) * slope_s[l, 1].astype(F32)).astype(BF16) for r in right]
        yield
        w2_parts[l] = dot_nt(jnp.concatenate(c2, axis=0), act_s[l, 0])
        c1 = [(dot(w2t_s[l], jnp.concatenate([r, r], axis=0)) * slope_s[l, 0].astype(F32)).astype(BF16) for r in c2]
        yield
        w1_parts[l] = dot_nt(jnp.concatenate(c1, axis=0), basis)
        yield
        x = jnp.concatenate(
            [
                jnp.concatenate([pool, dpool], axis=1),
                jnp.concatenate([pool * pool, 2.0 * pool * dpool], axis=1),
                feats[l],
            ],
            axis=0,
        )
        a, b = pair_products(co_in, x)
        for i in range(3):
            put(G_MIX + (3 * l + i) * C, a[:, i * C : (i + 1) * C], b[:, i * C : (i + 1) * C])
        yield
        put(G_UP + l * C, *pair_products(cl, feats[l]))
        yield
    o = dot_nt(tall(jnp.concatenate([co[:, :ATOMS], co[:, ATOMS:]], axis=0)), spc.astype(BF16))
    emb = o[: 2 * C] + o[2 * C :]
    w3 = jnp.concatenate([w3_parts[0], w3_parts[1]], axis=1)
    put(G_W3, w3[:C], w3[C:])
    w2 = jnp.concatenate([w2_parts[0], w2_parts[1]], axis=1)
    put(G_W2, w2[:HID], w2[HID:])
    low = [jnp.concatenate([w1_parts[0][h], w1_parts[1][h]], axis=0) for h in (slice(0, HID), slice(HID, 2 * HID))]
    put(
        G_MISC,
        wide(jnp.concatenate([emb[:C], low[0]], axis=1)),
        wide(jnp.concatenate([emb[C:], low[1]], axis=1)),
    )
    return tally


def in_turns(frames):
    results = [None] * len(frames)
    waiting = list(range(len(frames)))
    for i, frame in enumerate(frames):
        for _ in range(2 * (len(frames) - 1 - i)):
            next(frame)
    while waiting:
        for i in list(waiting):
            try:
                next(frames[i])
            except StopIteration as end:
                results[i] = end.value
                waiting.remove(i)
    return results


N_WEIGHTS = 12
G_MIX, G_UP, G_W3, G_W2, G_MISC, G_HEAD, G_READ, G_OUT = 0, 768, 1024, 1152, 1216, 1344, 1360, 1376
G_ROWS = 1384
BATCH = 3


def pack_kernel(count_ref, window_ref, pos_ref, spc_ref, nb_ref, own_ref, send_ref, wide_s):
    n = nb_ref.shape[0]
    lane = lax.broadcasted_iota(jnp.int32, (1, 128), 1)
    for f in range(n):
        own_ref[f, :SLOTS, :] = nb_ref[f, :SLOTS, :].astype(F32)
        for d in range(3):
            own_ref[f, ROW_POS + d : ROW_POS + d + 1, :] = pos_ref[d, f : f + 1, :]
        own_ref[f, ROW_SPECIES : ROW_SPECIES + 1, :] = spc_ref[f : f + 1, :].astype(F32)
        own_ref[f, ROW_META + 1 :, :] = jnp.zeros((FRAME_ROWS - ROW_META - 1, 128), F32)
        own_ref[f, ROW_META : ROW_META + 1, :] = jnp.where(lane == 0, window_ref[f], count_ref[0]).astype(F32)
    for f in range(KEEP, n):
        wide_s[(f - KEEP) * FRAME_ROWS : (f - KEEP + 1) * FRAME_ROWS, :] = own_ref[f]
    wide = wide_s[...]
    for g in range(PLANE_CHIPS):
        send_ref[g] = wide


def deal_kernel(me_ref, here_ref, there_ref, plan_ref):
    n = 8
    lane = lax.broadcasted_iota(jnp.int32, (GROUP, 128), 1)
    gid = lax.broadcasted_iota(jnp.int32, (GROUP, 128), 0)
    core = me_ref[0] // PLANE_CHIPS
    here, there = here_ref[:, ROW_META % 8, :], there_ref[:, ROW_META % 8, :]
    meta = jnp.concatenate([jnp.where(core == 0, here, there), jnp.where(core == 0, there, here)], axis=0)
    counts = jnp.broadcast_to(jnp.sum(jnp.where(lane == 1, meta, 0.0), axis=1, keepdims=True), (GROUP, 128))
    base = jnp.minimum(counts, float(KEEP))
    surplus = counts - base
    total = jnp.sum(surplus, axis=0, keepdims=True)
    lane_f = lane.astype(F32)
    room = jnp.sum(jnp.maximum(lane_f + 1.0 - base, 0.0), axis=0, keepdims=True)
    full = jnp.where((room <= total) & (lane[:1] < n), 1.0, 0.0)
    level = jnp.broadcast_to(jnp.sum(full, axis=1, keepdims=True), (GROUP, 128))
    taken = jnp.maximum(level - base, 0.0)
    left = total - jnp.sum(taken, axis=0, keepdims=True)
    tri_r = lax.broadcasted_iota(jnp.int32, (GROUP, GROUP), 0)
    tri_c = lax.broadcasted_iota(jnp.int32, (GROUP, GROUP), 1)
    before = jnp.where(tri_c < tri_r, 1.0, 0.0).astype(BF16)
    open_ = jnp.where(base <= level, 1.0, 0.0)
    rank = dot(before, open_.astype(BF16))
    taken = taken + jnp.where(rank < left, open_, 0.0)
    offset = dot(before, surplus.astype(BF16))
    me = me_ref[0]
    start = jnp.sum(jnp.where(gid < me, taken, 0.0), axis=0, keepdims=True)
    mine = jnp.sum(jnp.where(gid == me, base + taken, 0.0), axis=0, keepdims=True)
    held = jnp.sum(jnp.where(gid == me, base, 0.0), axis=0, keepdims=True)
    order = jnp.where(lane_f < surplus, offset + lane_f, -1.0)
    place = ((gid % PLANE_CHIPS) * (n - KEEP) + lane).astype(F32)
    away = jnp.where(gid // PLANE_CHIPS == core, 0.0, 1.0)
    for j in range(n):
        hit = order == start + float(j)
        one = jnp.sum(jnp.sum(jnp.where(hit, place, 0.0), axis=0, keepdims=True), axis=1, keepdims=True)
        two = jnp.sum(jnp.sum(jnp.where(hit, away, 0.0), axis=0, keepdims=True), axis=1, keepdims=True)
        plan_ref[j : j + 1, :] = jnp.where(lane[:1] == 0, one, two).astype(jnp.int32)
    plan_ref[n : n + 1, :] = mine.astype(jnp.int32)
    plan_ref[n + 1 : n + 2, :] = held.astype(jnp.int32)
    plan_ref[n + 2 :, :] = jnp.zeros((PLAN_ROWS - n - 2, 128), jnp.int32)


def first_kernel(th_ref, own_ref, *refs):
    weights, spare = refs[:N_WEIGHTS], refs[N_WEIGHTS : N_WEIGHTS + 2]
    deriv_ref, grad_ref, tally_ref, tmp_s, *scratch = refs[N_WEIGHTS + 2 :]
    prepare(th_ref, *weights, *spare, tmp_s)
    frame = run_frame(own_ref[0], weights, spare, deriv_ref.at[0], grad_ref.at[0], [ref.at[0] for ref in scratch])
    tally_ref[...] = in_turns([frame])[0]


def rest_kernel(plan_ref, own_ref, *refs):
    here, there = refs[:BATCH], refs[BATCH : 2 * BATCH]
    first_ref, *refs = refs[2 * BATCH :]
    weights, spare = refs[:N_WEIGHTS], refs[N_WEIGHTS : N_WEIGHTS + 2]
    deriv_ref, grad_ref, tally_ref, sum_s, *scratch = refs[N_WEIGHTS + 2 :]
    step = pl.program_id(0)
    count, own = plan_ref[PLAN_COUNT, 0], plan_ref[PLAN_OWN, 0]

    @pl.when(step == 0)
    def _():
        sum_s[...] = first_ref[...]

    @pl.when(step * BATCH + 1 < count)
    def _():
        frames = []
        for j in range(BATCH):
            at = step * BATCH + 1 + j
            away = plan_ref[jnp.clip(at - own, 0, 7), 1]
            taken = jnp.where(away == 0, here[j][0], there[j][0])
            kept = own_ref[jnp.where(at < own, at, 0)]
            x = jnp.where((at >= own) & (at < count), taken, kept)
            frames.append(
                run_frame(x, weights, spare, deriv_ref.at[j], grad_ref.at[j], [ref.at[j] for ref in scratch])
            )
        total = sum_s[...]
        for j, row in enumerate(in_turns(frames)):
            total = total + jnp.where(step * BATCH + 1 + j < count, row, 0.0)
        sum_s[...] = total

    @pl.when(step == pl.num_programs(0) - 1)
    def _():
        tally_ref[...] = jnp.broadcast_to(sum_s[:1, :], (CHIPS, 128))


def combine_kernel(
    plan_ref, core_ref, parts_ref, more_ref, deriv0_ref, grad0_ref, deriv_ref, grad_ref,
    mine_ref, other_ref, means_ref,
    all_s, acc_s, window_s, tmp_s,
):
    step = pl.program_id(0)

    def scaled(deriv, grads):
        mine = lax.broadcasted_iota(jnp.int32, (1, 128), 1) == deriv[:1, 1:2].astype(jnp.int32)
        centre = jnp.sum(jnp.where(mine, window_s[0, :1], 0.0), axis=1, keepdims=True)
        share = jnp.sum(jnp.where(mine, window_s[1, :1], 0.0), axis=1, keepdims=True)
        return share * grads[1] - share * (deriv[:1, :1] - centre) * grads[0]

    @pl.when(step == 0)
    def _():
        total = jnp.broadcast_to(jnp.sum(parts_ref[...] + more_ref[...], axis=0, keepdims=True), (8, 128))
        lane = lax.broadcasted_iota(jnp.int32, (8, 128), 1)
        sizes = jnp.maximum(total, 1.0)
        means = pltpu.roll(total, 128 - WINDOWS, 1) / sizes
        ends = (lane == 0) | (lane == WINDOWS - 1)
        weight = jnp.where(ends, 0.5, 1.0) / (WINDOWS - 1)
        means_ref[...] = means
        window_s[0] = means
        window_s[1] = weight / sizes
        acc_s[...] = scaled(deriv0_ref[0], grad0_ref[0])

    @pl.when((step > 0) & (step < plan_ref[PLAN_COUNT, 0]))
    def _():
        acc_s[...] += scaled(deriv_ref[0], grad_ref[0])

    @pl.when(step == pl.num_programs(0) - 1)
    def _():
        all_s[USED_ROWS // 8 * 8 :, :] = jnp.zeros((ROWS - USED_ROWS // 8 * 8, 128), F32)
        misc = acc_s[G_MISC : G_MISC + C, :]
        for r, row in enumerate(flatten(misc[:, :16], C, SPECIES, 10)):
            all_s[ROW_EMBED + r : ROW_EMBED + r + 1, :] = row
        for l in range(LAYERS):
            o = ROW_LAYER + l * LAYER_ROWS
            w1 = misc[l * HID : (l + 1) * HID, 16:32] * NB ** (-0.5)
            w1 = w1[:, :NB] + w1[:, NB:]
            w1 = jnp.concatenate([w1, jnp.zeros((HID, 8), F32)], axis=1)
            for r, row in enumerate(flatten(w1, HID, NB, 4)):
                all_s[o + OFF_W1 + r : o + OFF_W1 + r + 1, :] = row
            for off, rows, at in ((OFF_W2, 32, G_W2), (OFF_W3, 64, G_W3)):
                tmp_s[: 2 * rows, :] = acc_s[at : at + 2 * rows, :] * HID ** (-0.5)
                even = tmp_s[pl.ds(0, rows, stride=2), :]
                odd = tmp_s[pl.ds(1, rows, stride=2), :]
                left = lax.broadcasted_iota(jnp.int32, (rows, 128), 1) < HID
                if l == 0:
                    both = jnp.where(left, even, pltpu.roll(odd, HID, 1))
                else:
                    both = jnp.where(left, pltpu.roll(even, HID, 1), odd)
                all_s[o + off : o + off + rows, :] = both
            for i, off in enumerate((OFF_LIN, OFF_SQ, OFF_SKIP)):
                at = G_MIX + (3 * l + i) * C
                all_s[o + off : o + off + C, :] = acc_s[at : at + C, :] * C ** (-0.5)
            all_s[o + OFF_UP : o + OFF_UP + C, :] = acc_s[G_UP + l * C : G_UP + (l + 1) * C, :] * C ** (-0.5)
            all_s[o + OFF_READ : o + OFF_READ + 1, :] = acc_s[G_READ + 8 * l : G_READ + 8 * l + 1, :] * C ** (-0.5)
        all_s[ROW_HEAD : ROW_HEAD + RO, :] = acc_s[G_HEAD : G_HEAD + RO, :] * C ** (-0.5)
        all_s[ROW_OUT : ROW_OUT + 1, :] = acc_s[G_OUT : G_OUT + 1, :] * RO ** (-0.5)
        half = ROWS // 2
        core = core_ref[0]
        mine_ref[...] = all_s[pl.ds(pl.multiple_of(core * half, half), half), :]
        other_ref[...] = all_s[pl.ds(pl.multiple_of((1 - core) * half, half), half), :]


def whole_spec(shape):
    return pl.BlockSpec(shape, lambda i, *_: (0,) * len(shape))


SMEM_SPEC = pl.BlockSpec(memory_space=pltpu.SMEM)
WEIGHTS = (
    ((LAYERS, HID, 48), BF16),
    ((LAYERS, HID, 3 * HID), BF16),
    ((LAYERS, C, 3 * HID), BF16),
    ((LAYERS, C, 3 * C), BF16),
    ((LAYERS, C, 3 * C), BF16),
    ((LAYERS, C, 9 * C), BF16),
    ((LAYERS, 3 * C, 3 * C), BF16),
    ((RO, 3 * C), BF16),
    ((C, 3 * RO), BF16),
    ((C, 48), BF16),
    ((LAYERS, C, 128), F32),
    ((RO, 128), F32),
)
SPARE = (((LAYERS, HID, 2 * C), BF16), ((LAYERS, HID, 2 * HID), BF16))


def frame_scratch(n):
    return [
        pltpu.VMEM((n, ATOMS, EDGES), BF16),
        pltpu.VMEM((n, LAYERS, C, EDGES), F32),
        pltpu.VMEM((n, LAYERS, 2, HID, EDGES), BF16),
        pltpu.VMEM((n, LAYERS, 2, HID, EDGES), BF16),
        pltpu.VMEM((n, C, EDGES), F32),
        pltpu.VMEM((n, 2, C, EDGES), BF16),
        pltpu.VMEM((n, NB * K, ATOMS), F32),
    ]


LIMIT = pltpu.CompilerParams(vmem_limit_bytes=56 * 2**20)
SMALL_LIMIT = pltpu.CompilerParams(vmem_limit_bytes=4 * 2**20)


TALLY = jax.ShapeDtypeStruct((8, 128), F32)


def run_pack(count, window_of, positions, species, neighbours):
    n = positions.shape[0]
    return pl.pallas_call(
        pack_kernel,
        in_specs=[SMEM_SPEC, SMEM_SPEC] + [pl.BlockSpec(memory_space=pltpu.VMEM)] * 3,
        out_specs=[pl.BlockSpec(memory_space=pltpu.VMEM)] * 2,
        scratch_shapes=[pltpu.VMEM(((n - KEEP) * FRAME_ROWS, 128), F32)],
        out_shape=[
            jax.ShapeDtypeStruct((n, FRAME_ROWS, 128), F32),
            jax.ShapeDtypeStruct((PLANE_CHIPS, (n - KEEP) * FRAME_ROWS, 128), F32),
        ],
        name="pack",
    )(count, window_of, jnp.transpose(positions, (1, 0, 2)), species, neighbours)


def run_deal(me, here, there):
    return pl.pallas_call(
        deal_kernel,
        grid=(1,),
        in_specs=[SMEM_SPEC] + [pl.BlockSpec((PLANE_CHIPS, 8, 128), lambda i: (0, ROW_META // 8, 0))] * 2,
        out_specs=whole_spec((PLAN_ROWS, 128)),
        out_shape=jax.ShapeDtypeStruct((PLAN_ROWS, 128), jnp.int32),
        compiler_params=SMALL_LIMIT,
        name="deal",
    )(me, here, there)


def run_first(theta, own):
    held = WEIGHTS + SPARE
    shapes = [(s, t) for s, t in held] + [((1, 8, 128), F32), ((1, 2, G_ROWS, 128), F32), (TALLY.shape, F32)]
    out = pl.pallas_call(
        first_kernel,
        grid=(1,),
        in_specs=[whole_spec((ROWS, 128)), whole_spec((1, FRAME_ROWS, 128))],
        out_specs=[whole_spec(s) for s, _ in shapes],
        scratch_shapes=[pltpu.VMEM((128, 128), F32)] + frame_scratch(1),
        out_shape=[jax.ShapeDtypeStruct(s, t) for s, t in shapes],
        compiler_params=LIMIT,
        cost_estimate=pl.CostEstimate(flops=10**9, bytes_accessed=4 * 10**7, transcendentals=10**6),
        name="first_frame",
    )(theta, own)
    return out[: N_WEIGHTS + 2], out[N_WEIGHTS + 2], out[N_WEIGHTS + 3], out[N_WEIGHTS + 4]


def run_rest(plan, own, here, there, tally, held):
    n = own.shape[0]
    steps = -(-(n - 1) // BATCH)

    def taken_spec(j):
        def index(i, plan):
            return (plan[jnp.clip(i * BATCH + 1 + j - plan[PLAN_OWN, 0], 0, 7), 0], 0, 0)

        return pl.BlockSpec((1, FRAME_ROWS, 128), index)

    def result_spec(shape):
        def index(i, plan):
            return (jnp.minimum(i, jnp.maximum((plan[PLAN_COUNT, 0] + BATCH - 2) // BATCH - 1, 0)),) + (0,) * len(shape)

        return pl.BlockSpec((BATCH,) + shape, index)

    results = ((8, 128), (2, G_ROWS, 128))
    return pl.pallas_call(
        rest_kernel,
        grid_spec=pltpu.PrefetchScalarGridSpec(
            num_scalar_prefetch=1,
            grid=(steps,),
            in_specs=[whole_spec(own.shape)]
            + [taken_spec(j) for j in range(BATCH)] * 2
            + [whole_spec(TALLY.shape)]
            + [whole_spec(s) for s, _ in WEIGHTS + SPARE],
            out_specs=[result_spec(s) for s in results] + [whole_spec((CHIPS, 128))],
            scratch_shapes=[pltpu.VMEM(TALLY.shape, F32)] + frame_scratch(BATCH),
        ),
        out_shape=[jax.ShapeDtypeStruct((steps * BATCH,) + s, F32) for s in results]
        + [jax.ShapeDtypeStruct((CHIPS, 128), F32)],
        compiler_params=LIMIT,
        name="other_frames",
    )(plan, own, *[here] * BATCH, *[there] * BATCH, tally, *held)


def run_combine(plan, core, parts, more, deriv0, grad0, deriv, grad, n):
    def rest_spec(shape):
        def index(i, plan):
            return (jnp.clip(i - 1, 0, jnp.maximum(plan[PLAN_COUNT, 0] - 2, 0)),) + (0,) * len(shape)

        return pl.BlockSpec((1,) + shape, index)

    half = (ROWS // 2, 128)
    return pl.pallas_call(
        combine_kernel,
        grid_spec=pltpu.PrefetchScalarGridSpec(
            num_scalar_prefetch=1,
            grid=(n,),
            in_specs=[SMEM_SPEC]
            + [whole_spec(v.shape) for v in (parts, more, deriv0, grad0)]
            + [rest_spec(v.shape[1:]) for v in (deriv, grad)],
            out_specs=[whole_spec(half), whole_spec(half), whole_spec(TALLY.shape)],
            scratch_shapes=[
                pltpu.VMEM((ROWS, 128), F32),
                pltpu.VMEM((G_ROWS, 128), F32),
                pltpu.VMEM((2, 8, 128), F32),
                pltpu.VMEM((128, 128), F32),
            ],
        ),
        out_shape=[jax.ShapeDtypeStruct(half, F32), jax.ShapeDtypeStruct(half, F32), TALLY],
        compiler_params=LIMIT,
        name="combine",
    )(plan, core, parts, more, deriv0, grad0, deriv, grad)


def adam_step(params, first_moment, second_moment, unit):
    new_first = 0.9 * first_moment + 0.1 * unit
    new_second = 0.999 * second_moment + 0.001 * unit * unit
    unbiased_first = new_first / (1.0 - 0.9**10)
    unbiased_second = new_second / (1.0 - 0.999**10)
    new_params = params - 0.01 * unbiased_first / (jnp.sqrt(unbiased_second) + 1e-08)
    return (new_params, new_first, new_second)


def swap_cores(v):
    return lax.ppermute(v, "core", [(0, 1), (1, 0)])


def gather_tallies(v):
    own = lax.all_to_all(v, PLANE + ("z",), 0, 0, tiled=True)
    return own, swap_cores(own)


def to_all(v, axes, size):
    return lax.all_to_all(jnp.broadcast_to(v[None], (size,) + v.shape), axes, 0, 0, tiled=True)


def sum_large(mine, other, core):
    half = mine.shape[0]
    piece = half // PLANE_CHIPS
    own = mine + swap_cores(other)
    own = jnp.sum(lax.all_to_all(own.reshape(PLANE_CHIPS, piece, 128), PLANE, 0, 0, tiled=True), axis=0)
    own = jnp.sum(to_all(own, "z", DEPTH), axis=0)
    own = to_all(own, PLANE, PLANE_CHIPS).reshape(half, 128)
    other = swap_cores(own)
    first = core == 0
    return jnp.concatenate([jnp.where(first, own, other), jnp.where(first, other, own)], axis=0)


def on_device(
    params, first_moment, second_moment, positions, species, neighbours, window_of, frame_count
):
    n = positions.shape[0]
    core = lax.axis_index("core")
    own, send = run_pack(frame_count, window_of, positions, species, neighbours)
    here = lax.all_to_all(send, PLANE, 0, 0, tiled=True)
    theta = jnp.pad(params, (0, ROWS * 128 - NPAR)).reshape(ROWS, 128)
    held, deriv0, grad0, tally = run_first(theta, own)
    here, tally = lax.optimization_barrier((here, tally))
    there = swap_cores(here)
    plan = run_deal((core * PLANE_CHIPS + lax.axis_index(PLANE))[None], here, there)
    here, there = (v.reshape(PLANE_CHIPS * (n - KEEP), FRAME_ROWS, 128) for v in (here, there))
    deriv, grad, tally = run_rest(plan, own, here, there, tally, held)
    mine, other, means = run_combine(plan, core[None], *gather_tallies(tally), deriv0, grad0, deriv, grad, n)
    summed = sum_large(mine, other, core).reshape(-1)[:NPAR]
    norm = jnp.sqrt(jnp.sum(summed * summed))
    unit = summed * (GRAD_SCALE * math.sqrt(NPAR) / (norm + 1e-06))
    new_params, new_first, new_second = adam_step(params, first_moment, second_moment, unit)
    return (new_params, new_first, new_second, means[0, :WINDOWS])


def solution(mesh):
    axes = tuple(AXES)
    split = Mesh(mesh.devices.reshape(tuple(AXES.values())), axes)
    in_specs = (
        P(),
        P(),
        P(),
        P(axes, None, None),
        P(axes, None),
        P(axes, None, None),
        P(axes),
        P(axes),
    )
    out_specs = (P(), P(), P(), P())
    return jax.shard_map(
        on_device, mesh=split, in_specs=in_specs, out_specs=out_specs, check_vma=False
    )
```

```python
import math

import jax
import jax.numpy as jnp
from jax import lax
from jax.experimental import pallas as pl
from jax.experimental.pallas import tpu as pltpu
from jax.sharding import Mesh
from jax.sharding import PartitionSpec as P

C = 128
HID = 64
NB = 8
SPECIES = 10
RO = 16
LAYERS = 2
WINDOWS = 32
ATOMS = 128
SOLUTE = 16
K = 16
SLOTS = K - 1
EDGES = SLOTS * ATOMS
NPAR = 160272
ROWS = 1280

RADIUS_CUT = 8.0
SOFTENING = 0.01
GRAD_SCALE = 4.0

ROW_EMBED = 0
ROW_LAYER = 10
LAYER_ROWS = 613
OFF_W1, OFF_W2, OFF_W3, OFF_UP, OFF_LIN, OFF_SQ, OFF_SKIP, OFF_READ = 0, 4, 36, 100, 228, 356, 484, 612
ROW_HEAD = ROW_LAYER + LAYERS * LAYER_ROWS
ROW_OUT = ROW_HEAD + RO
USED_ROWS = ROW_OUT + 1

ROW_POS, ROW_SPECIES, ROW_META, FRAME_ROWS = SLOTS, SLOTS + 3, SLOTS + 4, 24
KEEP = 4
GROUP = 32
PLAN_ROWS = 16
PLAN_COUNT, PLAN_OWN = 8, 9

AXES = {"x": 4, "y": 4, "z": 8, "core": 2}
PLANE = ("x", "y")
PLANE_CHIPS = 16
CHIPS = 128
DEPTH = 8

F32, BF16 = jnp.float32, jnp.bfloat16


def halves(x):
    hi = x.astype(BF16)
    return hi, (x - hi.astype(F32)).astype(BF16)


def stack_left(w):
    hi, lo = halves(w)
    return jnp.concatenate([hi, hi, lo], axis=1)


def dot(a, b):
    return jnp.dot(a, b, preferred_element_type=F32)


def dot_nt(a, b):
    return lax.dot_general(a, b, (((1,), (1,)), ((), ())), preferred_element_type=F32)


def mm(left, x):
    hi, lo = halves(x)
    return dot(left, jnp.concatenate([hi, lo, hi], axis=0))


def nt_stacked(xs, ys):
    m, n = xs.shape[0] // 2, ys.shape[0] // 2
    o = dot_nt(xs, ys)
    return o[:m, :n] + (o[:m, n:] + o[m:, :n])


def tall(x):
    return jnp.concatenate(halves(x), axis=0)


def nt(x, y):
    return nt_stacked(tall(x), tall(y))


def tile_rows(x, reps):
    return jnp.concatenate([x] * reps, axis=1)


def unflatten(rows, height, width):
    total = None
    for r, row in enumerate(rows):
        place = lax.broadcasted_iota(jnp.int32, (height, 128), 1) + 128 * r
        own = lax.broadcasted_iota(jnp.int32, (height, 128), 0)
        first = own * width
        kept = jnp.where((place >= first) & (place < first + width), jnp.broadcast_to(row, (height, 128)), 0.0)
        col = lax.broadcasted_iota(jnp.int32, (128, 16), 1)
        pos = (lax.broadcasted_iota(jnp.int32, (128, 16), 0) + 128 * r) % width
        pick = (col == pos).astype(BF16)
        a = kept.astype(BF16)
        rest = kept - a.astype(F32)
        b = rest.astype(BF16)
        c = (rest - b.astype(F32)).astype(BF16)
        piece = dot(a, pick) + (dot(b, pick) + dot(c, pick))
        total = piece if total is None else total + piece
    return total


def flatten(mat, height, width, n_rows):
    a = mat.astype(BF16)
    rest = mat - a.astype(F32)
    b = rest.astype(BF16)
    c = (rest - b.astype(F32)).astype(BF16)
    out = []
    for r in range(n_rows):
        col = lax.broadcasted_iota(jnp.int32, (16, 128), 0)
        pos = (lax.broadcasted_iota(jnp.int32, (16, 128), 1) + 128 * r) % width
        pick = (col == pos).astype(BF16)
        spread = dot(a, pick) + (dot(b, pick) + dot(c, pick))
        place = lax.broadcasted_iota(jnp.int32, (height, 128), 1) + 128 * r
        first = lax.broadcasted_iota(jnp.int32, (height, 128), 0) * width
        kept = jnp.where((place >= first) & (place < first + width), spread, 0.0)
        out.append(jnp.sum(kept, axis=0, keepdims=True))
    return out


def silu_parts(z):
    s = 0.5 * jnp.tanh(0.5 * z) + 0.5
    value = z * s
    return value, s + value * (1.0 - s)


def prepare(th_ref, w1_s, w2_s, w3_s, up_s, upt_s, mix_s, mixt_s, hd_s, hdt_s, emb_s, read_s, out_s, w3t_ref, w2t_ref, tmp_s):
    emb = unflatten([th_ref[ROW_EMBED + r : ROW_EMBED + r + 1, :] for r in range(10)], C, SPECIES)
    emb_s[...] = stack_left(emb)
    for l in range(LAYERS):
        o = ROW_LAYER + l * LAYER_ROWS
        w1 = unflatten([th_ref[o + OFF_W1 + r : o + OFF_W1 + r + 1, :] for r in range(4)], HID, NB) * NB ** (-0.5)
        w1_s[l] = stack_left(w1)
        for off, rows, reach, dst, dst_t in ((OFF_W2, 32, HID, w2_s, w2t_ref), (OFF_W3, 64, HID, w3_s, w3t_ref)):
            packed = th_ref[o + off : o + off + rows, :] * reach ** (-0.5)
            tmp_s[pl.ds(0, rows, stride=2), :] = packed
            tmp_s[pl.ds(1, rows, stride=2), :] = pltpu.roll(packed, HID, 1)
            wide = tmp_s[: 2 * rows, :]
            w = wide[:, :HID]
            dst[l] = stack_left(w)
            if rows == 32:
                wide = jnp.concatenate([wide, wide], axis=0)
            wt = jnp.transpose(wide)[:HID, : 2 * rows]
            dst_t[l] = jnp.concatenate(halves(wt), axis=1)
        mats, mats_t = [], []
        for off in (OFF_LIN, OFF_SQ, OFF_SKIP):
            w = th_ref[o + off : o + off + C, :] * C ** (-0.5)
            mats.append(w)
            mats_t.append(jnp.transpose(w))
        mix_s[l] = stack_left(jnp.concatenate(mats, axis=1))
        mixt_s[l] = stack_left(jnp.concatenate(mats_t, axis=0))
        w = th_ref[o + OFF_UP : o + OFF_UP + C, :] * C ** (-0.5)
        up_s[l] = stack_left(w)
        upt_s[l] = stack_left(jnp.transpose(w))
        read_s[l] = jnp.transpose(
            jnp.broadcast_to(th_ref[o + OFF_READ : o + OFF_READ + 1, :] * C ** (-0.5), (128, 128))
        )
    w = th_ref[ROW_HEAD : ROW_HEAD + RO, :] * C ** (-0.5)
    hd_s[...] = stack_left(w)
    wide = jnp.concatenate([w, jnp.zeros((128 - RO, 128), F32)], axis=0)
    hdt_s[...] = stack_left(jnp.transpose(wide)[:, :RO])
    out_s[...] = jnp.transpose(jnp.broadcast_to(th_ref[ROW_OUT : ROW_OUT + 1, :] * RO ** (-0.5), (128, 128)))[:RO, :]


def pair_products(co, x):
    m = co.shape[0]
    a, b = co[:, :ATOMS], co[:, ATOMS:]
    left = jnp.concatenate([jnp.concatenate([a, jnp.zeros_like(a)], axis=1), jnp.concatenate([b, a], axis=1)], axis=0)
    o = nt(left, x)
    return o[:m], o[m:]


def pair_sums(x):
    n = x.shape[0]
    row = lax.broadcasted_iota(jnp.int32, (16, 2 * ATOMS), 0)
    col = lax.broadcasted_iota(jnp.int32, (16, 2 * ATOMS), 1)
    o = dot_nt(jnp.where((row < 8) == (col < ATOMS), 1.0, 0.0).astype(BF16), tall(x))
    return o[:, :n] + o[:, n:]


def wide(x):
    return jnp.concatenate([x, jnp.zeros((x.shape[0], 128 - x.shape[1]), x.dtype)], axis=1)


def run_frame(x, weights, spare, deriv_ref, grad_ref, scratch):
    w1_s, w2_s, w3_s, up_s, upt_s, mix_s, mixt_s, hd_s, hdt_s, emb_s, read_s, out_s = weights
    w3t_s, w2t_s = spare
    oh_s, rad_s, act_s, slope_s, first_s, gath_s, dist_s = scratch
    window = x[ROW_META : ROW_META + 1, :1]
    lam = window / (WINDOWS - 1)
    slot = lax.broadcasted_iota(jnp.int32, (K, ATOMS), 0)
    nb = jnp.where(slot < SLOTS, x[:K].astype(jnp.int32), -1)
    partner = jnp.maximum(nb, 0)
    present = nb >= 0
    species = x[ROW_SPECIES : ROW_SPECIES + 1, :]
    r2 = jnp.full((K, ATOMS), SOFTENING, F32)
    for d in range(3):
        row = jnp.broadcast_to(x[ROW_POS + d : ROW_POS + d + 1, :], (K, ATOMS))
        delta = jnp.take_along_axis(row, partner, axis=1) - row
        r2 = r2 + delta * delta
    radius = jnp.sqrt(r2)
    ratio = radius * (1.0 / RADIUS_CUT)
    env = 1.0 - ratio * ratio
    env = jnp.where(present, env * env, 0.0) * (1.0 / K)
    atom = lax.broadcasted_iota(jnp.int32, (K, ATOMS), 1)
    crossing = (atom < SOLUTE) != (partner < SOLUTE)
    fac = jnp.where(crossing, lam * env, env)
    dfac = jnp.where(crossing, env, 0.0)
    angle = ratio * math.pi
    s1 = jnp.sin(angle) * (math.sqrt(2.0 / RADIUS_CUT) / radius)
    twice = 2.0 * jnp.cos(angle)
    prev, cur = jnp.zeros_like(s1), s1
    for m in range(NB):
        dist_s[m * K : (m + 1) * K, :] = cur
        prev, cur = cur, twice * cur - prev
    basis = jnp.concatenate([dist_s[pl.ds(k, NB, stride=K), :] for k in range(SLOTS)], axis=1)
    bhi = basis.astype(BF16).astype(F32)
    blo = basis - bhi
    basis = jnp.concatenate([bhi, blo], axis=0).astype(BF16)
    none = jnp.zeros_like(bhi)
    w1_rhs = jnp.concatenate([bhi, none, blo, none, bhi, none], axis=0).astype(BF16)
    yield
    sub = lax.broadcasted_iota(jnp.int32, (ATOMS, ATOMS), 0)
    for k in range(SLOTS):
        hit = jnp.broadcast_to(partner[k : k + 1, :], (ATOMS, ATOMS)) == sub
        oh_s[:, k * ATOMS : (k + 1) * ATOMS] = jnp.where(hit, 1.0, 0.0).astype(BF16)
    yield
    for l in range(LAYERS):
        z1 = dot(w1_s[l], w1_rhs)
        v1, d1 = silu_parts(z1)
        h1, l1 = halves(v1)
        act_s[l, 0] = h1
        slope_s[l, 0] = d1.astype(BF16)
        yield
        z2 = dot(w2_s[l], jnp.concatenate([h1, l1, h1], axis=0))
        v2, d2 = silu_parts(z2)
        h2, l2 = halves(v2)
        act_s[l, 1] = h2
        slope_s[l, 1] = d2.astype(BF16)
        yield
        rad_s[l] = dot(w3_s[l], jnp.concatenate([h2, l2, h2], axis=0))
        yield

    rows16 = lax.broadcasted_iota(jnp.int32, (16, ATOMS), 0)
    spc = jnp.where(rows16 == jnp.broadcast_to(species, (16, ATOMS)).astype(jnp.int32), 1.0, 0.0)
    feat = mm(emb_s[...], spc)
    zero = jnp.zeros((C, ATOMS), F32)
    feat = jnp.concatenate([feat, zero], axis=1)
    yield
    deriv = jnp.zeros((), F32)
    pools, feats = [], [feat]
    for l in range(LAYERS):
        if l == 0:
            lift = mm(up_s[l], feat[:, :ATOMS])
            lhs = jnp.concatenate(halves(lift), axis=1)
        else:
            lift = mm(up_s[l], feat)
            lhs = jnp.concatenate(
                [jnp.concatenate(halves(lift[:, :ATOMS]), axis=1), jnp.concatenate(halves(lift[:, ATOMS:]), axis=1)],
                axis=0,
            )
        yield
        oh = oh_s[...]
        g = dot(lhs, jnp.concatenate([oh, oh], axis=0))
        if l == 0:
            first_s[...] = g
        else:
            gath_s[0] = g[:C].astype(BF16)
            gath_s[1] = g[C:].astype(BF16)
        yield
        pool, dpool = zero, zero
        for k in range(SLOTS):
            t = slice(k * ATOMS, (k + 1) * ATOMS)
            rad = rad_s[l, :, t]
            rg = rad * g[:C, t]
            pool = pool + fac[k : k + 1, :] * rg
            dpool = dpool + dfac[k : k + 1, :] * rg
            if l == 1:
                dpool = dpool + fac[k : k + 1, :] * (rad * g[C:, t])
        pools.append((pool, dpool))
        yield
        x = jnp.concatenate(
            [
                jnp.concatenate([pool, dpool], axis=1),
                jnp.concatenate([pool * pool, 2.0 * pool * dpool], axis=1),
                feat,
            ],
            axis=0,
        )
        feat = mm(mix_s[l], x)
        feats.append(feat)
        deriv = deriv + jnp.sum(read_s[l] * feat[:, ATOMS:])
        yield
    q = mm(hd_s[...], feat)
    q0, q1 = q[:, :ATOMS], q[:, ATOMS:]
    sg = 0.5 * jnp.tanh(0.5 * q0) + 0.5
    val = q0 * sg
    first = sg + val * (1.0 - sg)
    second = sg * (1.0 - sg) * (2.0 + q0 * (1.0 - 2.0 * sg))
    tail = first * q1
    deriv = deriv + jnp.sum(out_s[...] * tail)
    lane = lax.broadcasted_iota(jnp.int32, (8, 128), 1)
    deriv_ref[...] = jnp.where(lane == 0, deriv, jnp.broadcast_to(window, (8, 128)))
    at = jnp.broadcast_to(window.astype(jnp.int32), (8, 128))
    tally = jnp.where(lane == at, 1.0, jnp.where(lane == at + WINDOWS, deriv, 0.0))

    def put(row, a, b):
        grad_ref[0, row : row + a.shape[0], :] = a
        grad_ref[1, row : row + b.shape[0], :] = b

    co_q = jnp.concatenate([out_s[...] * first, out_s[...] * second * q1], axis=1)
    co = mm(hdt_s[...], co_q) + jnp.concatenate([read_s[1], zero], axis=1)
    yield
    put(G_HEAD, *pair_products(co_q, feat))
    o = wide(pair_sums(jnp.concatenate([val, tail], axis=1)))
    put(G_OUT, o[:8], o[8:])
    for l in range(LAYERS):
        o = pair_sums(feats[l + 1])
        put(G_READ + 8 * l, o[:8], o[8:])
    yield
    w3_parts, w2_parts, w1_parts = {}, {}, {}
    for l in (1, 0):
        y = mm(mixt_s[l], co)
        pool, dpool = pools[l]
        ya, yb = y[:, :ATOMS], y[:, ATOMS:]
        ap = ya[:C] + 2.0 * pool * ya[C : 2 * C]
        bp = yb[:C] + 2.0 * pool * yb[C : 2 * C] + 2.0 * dpool * ya[C : 2 * C]
        yield
        lefts, rights = [[], []], [[], []]
        for k in range(SLOTS):
            t = slice(k * ATOMS, (k + 1) * ATOMS)
            f, df = fac[k : k + 1, :], dfac[k : k + 1, :]
            u, v = f * ap, f * bp + df * ap
            rad = rad_s[l, :, t]
            lefts[0].append((rad * u).astype(BF16))
            lefts[1].append((rad * v).astype(BF16))
            if l == 0:
                g = first_s[:, t]
                rights[0].append((g * u).astype(BF16))
                rights[1].append((g * v).astype(BF16))
            else:
                g = gath_s[0, :, t].astype(F32)
                rights[0].append((g * u).astype(BF16))
                rights[1].append((g * v + gath_s[1, :, t].astype(F32) * u).astype(BF16))
        left = jnp.concatenate([jnp.concatenate(lst, axis=1) for lst in lefts], axis=0)
        yield
        acc = dot_nt(left, oh_s[...])
        cl = jnp.concatenate([acc[:C], acc[C:]], axis=1)
        yield
        co_in, co = co, y[2 * C :] + mm(upt_s[l], cl)
        if l == 1:
            co = co + jnp.concatenate([read_s[0], zero], axis=1)
        yield
        right = [jnp.concatenate(lst, axis=1) for lst in rights]
        o = dot_nt(jnp.concatenate(right, axis=0), act_s[l, 1])
        w3_parts[l] = o
        c2 = [(dot(w3t_s[l], jnp.concatenate([r, r], axis=0)) * slope_s[l, 1].astype(F32)).astype(BF16) for r in right]
        yield
        w2_parts[l] = dot_nt(jnp.concatenate(c2, axis=0), act_s[l, 0])
        c1 = [(dot(w2t_s[l], jnp.concatenate([r, r], axis=0)) * slope_s[l, 0].astype(F32)).astype(BF16) for r in c2]
        yield
        w1_parts[l] = dot_nt(jnp.concatenate(c1, axis=0), basis)
        yield
        x = jnp.concatenate(
            [
                jnp.concatenate([pool, dpool], axis=1),
                jnp.concatenate([pool * pool, 2.0 * pool * dpool], axis=1),
                feats[l],
            ],
            axis=0,
        )
        a, b = pair_products(co_in, x)
        for i in range(3):
            put(G_MIX + (3 * l + i) * C, a[:, i * C : (i + 1) * C], b[:, i * C : (i + 1) * C])
        yield
        put(G_UP + l * C, *pair_products(cl, feats[l]))
        yield
    o = dot_nt(tall(jnp.concatenate([co[:, :ATOMS], co[:, ATOMS:]], axis=0)), spc.astype(BF16))
    emb = o[: 2 * C] + o[2 * C :]
    w3 = jnp.concatenate([w3_parts[0], w3_parts[1]], axis=1)
    put(G_W3, w3[:C], w3[C:])
    w2 = jnp.concatenate([w2_parts[0], w2_parts[1]], axis=1)
    put(G_W2, w2[:HID], w2[HID:])
    low = [jnp.concatenate([w1_parts[0][h], w1_parts[1][h]], axis=0) for h in (slice(0, HID), slice(HID, 2 * HID))]
    put(
        G_MISC,
        wide(jnp.concatenate([emb[:C], low[0]], axis=1)),
        wide(jnp.concatenate([emb[C:], low[1]], axis=1)),
    )
    return tally


def in_turns(frames):
    results = [None] * len(frames)
    waiting = list(range(len(frames)))
    for i, frame in enumerate(frames):
        for _ in range(2 * (len(frames) - 1 - i)):
            next(frame)
    while waiting:
        for i in list(waiting):
            try:
                next(frames[i])
            except StopIteration as end:
                results[i] = end.value
                waiting.remove(i)
    return results


N_WEIGHTS = 12
G_MIX, G_UP, G_W3, G_W2, G_MISC, G_HEAD, G_READ, G_OUT = 0, 768, 1024, 1152, 1216, 1344, 1360, 1376
G_ROWS = 1384
BATCH = 3


def pack_kernel(count_ref, window_ref, pos_ref, spc_ref, nb_ref, own_ref, send_ref, wide_s):
    n = nb_ref.shape[0]
    lane = lax.broadcasted_iota(jnp.int32, (1, 128), 1)
    for f in range(n):
        own_ref[f, :SLOTS, :] = nb_ref[f, :SLOTS, :].astype(F32)
        for d in range(3):
            own_ref[f, ROW_POS + d : ROW_POS + d + 1, :] = pos_ref[d, f : f + 1, :]
        own_ref[f, ROW_SPECIES : ROW_SPECIES + 1, :] = spc_ref[f : f + 1, :].astype(F32)
        own_ref[f, ROW_META + 1 :, :] = jnp.zeros((FRAME_ROWS - ROW_META - 1, 128), F32)
        own_ref[f, ROW_META : ROW_META + 1, :] = jnp.where(lane == 0, window_ref[f], count_ref[0]).astype(F32)
    for f in range(KEEP, n):
        wide_s[(f - KEEP) * FRAME_ROWS : (f - KEEP + 1) * FRAME_ROWS, :] = own_ref[f]
    wide = wide_s[...]
    for g in range(PLANE_CHIPS):
        send_ref[g] = wide


def deal_kernel(me_ref, here_ref, there_ref, plan_ref):
    n = 8
    lane = lax.broadcasted_iota(jnp.int32, (GROUP, 128), 1)
    gid = lax.broadcasted_iota(jnp.int32, (GROUP, 128), 0)
    core = me_ref[0] // PLANE_CHIPS
    here, there = here_ref[:, ROW_META % 8, :], there_ref[:, ROW_META % 8, :]
    meta = jnp.concatenate([jnp.where(core == 0, here, there), jnp.where(core == 0, there, here)], axis=0)
    counts = jnp.broadcast_to(jnp.sum(jnp.where(lane == 1, meta, 0.0), axis=1, keepdims=True), (GROUP, 128))
    base = jnp.minimum(counts, float(KEEP))
    surplus = counts - base
    total = jnp.sum(surplus, axis=0, keepdims=True)
    lane_f = lane.astype(F32)
    room = jnp.sum(jnp.maximum(lane_f + 1.0 - base, 0.0), axis=0, keepdims=True)
    full = jnp.where((room <= total) & (lane[:1] < n), 1.0, 0.0)
    level = jnp.broadcast_to(jnp.sum(full, axis=1, keepdims=True), (GROUP, 128))
    taken = jnp.maximum(level - base, 0.0)
    left = total - jnp.sum(taken, axis=0, keepdims=True)
    tri_r = lax.broadcasted_iota(jnp.int32, (GROUP, GROUP), 0)
    tri_c = lax.broadcasted_iota(jnp.int32, (GROUP, GROUP), 1)
    before = jnp.where(tri_c < tri_r, 1.0, 0.0).astype(BF16)
    open_ = jnp.where(base <= level, 1.0, 0.0)
    rank = dot(before, open_.astype(BF16))
    taken = taken + jnp.where(rank < left, open_, 0.0)
    offset = dot(before, surplus.astype(BF16))
    me = me_ref[0]
    start = jnp.sum(jnp.where(gid < me, taken, 0.0), axis=0, keepdims=True)
    mine = jnp.sum(jnp.where(gid == me, base + taken, 0.0), axis=0, keepdims=True)
    held = jnp.sum(jnp.where(gid == me, base, 0.0), axis=0, keepdims=True)
    order = jnp.where(lane_f < surplus, offset + lane_f, -1.0)
    place = ((gid % PLANE_CHIPS) * (n - KEEP) + lane).astype(F32)
    away = jnp.where(gid // PLANE_CHIPS == core, 0.0, 1.0)
    for j in range(n):
        hit = order == start + float(j)
        one = jnp.sum(jnp.sum(jnp.where(hit, place, 0.0), axis=0, keepdims=True), axis=1, keepdims=True)
        two = jnp.sum(jnp.sum(jnp.where(hit, away, 0.0), axis=0, keepdims=True), axis=1, keepdims=True)
        plan_ref[j : j + 1, :] = jnp.where(lane[:1] == 0, one, two).astype(jnp.int32)
    plan_ref[n : n + 1, :] = mine.astype(jnp.int32)
    plan_ref[n + 1 : n + 2, :] = held.astype(jnp.int32)
    plan_ref[n + 2 :, :] = jnp.zeros((PLAN_ROWS - n - 2, 128), jnp.int32)


def first_kernel(th_ref, own_ref, *refs):
    weights, spare = refs[:N_WEIGHTS], refs[N_WEIGHTS : N_WEIGHTS + 2]
    deriv_ref, grad_ref, tally_ref, tmp_s, *scratch = refs[N_WEIGHTS + 2 :]
    prepare(th_ref, *weights, *spare, tmp_s)
    frame = run_frame(own_ref[0], weights, spare, deriv_ref.at[0], grad_ref.at[0], [ref.at[0] for ref in scratch])
    tally_ref[...] = in_turns([frame])[0]


def rest_kernel(plan_ref, own_ref, *refs):
    here, there = refs[:BATCH], refs[BATCH : 2 * BATCH]
    first_ref, *refs = refs[2 * BATCH :]
    weights, spare = refs[:N_WEIGHTS], refs[N_WEIGHTS : N_WEIGHTS + 2]
    deriv_ref, grad_ref, tally_ref, sum_s, *scratch = refs[N_WEIGHTS + 2 :]
    step = pl.program_id(0)
    count, own = plan_ref[PLAN_COUNT, 0], plan_ref[PLAN_OWN, 0]

    @pl.when(step == 0)
    def _():
        sum_s[...] = first_ref[...]

    @pl.when(step * BATCH + 1 < count)
    def _():
        frames = []
        for j in range(BATCH):
            at = step * BATCH + 1 + j
            away = plan_ref[jnp.clip(at - own, 0, 7), 1]
            taken = jnp.where(away == 0, here[j][0], there[j][0])
            kept = own_ref[jnp.where(at < own, at, 0)]
            x = jnp.where((at >= own) & (at < count), taken, kept)
            frames.append(
                run_frame(x, weights, spare, deriv_ref.at[j], grad_ref.at[j], [ref.at[j] for ref in scratch])
            )
        total = sum_s[...]
        for j, row in enumerate(in_turns(frames)):
            total = total + jnp.where(step * BATCH + 1 + j < count, row, 0.0)
        sum_s[...] = total

    @pl.when(step == pl.num_programs(0) - 1)
    def _():
        tally_ref[...] = jnp.broadcast_to(sum_s[:1, :], (CHIPS, 128))


def combine_kernel(
    plan_ref, core_ref, parts_ref, more_ref, deriv0_ref, grad0_ref, deriv_ref, grad_ref,
    mine_ref, other_ref, means_ref,
    all_s, acc_s, window_s, tmp_s,
):
    step = pl.program_id(0)

    def scaled(deriv, grads):
        mine = lax.broadcasted_iota(jnp.int32, (1, 128), 1) == deriv[:1, 1:2].astype(jnp.int32)
        centre = jnp.sum(jnp.where(mine, window_s[0, :1], 0.0), axis=1, keepdims=True)
        share = jnp.sum(jnp.where(mine, window_s[1, :1], 0.0), axis=1, keepdims=True)
        return share * grads[1] - share * (deriv[:1, :1] - centre) * grads[0]

    @pl.when(step == 0)
    def _():
        total = jnp.broadcast_to(jnp.sum(parts_ref[...] + more_ref[...], axis=0, keepdims=True), (8, 128))
        lane = lax.broadcasted_iota(jnp.int32, (8, 128), 1)
        sizes = jnp.maximum(total, 1.0)
        means = pltpu.roll(total, 128 - WINDOWS, 1) / sizes
        ends = (lane == 0) | (lane == WINDOWS - 1)
        weight = jnp.where(ends, 0.5, 1.0) / (WINDOWS - 1)
        means_ref[...] = means
        window_s[0] = means
        window_s[1] = weight / sizes
        acc_s[...] = scaled(deriv0_ref[0], grad0_ref[0])

    @pl.when((step > 0) & (step < plan_ref[PLAN_COUNT, 0]))
    def _():
        acc_s[...] += scaled(deriv_ref[0], grad_ref[0])

    @pl.when(step == pl.num_programs(0) - 1)
    def _():
        all_s[USED_ROWS // 8 * 8 :, :] = jnp.zeros((ROWS - USED_ROWS // 8 * 8, 128), F32)
        misc = acc_s[G_MISC : G_MISC + C, :]
        for r, row in enumerate(flatten(misc[:, :16], C, SPECIES, 10)):
            all_s[ROW_EMBED + r : ROW_EMBED + r + 1, :] = row
        for l in range(LAYERS):
            o = ROW_LAYER + l * LAYER_ROWS
            w1 = misc[l * HID : (l + 1) * HID, 16:32] * NB ** (-0.5)
            w1 = w1[:, :NB] + w1[:, NB:]
            w1 = jnp.concatenate([w1, jnp.zeros((HID, 8), F32)], axis=1)
            for r, row in enumerate(flatten(w1, HID, NB, 4)):
                all_s[o + OFF_W1 + r : o + OFF_W1 + r + 1, :] = row
            for off, rows, at in ((OFF_W2, 32, G_W2), (OFF_W3, 64, G_W3)):
                tmp_s[: 2 * rows, :] = acc_s[at : at + 2 * rows, :] * HID ** (-0.5)
                even = tmp_s[pl.ds(0, rows, stride=2), :]
                odd = tmp_s[pl.ds(1, rows, stride=2), :]
                left = lax.broadcasted_iota(jnp.int32, (rows, 128), 1) < HID
                if l == 0:
                    both = jnp.where(left, even, pltpu.roll(odd, HID, 1))
                else:
                    both = jnp.where(left, pltpu.roll(even, HID, 1), odd)
                all_s[o + off : o + off + rows, :] = both
            for i, off in enumerate((OFF_LIN, OFF_SQ, OFF_SKIP)):
                at = G_MIX + (3 * l + i) * C
                all_s[o + off : o + off + C, :] = acc_s[at : at + C, :] * C ** (-0.5)
            all_s[o + OFF_UP : o + OFF_UP + C, :] = acc_s[G_UP + l * C : G_UP + (l + 1) * C, :] * C ** (-0.5)
            all_s[o + OFF_READ : o + OFF_READ + 1, :] = acc_s[G_READ + 8 * l : G_READ + 8 * l + 1, :] * C ** (-0.5)
        all_s[ROW_HEAD : ROW_HEAD + RO, :] = acc_s[G_HEAD : G_HEAD + RO, :] * C ** (-0.5)
        all_s[ROW_OUT : ROW_OUT + 1, :] = acc_s[G_OUT : G_OUT + 1, :] * RO ** (-0.5)
        half = ROWS // 2
        core = core_ref[0]
        mine_ref[...] = all_s[pl.ds(pl.multiple_of(core * half, half), half), :]
        other_ref[...] = all_s[pl.ds(pl.multiple_of((1 - core) * half, half), half), :]


def whole_spec(shape):
    return pl.BlockSpec(shape, lambda i, *_: (0,) * len(shape))


SMEM_SPEC = pl.BlockSpec(memory_space=pltpu.SMEM)
WEIGHTS = (
    ((LAYERS, HID, 48), BF16),
    ((LAYERS, HID, 3 * HID), BF16),
    ((LAYERS, C, 3 * HID), BF16),
    ((LAYERS, C, 3 * C), BF16),
    ((LAYERS, C, 3 * C), BF16),
    ((LAYERS, C, 9 * C), BF16),
    ((LAYERS, 3 * C, 3 * C), BF16),
    ((RO, 3 * C), BF16),
    ((C, 3 * RO), BF16),
    ((C, 48), BF16),
    ((LAYERS, C, 128), F32),
    ((RO, 128), F32),
)
SPARE = (((LAYERS, HID, 2 * C), BF16), ((LAYERS, HID, 2 * HID), BF16))


def frame_scratch(n):
    return [
        pltpu.VMEM((n, ATOMS, EDGES), BF16),
        pltpu.VMEM((n, LAYERS, C, EDGES), F32),
        pltpu.VMEM((n, LAYERS, 2, HID, EDGES), BF16),
        pltpu.VMEM((n, LAYERS, 2, HID, EDGES), BF16),
        pltpu.VMEM((n, C, EDGES), F32),
        pltpu.VMEM((n, 2, C, EDGES), BF16),
        pltpu.VMEM((n, NB * K + K, ATOMS), F32),
    ]


LIMIT = pltpu.CompilerParams(vmem_limit_bytes=56 * 2**20)
COMBINE_LIMIT = pltpu.CompilerParams(vmem_limit_bytes=54 * 2**20)
SMALL_LIMIT = pltpu.CompilerParams(vmem_limit_bytes=4 * 2**20)


TALLY = jax.ShapeDtypeStruct((8, 128), F32)


def run_pack(count, window_of, positions, species, neighbours):
    n = positions.shape[0]
    return pl.pallas_call(
        pack_kernel,
        in_specs=[SMEM_SPEC, SMEM_SPEC] + [pl.BlockSpec(memory_space=pltpu.VMEM)] * 3,
        out_specs=[pl.BlockSpec(memory_space=pltpu.VMEM)] * 2,
        scratch_shapes=[pltpu.VMEM(((n - KEEP) * FRAME_ROWS, 128), F32)],
        out_shape=[
            jax.ShapeDtypeStruct((n, FRAME_ROWS, 128), F32),
            jax.ShapeDtypeStruct((PLANE_CHIPS, (n - KEEP) * FRAME_ROWS, 128), F32),
        ],
        name="pack",
    )(count, window_of, jnp.transpose(positions, (1, 0, 2)), species, neighbours)


def run_deal(me, here, there):
    return pl.pallas_call(
        deal_kernel,
        grid=(1,),
        in_specs=[SMEM_SPEC] + [pl.BlockSpec((PLANE_CHIPS, 8, 128), lambda i: (0, ROW_META // 8, 0))] * 2,
        out_specs=whole_spec((PLAN_ROWS, 128)),
        out_shape=jax.ShapeDtypeStruct((PLAN_ROWS, 128), jnp.int32),
        compiler_params=SMALL_LIMIT,
        name="deal",
    )(me, here, there)


def run_first(theta, own):
    held = WEIGHTS + SPARE
    shapes = [(s, t) for s, t in held] + [((1, 8, 128), F32), ((1, 2, G_ROWS, 128), F32), (TALLY.shape, F32)]
    out = pl.pallas_call(
        first_kernel,
        grid=(1,),
        in_specs=[whole_spec((ROWS, 128)), whole_spec((1, FRAME_ROWS, 128))],
        out_specs=[whole_spec(s) for s, _ in shapes],
        scratch_shapes=[pltpu.VMEM((136, 128), F32)] + frame_scratch(1),
        out_shape=[jax.ShapeDtypeStruct(s, t) for s, t in shapes],
        compiler_params=LIMIT,
        cost_estimate=pl.CostEstimate(flops=10**9, bytes_accessed=4 * 10**7, transcendentals=10**6),
        name="first_frame",
    )(theta, own)
    return out[: N_WEIGHTS + 2], out[N_WEIGHTS + 2], out[N_WEIGHTS + 3], out[N_WEIGHTS + 4]


def run_rest(plan, own, here, there, tally, held):
    n = own.shape[0]
    steps = -(-(n - 1) // BATCH)

    def taken_spec(j):
        def index(i, plan):
            return (plan[jnp.clip(i * BATCH + 1 + j - plan[PLAN_OWN, 0], 0, 7), 0], 0, 0)

        return pl.BlockSpec((1, FRAME_ROWS, 128), index)

    def result_spec(shape):
        def index(i, plan):
            return (jnp.minimum(i, jnp.maximum((plan[PLAN_COUNT, 0] + BATCH - 2) // BATCH - 1, 0)),) + (0,) * len(shape)

        return pl.BlockSpec((BATCH,) + shape, index)

    results = ((8, 128), (2, G_ROWS, 128))
    return pl.pallas_call(
        rest_kernel,
        grid_spec=pltpu.PrefetchScalarGridSpec(
            num_scalar_prefetch=1,
            grid=(steps,),
            in_specs=[whole_spec(own.shape)]
            + [taken_spec(j) for j in range(BATCH)] * 2
            + [whole_spec(TALLY.shape)]
            + [whole_spec(s) for s, _ in WEIGHTS + SPARE],
            out_specs=[result_spec(s) for s in results] + [whole_spec((CHIPS, 128))],
            scratch_shapes=[pltpu.VMEM(TALLY.shape, F32)] + frame_scratch(BATCH),
        ),
        out_shape=[jax.ShapeDtypeStruct((steps * BATCH,) + s, F32) for s in results]
        + [jax.ShapeDtypeStruct((CHIPS, 128), F32)],
        compiler_params=LIMIT,
        name="other_frames",
    )(plan, own, *[here] * BATCH, *[there] * BATCH, tally, *held)


def run_combine(plan, core, parts, more, deriv0, grad0, deriv, grad, n):
    def rest_spec(shape):
        def index(i, plan):
            return (jnp.clip(i - 1, 0, jnp.maximum(plan[PLAN_COUNT, 0] - 2, 0)),) + (0,) * len(shape)

        return pl.BlockSpec((1,) + shape, index)

    half = (ROWS // 2, 128)
    return pl.pallas_call(
        combine_kernel,
        grid_spec=pltpu.PrefetchScalarGridSpec(
            num_scalar_prefetch=1,
            grid=(n,),
            in_specs=[SMEM_SPEC]
            + [whole_spec(v.shape) for v in (parts, more, deriv0, grad0)]
            + [rest_spec(v.shape[1:]) for v in (deriv, grad)],
            out_specs=[whole_spec(half), whole_spec(half), whole_spec(TALLY.shape)],
            scratch_shapes=[
                pltpu.VMEM((ROWS, 128), F32),
                pltpu.VMEM((G_ROWS, 128), F32),
                pltpu.VMEM((2, 8, 128), F32),
                pltpu.VMEM((136, 128), F32),
            ],
        ),
        out_shape=[jax.ShapeDtypeStruct(half, F32), jax.ShapeDtypeStruct(half, F32), TALLY],
        compiler_params=COMBINE_LIMIT,
        name="combine",
    )(plan, core, parts, more, deriv0, grad0, deriv, grad)


def adam_step(params, first_moment, second_moment, unit):
    new_first = 0.9 * first_moment + 0.1 * unit
    new_second = 0.999 * second_moment + 0.001 * unit * unit
    unbiased_first = new_first / (1.0 - 0.9**10)
    unbiased_second = new_second / (1.0 - 0.999**10)
    new_params = params - 0.01 * unbiased_first / (jnp.sqrt(unbiased_second) + 1e-08)
    return (new_params, new_first, new_second)


def swap_cores(v):
    return lax.ppermute(v, "core", [(0, 1), (1, 0)])


def gather_tallies(v):
    own = lax.all_to_all(v, PLANE + ("z",), 0, 0, tiled=True)
    return own, swap_cores(own)


def to_all(v, axes, size):
    return lax.all_to_all(jnp.broadcast_to(v[None], (size,) + v.shape), axes, 0, 0, tiled=True)


def sum_large(mine, other, core):
    half = mine.shape[0]
    piece = half // PLANE_CHIPS
    own = mine + swap_cores(other)
    own = jnp.sum(lax.all_to_all(own.reshape(PLANE_CHIPS, piece, 128), PLANE, 0, 0, tiled=True), axis=0)
    own = jnp.sum(to_all(own, "z", DEPTH), axis=0)
    own = to_all(own, PLANE, PLANE_CHIPS).reshape(half, 128)
    other = swap_cores(own)
    first = core == 0
    return jnp.concatenate([jnp.where(first, own, other), jnp.where(first, other, own)], axis=0)


def on_device(
    params, first_moment, second_moment, positions, species, neighbours, window_of, frame_count
):
    n = positions.shape[0]
    core = lax.axis_index("core")
    own, send = run_pack(frame_count, window_of, positions, species, neighbours)
    here = lax.all_to_all(send, PLANE, 0, 0, tiled=True)
    theta = jnp.pad(params, (0, ROWS * 128 - NPAR)).reshape(ROWS, 128)
    held, deriv0, grad0, tally = run_first(theta, own)
    here, tally = lax.optimization_barrier((here, tally))
    there = swap_cores(here)
    plan = run_deal((core * PLANE_CHIPS + lax.axis_index(PLANE))[None], here, there)
    here, there = (v.reshape(PLANE_CHIPS * (n - KEEP), FRAME_ROWS, 128) for v in (here, there))
    deriv, grad, tally = run_rest(plan, own, here, there, tally, held)
    mine, other, means = run_combine(plan, core[None], *gather_tallies(tally), deriv0, grad0, deriv, grad, n)
    summed = sum_large(mine, other, core).reshape(-1)[:NPAR]
    norm = jnp.sqrt(jnp.sum(summed * summed))
    unit = summed * (GRAD_SCALE * math.sqrt(NPAR) / (norm + 1e-06))
    new_params, new_first, new_second = adam_step(params, first_moment, second_moment, unit)
    return (new_params, new_first, new_second, means[0, :WINDOWS])


def solution(mesh):
    axes = tuple(AXES)
    split = Mesh(mesh.devices.reshape(tuple(AXES.values())), axes)
    in_specs = (
        P(),
        P(),
        P(),
        P(axes, None, None),
        P(axes, None),
        P(axes, None, None),
        P(axes),
        P(axes),
    )
    out_specs = (P(), P(), P(), P())
    return jax.shard_map(
        on_device, mesh=split, in_specs=in_specs, out_specs=out_specs, check_vma=False
    )
```
